512 devices in a mesh: dp: 16 (over z), seq: 32 (over x, y, core).
Axes of the slice: x: 4, y: 4, z: 16, core: 2. Of those that a mesh axis runs over, the one named last changes fastest.
Arguments:
- queries: bfloat16 [16, 32, 256, 1152], P('dp', 'seq'), may hold values from -9 to 9
- key_vectors: bfloat16 [16, 32, 256, 1152], P('dp', 'seq'), may hold values from -9 to 9
- value_vectors: bfloat16 [16, 32, 256, 1152], P('dp', 'seq'), may hold values from -6 to 6
- out_grad: bfloat16 [16, 32, 256, 1152], P('dp', 'seq'), may hold values from -6 to 6
- out_weight: bfloat16 [1152, 1152], P(None, 'seq'), may hold values from -0.1875 to 0.1875
- clip_frames: int32 [16, 4], P('dp'), may hold values from 1 to 16, 32 in all within a row
Outputs:
- attn_out: bfloat16 [16, 32, 256, 1152], P('dp', 'seq')
- query_grad: bfloat16 [16, 32, 256, 1152], P('dp', 'seq')
- key_grad: bfloat16 [16, 32, 256, 1152], P('dp', 'seq')
- value_grad: bfloat16 [16, 32, 256, 1152], P('dp', 'seq')
- weight_grad: float32 [1152, 1152], P(None, 'seq')
The draws below stay inside these ranges and needn't reach their ends.
Inputs may be any that keep to these rules, and one draw needn't show every extreme that they name: `clip_frames`: row g lists the frame counts of the 4 clips of group g in frame order; they sum to 32, and the largest of each row is 16.
All inputs are finite; a program needn't handle non-finite values.
Results may differ from the reference program's by a relative error of at most 0.023.
Values may be sent and summed in bfloat16 or wider, within the bound.
No kernel may reach another device: no remote copies, remote signals or barrier semaphores. Data moves between devices by JAX's collectives and lax.ppermute only.
A program may use at most 64 MiB of HBM per device.

```python
import math
import jax
import jax.numpy as jnp
import numpy as np
from jax import lax

HEADS = 16
HEAD_DIM = 72
D = 1152
PATCHES = 256
FR_DEV = 1
CLIPS = 4
GROUPS = 16
FRAMES = 32
CLIP_MOST = 16
N_SEQ = 32


def draw_queries(key, part):
    own = jax.random.fold_in(key, 3)
    shape = (GROUPS, FRAMES, PATCHES, D)
    return jnp.clip(jax.random.normal(own, shape, jnp.float32), -4.0, 4.0).astype(jnp.bfloat16)


def draw_key_vectors(key, part):
    own = jax.random.fold_in(key, 5)
    shape = (GROUPS, FRAMES, PATCHES, D)
    return jnp.clip(jax.random.normal(own, shape, jnp.float32), -4.0, 4.0).astype(jnp.bfloat16)


def spiked(values, key, source, target, shards_of, factor):
    def block_of(dim):
        return (jnp.arange(values.shape[dim]) // (values.shape[dim] // shards_of)).reshape((-1,) + (1,) * (values.ndim - 1 - dim))

    one_side = jax.random.permutation(key, shards_of)[block_of(target)]
    second = (block_of(target) + shards_of // 2) % shards_of
    return jnp.where((block_of(source) == one_side) | (block_of(source) == second), factor * values, values)


def levels(stream_key, dims, pieces, least, high):
    factor_of = 1.0
    for position, blocks in pieces:
        heights = jax.random.uniform(jax.random.fold_in(jax.random.fold_in(stream_key, 6), position), (blocks,), jnp.float32, least / len(pieces), high / len(pieces))
        factor_of = factor_of * jnp.repeat(jnp.exp(heights), dims[position] // blocks).reshape((-1,) + (1,) * (len(dims) - 1 - position))
    return factor_of


def length_profile(amount, total, reach, lean):
    portions = [(1 << 20) // math.isqrt(standing ** lean) + 1 for standing in range(2, amount + 1)]
    rest, holding = total - reach - (amount - 1), [1] * (amount - 1)
    while rest > 0:
        movable = [i for i in range(amount - 1) if holding[i] < reach]
        mass, remaining = sum([portions[i] for i in movable]), rest
        for i in movable:
            more = min(reach - holding[i], max(1, remaining * portions[i] // mass), rest)
            holding[i] = holding[i] + more
            rest = rest - more
    return np.array([reach] + holding)


def uneven_parts(stream_key, number_of, total, reach, lean):
    if number_of == 2:
        one = jax.random.randint(stream_key, (), max(1, total - reach), min(reach, total - 1) + 1)
        return jnp.stack([one, total - one])
    sizes = jnp.asarray(length_profile(number_of, total, reach, lean), jnp.int32)
    twos = (number_of - 1) // 2
    giver, sink = sizes[1:1 + 2 * twos:2], sizes[2:2 + 2 * twos:2]
    room = jnp.minimum(giver - 1, reach - sink)
    shifted = jax.random.randint(jax.random.fold_in(stream_key, 1), (twos,), 0, 1 << 20) % (room + 1)
    sizes = sizes.at[1:1 + 2 * twos:2].set(giver - shifted).at[2:2 + 2 * twos:2].set(sink + shifted)
    return sizes[jax.random.permutation(jax.random.fold_in(stream_key, 2), number_of)]


def bell_draw(own_key, dims, deviation, limit, cuts=(), kind=jnp.bfloat16):
    array = deviation * jax.random.normal(own_key, dims, jnp.float32)
    if cuts:
        array = array * levels(own_key, dims, cuts, -0.22, 0.18)
    return jnp.clip(array, -limit, limit).astype(kind)


def heavy_noise(own_key, extent, scale, most, shards, heavy, kind=jnp.bfloat16):
    drawn = scale * jax.random.normal(own_key, extent, jnp.float32)
    if shards:
        drawn = drawn * levels(own_key, extent, shards, -0.22, 0.18)
    return jnp.clip(spiked(drawn, jax.random.fold_in(own_key, 3), *heavy), -most, most).astype(kind)


def setup_inputs(seed: int = 0) -> dict:
    seeds = jax.random.split(jax.random.key(seed), 7)
    return {
        "queries": draw_queries(jax.random.fold_in(seeds[6], 71), 0),
        "key_vectors": draw_key_vectors(jax.random.fold_in(seeds[6], 71), 0),
        "value_vectors": bell_draw(seeds[2], (GROUPS, FRAMES, PATCHES, D), 1.0, 6.0, ((0, 16), (1, 32))),
        "out_grad": heavy_noise(seeds[3], (GROUPS, FRAMES, PATCHES, D), 1.0, 6.0, ((0, 16), (1, 32)), (1, 3, 32, 2.75)),
        "out_weight": bell_draw(seeds[4], (D, D), D ** -0.5, 0.1875, ((1, 32),)),
        "clip_frames": jax.vmap(lambda own: uneven_parts(own, CLIPS, FRAMES, CLIP_MOST, 2))(jax.random.split(seeds[5], GROUPS)).reshape((GROUPS, CLIPS)).astype(jnp.int32),
    }


def clip_mask(lengths):
    clip_ends = jnp.cumsum(lengths).astype(jnp.int32)
    frame_ids = jnp.arange(FRAMES, dtype=jnp.int32)
    clip_ids = lax.optimization_barrier(jnp.sum((frame_ids[:, None] >= clip_ends[None, :]).astype(jnp.int32), axis=1))
    return clip_ids[:, None] == clip_ids[None, :]

def reference(queries, key_vectors, value_vectors, out_grad, out_weight, clip_frames):
    scale = 1.0 / math.sqrt(HEAD_DIM)
    heads_shape = (FRAMES, PATCHES, HEADS, HEAD_DIM)
    tokens = FRAMES * PATCHES

    def group_pass(items):
        query_g, key_g, value_g, grad_g, lengths = items
        query_heads = query_g.astype(jnp.float32).reshape(heads_shape)
        key_heads = key_g.astype(jnp.float32).reshape(heads_shape)
        value_heads = value_g.astype(jnp.float32).reshape(heads_shape)
        same_clip = clip_mask(lengths)
        scores = jnp.einsum('fphe,gphe->phfg', query_heads, key_heads) * scale
        scores = jnp.where(same_clip, scores, -jnp.inf)
        row_max = lax.optimization_barrier(jnp.max(scores, axis=-1, keepdims=True))
        raised = jnp.exp(scores - row_max)
        attention = raised / lax.optimization_barrier(jnp.sum(raised, axis=-1, keepdims=True))
        attention_bf = attention.astype(jnp.bfloat16)
        attention_up = attention_bf.astype(jnp.float32)
        mixed = jnp.einsum('phfg,gphe->fphe', attention_up, value_heads).astype(jnp.bfloat16)
        tok_rows = mixed.reshape(tokens, D)
        attn_out = jnp.dot(tok_rows, out_weight, preferred_element_type=jnp.float32).astype(jnp.bfloat16)
        grad_rows = grad_g.reshape(tokens, D)
        mixed_grad = jnp.dot(grad_rows, out_weight.T, preferred_element_type=jnp.float32).astype(jnp.bfloat16)
        blocks_a = tok_rows.astype(jnp.float32).reshape(N_SEQ, FR_DEV * PATCHES, D)
        blocks_g = grad_rows.astype(jnp.float32).reshape(N_SEQ, FR_DEV * PATCHES, D)
        partial_value = jnp.einsum('btd,bte->bde', blocks_a, blocks_g).astype(jnp.bfloat16)
        partial_value = lax.optimization_barrier(partial_value)
        weight_part = lax.optimization_barrier(jnp.sum(partial_value.astype(jnp.float32), axis=0))
        grad_heads = mixed_grad.astype(jnp.float32).reshape(heads_shape)
        value_grad = jnp.einsum('phfg,fphe->gphe', attention_up, grad_heads).astype(jnp.bfloat16)
        prob_grad = jnp.einsum('fphe,gphe->phfg', grad_heads, value_heads)
        inner = lax.optimization_barrier(jnp.sum(attention * prob_grad, axis=-1, keepdims=True))
        score_grad = (attention * (prob_grad - inner) * scale).astype(jnp.bfloat16).astype(jnp.float32)
        query_grad = jnp.einsum('phfg,gphe->fphe', score_grad, key_heads).astype(jnp.bfloat16)
        key_grad = jnp.einsum('phfg,fphe->gphe', score_grad, query_heads).astype(jnp.bfloat16)
        full_shape = (FRAMES, PATCHES, D)
        return (attn_out.reshape(full_shape), query_grad.reshape(full_shape), key_grad.reshape(full_shape), value_grad.reshape(full_shape), weight_part)
    attn_out, query_grad, key_grad, value_grad, weight_parts = lax.map(group_pass, (queries, key_vectors, value_vectors, out_grad, clip_frames))
    weight_grad = lax.optimization_barrier(jnp.sum(weight_parts, axis=0))
    return (attn_out, query_grad, key_grad, value_grad, weight_grad)
```

```python
import functools
import math

import jax
import jax.numpy as jnp
from jax import lax
from jax.experimental import pallas as pl
from jax.experimental.pallas import tpu as pltpu
from jax.sharding import PartitionSpec as P

HEADS = 16
HEAD_DIM = 72
LANES = 128
F32 = jnp.float32
BF16 = jnp.bfloat16
VMEM_LIMIT = 48 * 1024 * 1024
NT = (((1,), (1,)), ((), ()))
TN = (((0,), (0,)), ((), ()))


def dot(a, b):
    return jnp.dot(a, b, preferred_element_type=F32)


def dot_nt(a, b):
    return lax.dot_general(a, b, NT, preferred_element_type=F32)


def dot_tn(a, b):
    return lax.dot_general(a, b, TN, preferred_element_type=F32)


def window(head):
    first = head * HEAD_DIM // LANES
    last = (head * HEAD_DIM + HEAD_DIM - 1) // LANES
    return first * LANES, (last + 1 - first) * LANES


def head_lanes(head, rows):
    start, size = window(head)
    lane = lax.broadcasted_iota(jnp.int32, (rows, size), 1) + (start - head * HEAD_DIM)
    return (lane >= 0) & (lane < HEAD_DIM)


def clip_bias(lens_ref, rows, positions):
    def ids(axis):
        index = lax.broadcasted_iota(jnp.int32, (rows, rows), axis)
        frame = lax.div(index, jnp.int32(positions))
        clip = jnp.zeros_like(frame)
        end = jnp.int32(0)
        for j in range(lens_ref.shape[1]):
            end = end + lens_ref[0, j]
            clip = clip + jnp.where(frame >= end, 1, 0)
        return clip * positions + (index - frame * positions)

    return jnp.where(ids(0) == ids(1), 0.0, -jnp.inf).astype(F32)


def softmax(query_win, key_win, bias):
    scores = dot_nt(query_win, key_win) * (1.0 / math.sqrt(HEAD_DIM)) + bias
    raised = jnp.exp(scores - jnp.max(scores, axis=-1, keepdims=True))
    return raised * (1.0 / jnp.sum(raised, axis=-1, keepdims=True))


class Tiles:
    def __init__(self, ref, base=0):
        self.ref, self.base, self.held = ref, base, {}

    def add(self, head, value):
        start, size = window(head)
        for off in range(0, size, LANES):
            piece = value[:, off : off + LANES]
            tile = start + off
            self.held[tile] = piece if tile not in self.held else self.held[tile] + piece
        done = (head + 1) * HEAD_DIM
        for tile in [t for t in self.held if t + LANES <= done]:
            lanes = pl.ds(self.base + tile, LANES)
            self.ref[:, lanes] = self.held.pop(tile).astype(self.ref.dtype)


def forward_kernel(shard, pitch, positions, core_ref, lens_ref, x_ref, mixed_ref, keep_ref, send_ref):
    rows = x_ref.shape[0]
    width = x_ref.shape[1] // 4
    bias = clip_bias(lens_ref, rows, positions)
    mixed_tiles = Tiles(mixed_ref)
    for head in range(HEADS):
        start, size = window(head)
        lanes = head_lanes(head, rows)
        query_win = jnp.where(lanes, x_ref[:, pl.ds(start, size)], 0)
        key_win = x_ref[:, pl.ds(width + start, size)]
        value_win = jnp.where(lanes, x_ref[:, pl.ds(2 * width + start, size)], 0)
        attention = softmax(query_win, key_win, bias).astype(BF16)
        mixed_tiles.add(head, dot(attention, value_win))
    half = keep_ref.shape[0]
    feature = lax.broadcasted_iota(jnp.int32, (1, width), 1)
    owner = lax.div(feature, jnp.int32(shard))
    other = jnp.bitwise_and(owner + core_ref[0], 1)
    place = other * half + lax.div(owner, jnp.int32(2)) * pitch + (feature - owner * shard)
    mixed = mixed_ref[...]
    grad = x_ref[:, pl.ds(3 * width, width)]
    block = half // 4
    for step in range(8):
        at = lax.broadcasted_iota(jnp.int32, (block, width), 0) + step * block
        pick = jnp.where(at == place, 1.0, 0.0).astype(BF16)
        grad_rows = dot_nt(pick, grad).astype(BF16)
        part = dot(grad_rows, mixed).astype(BF16)
        out_ref = keep_ref if step < 4 else send_ref
        out_ref[pl.ds((step % 4) * block, block), :] = part


def backward_kernel(shard, pitch, positions, lens_ref, x_ref, mixed_ref, weight_ref, y_ref, back_ref):
    rows = x_ref.shape[0]
    width = x_ref.shape[1] // 4
    padded = weight_ref.shape[0]
    feature = lax.broadcasted_iota(jnp.int32, (1, width), 1)
    owner = lax.div(feature, jnp.int32(shard))
    place = owner * pitch + (feature - owner * shard)
    pick = jnp.where(lax.broadcasted_iota(jnp.int32, (padded, width), 0) == place, 1.0, 0.0).astype(BF16)
    grad_padded = dot_nt(x_ref[:, pl.ds(3 * width, width)], pick).astype(BF16)
    back_ref[...] = dot(grad_padded, weight_ref[...]).astype(BF16)
    out_padded = dot_nt(mixed_ref[...], weight_ref[...]).astype(BF16)
    y_ref[:, pl.ds(0, width)] = dot(out_padded, pick).astype(BF16)
    bias = clip_bias(lens_ref, rows, positions)
    query_tiles = Tiles(y_ref, width)
    key_tiles = Tiles(y_ref, 2 * width)
    value_tiles = Tiles(y_ref, 3 * width)
    for head in range(HEADS):
        start, size = window(head)
        lanes = head_lanes(head, rows)
        query_win = jnp.where(lanes, x_ref[:, pl.ds(start, size)], 0)
        key_win = jnp.where(lanes, x_ref[:, pl.ds(width + start, size)], 0)
        value_win = x_ref[:, pl.ds(2 * width + start, size)]
        back_win = jnp.where(lanes, back_ref[:, pl.ds(start, size)], 0)
        attention = softmax(query_win, key_win, bias)
        value_tiles.add(head, dot_tn(attention.astype(BF16), back_win))
        prob_grad = dot_nt(back_win, value_win)
        inner = jnp.sum(attention * prob_grad, axis=-1, keepdims=True)
        score_grad = (attention * (prob_grad - inner) * (1.0 / math.sqrt(HEAD_DIM))).astype(BF16)
        query_tiles.add(head, dot(score_grad, key_win))
        key_tiles.add(head, dot_tn(score_grad, query_win))


def spec(space=pltpu.VMEM):
    return pl.BlockSpec(memory_space=space)


def forward(core, lengths, x, shard, pitch, n_seq, positions):
    rows, wide = x.shape
    width = wide // 4
    half = n_seq * pitch // 2
    return pl.pallas_call(
        functools.partial(forward_kernel, shard, pitch, positions),
        out_shape=(
            jax.ShapeDtypeStruct((rows, width), BF16),
            jax.ShapeDtypeStruct((half, width), BF16),
            jax.ShapeDtypeStruct((half, width), BF16),
        ),
        in_specs=[spec(pltpu.SMEM), spec(pltpu.SMEM), spec()],
        out_specs=(spec(), spec(), spec()),
        compiler_params=pltpu.CompilerParams(vmem_limit_bytes=VMEM_LIMIT),
        cost_estimate=pl.CostEstimate(
            flops=4 * half * rows * width + 4 * HEADS * rows * rows * 256,
            bytes_accessed=16 * rows * width + 8 * half * width,
            transcendentals=HEADS * rows * rows,
        ),
        name="forward",
    )(core, lengths, x)


def backward(lengths, x, mixed, weight, shard, pitch, positions):
    rows, wide = x.shape
    width = wide // 4
    return pl.pallas_call(
        functools.partial(backward_kernel, shard, pitch, positions),
        out_shape=jax.ShapeDtypeStruct((rows, wide), BF16),
        in_specs=[spec(pltpu.SMEM), spec(), spec(), spec()],
        out_specs=spec(),
        scratch_shapes=[pltpu.VMEM((rows, width), BF16)],
        compiler_params=pltpu.CompilerParams(vmem_limit_bytes=VMEM_LIMIT),
        cost_estimate=pl.CostEstimate(
            flops=8 * rows * width * weight.shape[0] + 10 * HEADS * rows * rows * 256,
            bytes_accessed=20 * rows * width + 2 * weight.shape[0] * width,
            transcendentals=HEADS * rows * rows,
        ),
        name="backward",
    )(lengths, x, mixed, weight)


def on_device(n_seq, n_dp, queries, key_vectors, value_vectors, out_grad, out_weight, clip_frames):
    patches, width = queries.shape[2:]
    positions = patches // n_seq
    shard = out_weight.shape[1]
    pitch = -(-shard // 8) * 8
    core = jnp.bitwise_and(lax.axis_index("seq"), 1).astype(jnp.int32)

    def swap(block):
        return lax.all_to_all(block.reshape(n_seq, positions, -1), "seq", 0, 0, tiled=True)

    weight_rows = jnp.pad(out_weight.T, ((0, pitch - shard), (0, 0)))
    weight = lax.all_gather(weight_rows, "seq", axis=0, tiled=True)

    flat = [a.reshape(patches, width) for a in (queries, key_vectors, value_vectors, out_grad)]
    x = swap(jnp.concatenate(flat, axis=1)).reshape(patches, 4 * width)
    mixed, keep, send = forward(core.reshape(1), clip_frames, x, shard, pitch, n_seq, positions)

    partner = lax.ppermute(send, "seq", [(i, i ^ 1) for i in range(n_seq)])
    chip = (keep.astype(F32) + partner.astype(F32)).astype(BF16)
    planes = [[i for i in range(n_seq) if i % 2 == c] for c in (0, 1)]
    parts = lax.all_to_all(
        chip.reshape(n_seq // 2, pitch, width), "seq", 0, 0, tiled=True, axis_index_groups=planes
    )

    y = backward(clip_frames, x, mixed, weight, shard, pitch, positions)
    parts, y = lax.optimization_barrier((parts, y))
    back = swap(y).reshape(patches, 4 * width)

    total = jnp.sum(parts.astype(F32), axis=0)
    hop = 1
    while hop < n_dp:
        mine = total.astype(BF16)
        theirs = lax.ppermute(mine, "dp", [(i, i ^ hop) for i in range(n_dp)])
        total = mine.astype(F32) + theirs.astype(F32)
        hop *= 2
    weight_grad = total[:shard].T
    outs = [back[:, i * width : (i + 1) * width].reshape(queries.shape) for i in range(4)]
    return (*outs, weight_grad)


def solution(mesh):
    whole = P("dp", "seq", None, None)
    return jax.shard_map(
        functools.partial(on_device, mesh.shape["seq"], mesh.shape["dp"]),
        mesh=mesh,
        in_specs=(whole, whole, whole, whole, P(None, "seq"), P("dp", None)),
        out_specs=(whole, whole, whole, whole, P(None, "seq")),
        check_vma=False,
    )
```

```python
import functools
import math

import jax
import jax.numpy as jnp
from jax import lax
from jax.experimental import pallas as pl
from jax.experimental.pallas import tpu as pltpu
from jax.sharding import PartitionSpec as P

HEADS = 16
HEAD_DIM = 72
LANES = 128
SCALE = 1.0 / math.sqrt(HEAD_DIM)
F32 = jnp.float32
BF16 = jnp.bfloat16
VMEM_LIMIT = 28 * 1024 * 1024
NT = (((1,), (1,)), ((), ()))
TN = (((0,), (0,)), ((), ()))


def dot(a, b):
    return jnp.dot(a, b, preferred_element_type=F32)


def dot_nt(a, b):
    return lax.dot_general(a, b, NT, preferred_element_type=F32)


def dot_tn(a, b):
    return lax.dot_general(a, b, TN, preferred_element_type=F32)


def window(head):
    first = head * HEAD_DIM // LANES
    last = (head * HEAD_DIM + HEAD_DIM - 1) // LANES
    return first * LANES, (last + 1 - first) * LANES


def head_lanes(head, rows):
    start, size = window(head)
    lane = lax.broadcasted_iota(jnp.int32, (rows, size), 1) + (start - head * HEAD_DIM)
    return (lane >= 0) & (lane < HEAD_DIM)


def clip_bias(lens_ref, rows, positions):
    def ids(axis):
        index = lax.broadcasted_iota(jnp.int32, (rows, rows), axis)
        frame = lax.div(index, jnp.int32(positions))
        clip = jnp.zeros_like(frame)
        end = jnp.int32(0)
        for j in range(lens_ref.shape[1]):
            end = end + lens_ref[0, j]
            clip = clip + jnp.where(frame >= end, 1, 0)
        return clip * positions + (index - frame * positions)

    return jnp.where(ids(0) == ids(1), 0.0, -jnp.inf).astype(F32)


def softmax(query_win, key_win, bias):
    scores = dot_nt(query_win, key_win) * SCALE + bias
    raised = jnp.exp(scores - jnp.max(scores, axis=-1, keepdims=True))
    return raised, 1.0 / jnp.sum(raised, axis=-1, keepdims=True)


class Tiles:
    def __init__(self, ref, base=0):
        self.ref, self.base, self.held = ref, base, {}

    def add(self, head, value):
        start, size = window(head)
        for off in range(0, size, LANES):
            piece = value[:, off : off + LANES]
            tile = start + off
            self.held[tile] = piece if tile not in self.held else self.held[tile] + piece
        done = (head + 1) * HEAD_DIM
        for tile in [t for t in self.held if t + LANES <= done]:
            lanes = pl.ds(self.base + tile, LANES)
            self.ref[:, lanes] = self.held.pop(tile).astype(self.ref.dtype)


GROUP = 8
FULL = 16
ODD = 2
CHUNK = 3
ODD_LANES = 384


def selection(rows, columns, wanted):
    row = lax.broadcasted_iota(jnp.int32, (rows, columns), 0)
    column = lax.broadcasted_iota(jnp.int32, (rows, columns), 1)
    return jnp.where(column == wanted(row), 1.0, 0.0).astype(BF16)


def chunk_tiles(ref, q):
    pieces = [ref[:, pl.ds((CHUNK * u + q) * LANES, LANES)] for u in range(CHUNK)]
    return jnp.concatenate(pieces, axis=1)


def pack_kernel(*refs):
    *parts, weight_ref, x_ref, held_ref, sems = refs
    shard, width = weight_ref.shape
    rows = held_ref.shape[0]
    copies = [
        pltpu.make_async_copy(part, x_ref.at[:, pl.ds(i * width, width)], sems.at[i])
        for i, part in enumerate(parts)
    ]
    for copy in copies:
        copy.start()
    weight = weight_ref[...]

    def core(row):
        return jnp.bitwise_and(lax.div(row, jnp.int32(GROUP)), 1)

    def place(row):
        return jnp.bitwise_and(row, GROUP - 1)

    for block in range(FULL // GROUP):
        pick = selection(rows, shard, lambda row: FULL * core(row) + GROUP * block + place(row))
        held_ref[:, pl.ds(block * width, width)] = dot(pick, weight).astype(BF16)
    odd = jnp.zeros((rows, ODD_LANES), F32)
    for q in range(CHUNK):

        def wanted(row):
            k = lax.div(place(row) - q, jnp.int32(CHUNK))
            exact = (place(row) == CHUNK * k + q) & (k < ODD)
            return jnp.where(exact, 2 * FULL + ODD * core(row) + k, -1)

        odd = odd + dot(selection(rows, shard, wanted), chunk_tiles(weight_ref, q))
    held_ref[:, pl.ds(FULL // GROUP * width, ODD_LANES)] = odd.astype(BF16)
    lanes = pl.ds(len(parts) * width, held_ref.shape[1])
    copies.append(pltpu.make_async_copy(held_ref, x_ref.at[:, lanes], sems.at[len(parts)]))
    copies[-1].start()
    for copy in copies:
        copy.wait()


def pick_rows(ref, place):
    padded, width = ref.shape
    block = padded // 8
    for step in range(8):
        at = lax.broadcasted_iota(jnp.int32, (block, width), 0) + step * block
        ref[pl.ds(step * block, block), :] = jnp.where(at == place, 1.0, 0.0).astype(BF16)


def tables_kernel(shard, pitch, positions, core_ref, lens_ref, pick_ref, turned_ref, bias_ref, held_ref, sems):
    padded, width = turned_ref.shape
    feature = lax.broadcasted_iota(jnp.int32, (1, width), 1)
    owner = lax.div(feature, jnp.int32(shard))
    rest = feature - owner * shard
    other = jnp.bitwise_and(owner + core_ref[0], 1)
    turned = other * (padded // 2) + lax.div(owner, jnp.int32(2)) * pitch + rest
    holder = jnp.where(rest < 2 * FULL, lax.div(rest, jnp.int32(FULL)), lax.div(rest - 2 * FULL, jnp.int32(ODD)))
    other = jnp.bitwise_and(holder + core_ref[0], 1)
    within = rest - FULL * holder
    block = lax.div(within, jnp.int32(GROUP))
    size = width // shard * GROUP
    full = (other * (FULL // GROUP) + block) * size + owner * GROUP + within - block * GROUP
    odd = 2 * (FULL // GROUP) * size + (other * (width // shard) + owner) * ODD + rest - 2 * FULL - ODD * holder
    picked = jnp.where(rest < 2 * FULL, full, odd)
    copies = []
    for i, (ref, place) in enumerate(((turned_ref, turned), (pick_ref, picked))):
        rows = pl.ds(0, ref.shape[0])
        pick_rows(held_ref.at[i, rows], place)
        copies.append(pltpu.make_async_copy(held_ref.at[i, rows], ref, sems.at[i]))
        copies[-1].start()
    bias_ref[...] = clip_bias(lens_ref, bias_ref.shape[0], positions)
    for copy in copies:
        copy.wait()


def forward_kernel(turned_ref, x_ref, bias_ref, mixed_ref, keep_ref, send_ref, pick_ref, held_ref, sems):
    fetch = pltpu.make_async_copy(turned_ref, pick_ref, sems.at[4])
    fetch.start()
    rows, width = mixed_ref.shape
    bias = bias_ref[...]
    mixed_tiles = Tiles(mixed_ref)
    for head in range(HEADS):
        start, size = window(head)
        lanes = head_lanes(head, rows)
        query_win = jnp.where(lanes, x_ref[:, pl.ds(start, size)], 0)
        key_win = x_ref[:, pl.ds(width + start, size)]
        value_win = jnp.where(lanes, x_ref[:, pl.ds(2 * width + start, size)], 0)
        raised, recip = softmax(query_win, key_win, bias)
        mixed_tiles.add(head, dot((raised * recip).astype(BF16), value_win))
    mixed = mixed_ref[...]
    grad = x_ref[:, pl.ds(3 * width, width)]
    half = keep_ref.shape[0]
    block = half // 4
    copies = []
    fetch.wait()
    for step in (4, 5, 6, 7, 0, 1, 2, 3):
        grad_rows = dot_nt(pick_ref[pl.ds(step * block, block), :], grad).astype(BF16)
        part = dot(grad_rows, mixed).astype(BF16)
        at = pl.ds((step % 4) * block, block)
        if step < 4:
            keep_ref[at, :] = part
        else:
            held_ref[at, :] = part
            copies.append(pltpu.make_async_copy(held_ref.at[at, :], send_ref.at[at, :], sems.at[step % 4]))
            copies[-1].start()
    for copy in copies:
        copy.wait()


def join_kernel(keep_ref, theirs_ref, out_ref):
    size = out_ref.shape[2]
    total = (keep_ref[...].astype(F32) + theirs_ref[...].astype(F32)).astype(BF16)
    out_ref[0] = total[:, :size]
    out_ref[1] = total[:, total.shape[1] - size :]


def backward_kernel(
    pick_hbm, x_ref, other_ref, bias_ref, mixed_ref, y_ref, pick_ref, odd_ref, back_ref, out_ref, held_ref, sems
):
    rows, width = mixed_ref.shape
    fetch = pltpu.make_async_copy(pick_hbm, pick_ref, sems.at[7])
    fetch.start()
    copies = []

    def send(start, size):
        lanes = pl.ds(start, size)
        copies.append(pltpu.make_async_copy(held_ref.at[:, lanes], y_ref.at[:, lanes], sems.at[len(copies)]))
        copies[-1].start()

    blocks = FULL // GROUP
    weight = []
    for ref, base in ((x_ref, 4 * width), (other_ref, 0)):
        weight += [ref[:, pl.ds(base + b * width, width)] for b in range(blocks)]
    odd_rows = odd_ref.shape[0] // 2
    for i, (ref, base) in enumerate(((x_ref, 4 * width), (other_ref, 0))):
        left = ref[:, pl.ds(base + blocks * width, ODD_LANES)]
        for q in range(CHUNK):

            def wanted(row):
                source = lax.div(row, jnp.int32(ODD))
                return source * GROUP + CHUNK * (row - ODD * source) + q

            got = dot(selection(odd_rows, rows, wanted), left).astype(BF16)
            for u in range(CHUNK):
                lanes = pl.ds((CHUNK * u + q) * LANES, LANES)
                odd_ref[pl.ds(i * odd_rows, odd_rows), lanes] = got[:, u * LANES : (u + 1) * LANES]
    weight.append(odd_ref[...])
    fetch.wait()
    grad = dot_nt(x_ref[:, pl.ds(3 * width, width)], pick_ref[...]).astype(BF16)
    mixed = mixed_ref[...]
    back = jnp.zeros((rows, width), F32)
    at = 0
    for block in weight:
        size = block.shape[0]
        back = back + dot(grad[:, at : at + size], block)
        out_ref[:, pl.ds(at, size)] = dot_nt(mixed, block).astype(BF16)
        at += size
    back_ref[...] = back.astype(BF16)
    held_ref[:, pl.ds(0, width)] = dot(out_ref[...], pick_ref[...]).astype(BF16)
    send(0, width)
    query_tiles, key_tiles, value_tiles = [Tiles(held_ref, i * width) for i in (1, 2, 3)]
    bias = bias_ref[...]
    sent = 0
    for head in range(HEADS):
        start, size = window(head)
        lanes = head_lanes(head, rows)
        query_win = jnp.where(lanes, x_ref[:, pl.ds(start, size)], 0)
        key_win = jnp.where(lanes, x_ref[:, pl.ds(width + start, size)], 0)
        value_win = x_ref[:, pl.ds(2 * width + start, size)]
        back_win = jnp.where(lanes, back_ref[:, pl.ds(start, size)], 0)
        raised, recip = softmax(query_win, key_win, bias)
        attention = raised * recip
        value_tiles.add(head, dot_tn(attention.astype(BF16), back_win))
        drawn = attention * dot_nt(back_win, value_win)
        inner = jnp.sum(drawn, axis=-1, keepdims=True)
        score_grad = ((drawn - attention * inner) * SCALE).astype(BF16)
        query_tiles.add(head, dot(score_grad, key_win))
        key_tiles.add(head, dot_tn(score_grad, query_win))
        if head in (HEADS // 2 - 1, HEADS - 1):
            done = (head + 1) * HEAD_DIM // LANES * LANES
            for i in (1, 2, 3):
                send(i * width + sent, done - sent)
            sent = done
    for copy in copies:
        copy.wait()


def call(kernel, name, outs, args, smem=0, hbm_in=0, hbm_out=(), scratch=(), flops=0):
    space = [pltpu.SMEM] * smem + [pltpu.HBM] * hbm_in + [pltpu.VMEM] * (len(args) - smem - hbm_in)
    args = [pltpu.with_memory_space_constraint(a, s) if s == pltpu.HBM else a for a, s in zip(args, space)]
    shapes = [jax.ShapeDtypeStruct(shape, dtype) for shape, dtype in outs]
    moved = sum(a.size * a.dtype.itemsize for a in args) + sum(math.prod(s.shape) * s.dtype.itemsize for s in shapes)
    return pl.pallas_call(
        kernel,
        out_shape=[pltpu.HBM(s.shape, s.dtype) if i in hbm_out else s for i, s in enumerate(shapes)],
        in_specs=[pl.BlockSpec(memory_space=s) for s in space],
        out_specs=[pl.BlockSpec(memory_space=pltpu.HBM if i in hbm_out else pltpu.VMEM) for i in range(len(outs))],
        scratch_shapes=scratch,
        compiler_params=pltpu.CompilerParams(vmem_limit_bytes=VMEM_LIMIT),
        cost_estimate=pl.CostEstimate(flops=flops, bytes_accessed=moved, transcendentals=0),
        name=name,
    )(*args)


def dma(count):
    return pltpu.SemaphoreType.DMA((count,))


def pack(arrays, weight_t):
    rows, width = arrays[0].shape
    extra = FULL // GROUP * width + ODD_LANES
    outs = [((rows, len(arrays) * width + extra), BF16)]
    scratch = [pltpu.VMEM((rows, extra), BF16), dma(len(arrays) + 1)]
    return call(pack_kernel, "pack", outs, (*arrays, weight_t), hbm_in=len(arrays), hbm_out=(0,), scratch=scratch)[0]


def tables(core, lengths, rows, width, shard, pitch, positions):
    kernel = functools.partial(tables_kernel, shard, pitch, positions)
    padded = width // shard * pitch
    outs = [((width, width), BF16), ((padded, width), BF16), ((rows, rows), F32)]
    scratch = [pltpu.VMEM((2, padded, width), BF16), dma(2)]
    return call(kernel, "tables", outs, (core, lengths), smem=2, hbm_out=(0, 1), scratch=scratch)


def forward(x, turned, bias):
    rows = x.shape[0]
    padded, width = turned.shape
    half = (padded // 2, width)
    outs = [((rows, width), BF16), (half, BF16), (half, BF16)]
    flops = 4 * padded * rows * width + 4 * HEADS * rows * rows * 256
    scratch = [pltpu.VMEM(turned.shape, BF16), pltpu.VMEM(half, BF16), dma(5)]
    return call(forward_kernel, "forward", outs, (turned, x, bias), hbm_in=1, hbm_out=(2,), scratch=scratch, flops=flops)


def join(keep, theirs):
    rows, width = keep.shape
    return call(join_kernel, "join", [((2, rows, lane_half(width)), BF16)], (keep, theirs))[0]


def backward(pick, x, other, bias, mixed):
    rows, width = mixed.shape
    flops = 8 * width * rows * width + 12 * HEADS * rows * rows * 256
    one = pltpu.VMEM((rows, width), BF16)
    odd = pltpu.VMEM((width - 4 * rows, width), BF16)
    scratch = [pltpu.VMEM((width, width), BF16), odd, one, one, pltpu.VMEM((rows, 4 * width), BF16), dma(8)]
    args = (pick, x, other, bias, mixed)
    outs = [((rows, 4 * width), BF16)]
    return call(backward_kernel, "backward", outs, args, hbm_in=1, hbm_out=(0,), scratch=scratch, flops=flops)[0]


def lane_half(width):
    return (width // LANES + 1) // 2 * LANES


def sum_over_pairs(block, n_dp, width):
    def exchange(block, hop):
        return lax.ppermute(block, "dp", [(i, i ^ hop) for i in range(n_dp)])

    hop = 2
    while hop < n_dp:
        block = (block.astype(F32) + exchange(block, hop).astype(F32)).astype(BF16)
        hop *= 2
    theirs = exchange(block, 1)
    low = jnp.bitwise_and(lax.axis_index("dp"), 1) == 0
    lower, upper = jnp.where(low, block, theirs), jnp.where(low, theirs, block)
    return jnp.concatenate([lower, upper[:, 2 * lower.shape[1] - width :]], axis=1).astype(F32)


def on_device(n_seq, n_dp, queries, key_vectors, value_vectors, out_grad, out_weight, clip_frames):
    patches, width = queries.shape[2:]
    positions = patches // n_seq
    shard = out_weight.shape[1]
    pitch = -(-shard // 8) * 8
    core = jnp.bitwise_and(lax.axis_index("seq"), 1).astype(jnp.int32)

    def swap(block):
        return lax.all_to_all(block.reshape(n_seq, positions, -1), "seq", 0, 0, tiled=True)

    def partner(block):
        return lax.ppermute(block, "seq", [(i, i ^ 1) for i in range(n_seq)])

    arrays = [a.reshape(patches, width) for a in (queries, key_vectors, value_vectors, out_grad)]
    x = swap(pack(arrays, out_weight.T)).reshape(patches, -1)
    pick, turned, bias = tables(core.reshape(1), clip_frames, patches, width, shard, pitch, positions)
    mixed, keep, send = forward(x, turned, bias)

    chip = join(keep, partner(send)).reshape(n_seq, pitch, -1)
    pairs = [
        [(p + d) * n_seq + i for d in (0, 1) for i in range(c, n_seq, 2)] for p in range(0, n_dp, 2) for c in (0, 1)
    ]
    parts = lax.all_to_all(chip, ("dp", "seq"), 0, 0, tiled=True, axis_index_groups=pairs)

    y = backward(pick, x, partner(x[:, 4 * width :]), bias, mixed)
    parts, y = lax.optimization_barrier((parts, y))
    back = swap(y).reshape(patches, 4 * width)
    total = jnp.sum(parts.astype(F32), axis=0).astype(BF16)
    weight_grad = sum_over_pairs(total, n_dp, width)[:shard].T
    outs = [back[:, i * width : (i + 1) * width].reshape(queries.shape) for i in range(4)]
    return (*outs, weight_grad)


def solution(mesh):
    whole = P("dp", "seq", None, None)
    return jax.shard_map(
        functools.partial(on_device, mesh.shape["seq"], mesh.shape["dp"]),
        mesh=mesh,
        in_specs=(whole, whole, whole, whole, P(None, "seq"), P("dp", None)),
        out_specs=(whole, whole, whole, whole, P(None, "seq")),
        check_vma=False,
    )
```

```python
import functools
import math

import jax
import jax.numpy as jnp
from jax import lax
from jax.experimental import pallas as pl
from jax.experimental.pallas import tpu as pltpu
from jax.sharding import PartitionSpec as P

HEADS = 16
HEAD_DIM = 72
LANES = 128
SCALE = 1.0 / math.sqrt(HEAD_DIM)
F32 = jnp.float32
BF16 = jnp.bfloat16
VMEM_LIMIT = 28 * 1024 * 1024
NT = (((1,), (1,)), ((), ()))
TN = (((0,), (0,)), ((), ()))


def dot(a, b):
    return jnp.dot(a, b, preferred_element_type=F32)


def dot_nt(a, b):
    return lax.dot_general(a, b, NT, preferred_element_type=F32)


def dot_tn(a, b):
    return lax.dot_general(a, b, TN, preferred_element_type=F32)


def window(head):
    first = head * HEAD_DIM // LANES
    last = (head * HEAD_DIM + HEAD_DIM - 1) // LANES
    return first * LANES, (last + 1 - first) * LANES


def head_lanes(head, rows):
    start, size = window(head)
    lane = lax.broadcasted_iota(jnp.int32, (rows, size), 1) + (start - head * HEAD_DIM)
    return (lane >= 0) & (lane < HEAD_DIM)


def clip_bias(lens_ref, rows, positions):
    def ids(axis):
        index = lax.broadcasted_iota(jnp.int32, (rows, rows), axis)
        frame = lax.div(index, jnp.int32(positions))
        clip = jnp.zeros_like(frame)
        end = jnp.int32(0)
        for j in range(lens_ref.shape[1]):
            end = end + lens_ref[0, j]
            clip = clip + jnp.where(frame >= end, 1, 0)
        return clip * positions + (index - frame * positions)

    return jnp.where(ids(0) == ids(1), 0.0, -jnp.inf).astype(F32)


def softmax(query_win, key_win, bias):
    scores = dot_nt(query_win, key_win) * SCALE + bias
    raised = jnp.exp(scores - jnp.max(scores, axis=-1, keepdims=True))
    return raised, 1.0 / jnp.sum(raised, axis=-1, keepdims=True)


class Tiles:
    def __init__(self, ref, base=0):
        self.ref, self.base, self.held = ref, base, {}

    def add(self, head, value):
        start, size = window(head)
        for off in range(0, size, LANES):
            piece = value[:, off : off + LANES]
            tile = start + off
            self.held[tile] = piece if tile not in self.held else self.held[tile] + piece
        done = (head + 1) * HEAD_DIM
        for tile in [t for t in self.held if t + LANES <= done]:
            lanes = pl.ds(self.base + tile, LANES)
            self.ref[:, lanes] = self.held.pop(tile).astype(self.ref.dtype)


GROUP = 8
FULL = 16
ODD = 2
CHUNK = 3
ODD_LANES = 384


def selection(rows, columns, wanted):
    row = lax.broadcasted_iota(jnp.int32, (rows, columns), 0)
    column = lax.broadcasted_iota(jnp.int32, (rows, columns), 1)
    return jnp.where(column == wanted(row), 1.0, 0.0).astype(BF16)


def chunk_tiles(ref, q):
    pieces = [ref[:, pl.ds((CHUNK * u + q) * LANES, LANES)] for u in range(CHUNK)]
    return jnp.concatenate(pieces, axis=1)


def pack_kernel(*refs):
    *parts, weight_ref, x_ref, staged_ref, held_ref, sems = refs
    shard, width = weight_ref.shape
    rows = held_ref.shape[0]
    fetches = [pltpu.make_async_copy(part, staged_ref.at[i], sems.at[i]) for i, part in enumerate(parts)]
    for fetch in fetches:
        fetch.start()
    weight = weight_ref[...]

    def core(row):
        return jnp.bitwise_and(lax.div(row, jnp.int32(GROUP)), 1)

    def place(row):
        return jnp.bitwise_and(row, GROUP - 1)

    for block in range(FULL // GROUP):
        pick = selection(rows, shard, lambda row: FULL * core(row) + GROUP * block + place(row))
        held_ref[:, pl.ds(block * width, width)] = dot(pick, weight).astype(BF16)
    odd = jnp.zeros((rows, ODD_LANES), F32)
    for q in range(CHUNK):

        def wanted(row):
            k = lax.div(place(row) - q, jnp.int32(CHUNK))
            exact = (place(row) == CHUNK * k + q) & (k < ODD)
            return jnp.where(exact, 2 * FULL + ODD * core(row) + k, -1)

        odd = odd + dot(selection(rows, shard, wanted), chunk_tiles(weight_ref, q))
    held_ref[:, pl.ds(FULL // GROUP * width, ODD_LANES)] = odd.astype(BF16)
    lanes = pl.ds(len(parts) * width, held_ref.shape[1])
    copies = [pltpu.make_async_copy(held_ref, x_ref.at[:, lanes], sems.at[2 * len(parts)])]
    copies[-1].start()
    for i, fetch in enumerate(fetches):
        fetch.wait()
        lanes = pl.ds(i * width, width)
        copies.append(pltpu.make_async_copy(staged_ref.at[i], x_ref.at[:, lanes], sems.at[len(parts) + i]))
        copies[-1].start()
    for copy in copies:
        copy.wait()


def pick_rows(ref, place):
    padded, width = ref.shape
    block = padded // 8
    for step in range(8):
        at = lax.broadcasted_iota(jnp.int32, (block, width), 0) + step * block
        ref[pl.ds(step * block, block), :] = jnp.where(at == place, 1.0, 0.0).astype(BF16)


def tables_kernel(shard, pitch, positions, core_ref, lens_ref, pick_ref, turned_ref, bias_ref, held_ref, sems):
    padded, width = turned_ref.shape
    feature = lax.broadcasted_iota(jnp.int32, (1, width), 1)
    owner = lax.div(feature, jnp.int32(shard))
    rest = feature - owner * shard
    other = jnp.bitwise_and(owner + core_ref[0], 1)
    turned = other * (padded // 2) + lax.div(owner, jnp.int32(2)) * pitch + rest
    holder = jnp.where(rest < 2 * FULL, lax.div(rest, jnp.int32(FULL)), lax.div(rest - 2 * FULL, jnp.int32(ODD)))
    other = jnp.bitwise_and(holder + core_ref[0], 1)
    within = rest - FULL * holder
    block = lax.div(within, jnp.int32(GROUP))
    size = width // shard * GROUP
    full = (other * (FULL // GROUP) + block) * size + owner * GROUP + within - block * GROUP
    odd = 2 * (FULL // GROUP) * size + (other * (width // shard) + owner) * ODD + rest - 2 * FULL - ODD * holder
    picked = jnp.where(rest < 2 * FULL, full, odd)
    copies = []
    for i, (ref, place) in enumerate(((turned_ref, turned), (pick_ref, picked))):
        rows = pl.ds(0, ref.shape[0])
        pick_rows(held_ref.at[i, rows], place)
        copies.append(pltpu.make_async_copy(held_ref.at[i, rows], ref, sems.at[i]))
        copies[-1].start()
    bias_ref[...] = clip_bias(lens_ref, bias_ref.shape[0], positions)
    for copy in copies:
        copy.wait()


def forward_kernel(turned_ref, x_ref, bias_ref, mixed_ref, keep_ref, send_ref, pick_ref, held_ref, sems):
    fetch = pltpu.make_async_copy(turned_ref, pick_ref, sems.at[4])
    fetch.start()
    rows, width = mixed_ref.shape
    bias = bias_ref[...]
    mixed_tiles = Tiles(mixed_ref)
    for head in range(HEADS):
        start, size = window(head)
        lanes = head_lanes(head, rows)
        query_win = jnp.where(lanes, x_ref[:, pl.ds(start, size)], 0)
        key_win = x_ref[:, pl.ds(width + start, size)]
        value_win = jnp.where(lanes, x_ref[:, pl.ds(2 * width + start, size)], 0)
        raised, recip = softmax(query_win, key_win, bias)
        mixed_tiles.add(head, dot((raised * recip).astype(BF16), value_win))
    mixed = mixed_ref[...]
    grad = x_ref[:, pl.ds(3 * width, width)]
    half = keep_ref.shape[0]
    block = half // 4
    copies = []
    fetch.wait()
    for step in (4, 5, 6, 7, 0, 1, 2, 3):
        grad_rows = dot_nt(pick_ref[pl.ds(step * block, block), :], grad).astype(BF16)
        part = dot(grad_rows, mixed).astype(BF16)
        at = pl.ds((step % 4) * block, block)
        if step < 4:
            keep_ref[at, :] = part
        else:
            held_ref[at, :] = part
            copies.append(pltpu.make_async_copy(held_ref.at[at, :], send_ref.at[at, :], sems.at[step % 4]))
            copies[-1].start()
    for copy in copies:
        copy.wait()


def join_kernel(keep_ref, theirs_ref, out_ref):
    size = out_ref.shape[2]
    total = (keep_ref[...].astype(F32) + theirs_ref[...].astype(F32)).astype(BF16)
    out_ref[0] = total[:, :size]
    out_ref[1] = total[:, total.shape[1] - size :]


def backward_kernel(
    pick_hbm, x_ref, other_ref, bias_ref, mixed_ref, y_ref, pick_ref, odd_ref, back_ref, out_ref, held_ref, sems
):
    rows, width = mixed_ref.shape
    fetch = pltpu.make_async_copy(pick_hbm, pick_ref, sems.at[7])
    fetch.start()
    copies = []

    def send(start, size):
        lanes = pl.ds(start, size)
        copies.append(pltpu.make_async_copy(held_ref.at[:, lanes], y_ref.at[:, lanes], sems.at[len(copies)]))
        copies[-1].start()

    blocks = FULL // GROUP
    weight = []
    for ref, base in ((x_ref, 4 * width), (other_ref, 0)):
        weight += [ref[:, pl.ds(base + b * width, width)] for b in range(blocks)]
    odd_rows = odd_ref.shape[0] // 2
    for i, (ref, base) in enumerate(((x_ref, 4 * width), (other_ref, 0))):
        left = ref[:, pl.ds(base + blocks * width, ODD_LANES)]
        for q in range(CHUNK):

            def wanted(row):
                source = lax.div(row, jnp.int32(ODD))
                return source * GROUP + CHUNK * (row - ODD * source) + q

            got = dot(selection(odd_rows, rows, wanted), left).astype(BF16)
            for u in range(CHUNK):
                lanes = pl.ds((CHUNK * u + q) * LANES, LANES)
                odd_ref[pl.ds(i * odd_rows, odd_rows), lanes] = got[:, u * LANES : (u + 1) * LANES]
    weight.append(odd_ref[...])
    fetch.wait()
    grad = dot_nt(x_ref[:, pl.ds(3 * width, width)], pick_ref[...]).astype(BF16)
    mixed = mixed_ref[...]
    back = jnp.zeros((rows, width), F32)
    at = 0
    for block in weight:
        size = block.shape[0]
        back = back + dot(grad[:, at : at + size], block)
        out_ref[:, pl.ds(at, size)] = dot_nt(mixed, block).astype(BF16)
        at += size
    back_ref[...] = back.astype(BF16)
    held_ref[:, pl.ds(0, width)] = dot(out_ref[...], pick_ref[...]).astype(BF16)
    send(0, width)
    query_tiles, key_tiles, value_tiles = [Tiles(held_ref, i * width) for i in (1, 2, 3)]
    bias = bias_ref[...]
    sent = 0
    for head in range(HEADS):
        start, size = window(head)
        lanes = head_lanes(head, rows)
        query_win = jnp.where(lanes, x_ref[:, pl.ds(start, size)], 0)
        key_win = jnp.where(lanes, x_ref[:, pl.ds(width + start, size)], 0)
        value_win = x_ref[:, pl.ds(2 * width + start, size)]
        back_win = jnp.where(lanes, back_ref[:, pl.ds(start, size)], 0)
        scores = dot_nt(key_win, query_win) * SCALE + bias
        raised = jnp.exp(scores - jnp.max(scores, axis=0, keepdims=True))
        attention = raised * (1.0 / jnp.sum(raised, axis=0, keepdims=True))
        value_tiles.add(head, dot(attention.astype(BF16), back_win))
        drawn = attention * dot_nt(value_win, back_win)
        inner = jnp.sum(drawn, axis=0, keepdims=True)
        score_grad = ((drawn - attention * inner) * SCALE).astype(BF16)
        key_tiles.add(head, dot(score_grad, query_win))
        query_tiles.add(head, dot_tn(score_grad, key_win))
        if head in (HEADS // 2 - 1, HEADS - 1):
            done = (head + 1) * HEAD_DIM // LANES * LANES
            for i in (1, 2, 3):
                send(i * width + sent, done - sent)
            sent = done
    for copy in copies:
        copy.wait()


def call(kernel, name, outs, args, smem=0, hbm_in=0, hbm_out=(), scratch=(), flops=0):
    space = [pltpu.SMEM] * smem + [pltpu.HBM] * hbm_in + [pltpu.VMEM] * (len(args) - smem - hbm_in)
    args = [pltpu.with_memory_space_constraint(a, s) if s == pltpu.HBM else a for a, s in zip(args, space)]
    shapes = [jax.ShapeDtypeStruct(shape, dtype) for shape, dtype in outs]
    moved = sum(a.size * a.dtype.itemsize for a in args) + sum(math.prod(s.shape) * s.dtype.itemsize for s in shapes)
    return pl.pallas_call(
        kernel,
        out_shape=[pltpu.HBM(s.shape, s.dtype) if i in hbm_out else s for i, s in enumerate(shapes)],
        in_specs=[pl.BlockSpec(memory_space=s) for s in space],
        out_specs=[pl.BlockSpec(memory_space=pltpu.HBM if i in hbm_out else pltpu.VMEM) for i in range(len(outs))],
        scratch_shapes=scratch,
        compiler_params=pltpu.CompilerParams(vmem_limit_bytes=VMEM_LIMIT),
        cost_estimate=pl.CostEstimate(flops=flops, bytes_accessed=moved, transcendentals=0),
        name=name,
    )(*args)


def dma(count):
    return pltpu.SemaphoreType.DMA((count,))


def pack(arrays, weight_t):
    rows, width = arrays[0].shape
    extra = FULL // GROUP * width + ODD_LANES
    outs = [((rows, len(arrays) * width + extra), BF16)]
    scratch = [pltpu.VMEM((len(arrays), rows, width), BF16), pltpu.VMEM((rows, extra), BF16), dma(2 * len(arrays) + 1)]
    return call(pack_kernel, "pack", outs, (*arrays, weight_t), hbm_in=len(arrays), hbm_out=(0,), scratch=scratch)[0]


def tables(core, lengths, rows, width, shard, pitch, positions):
    kernel = functools.partial(tables_kernel, shard, pitch, positions)
    padded = width // shard * pitch
    outs = [((width, width), BF16), ((padded, width), BF16), ((rows, rows), F32)]
    scratch = [pltpu.VMEM((2, padded, width), BF16), dma(2)]
    return call(kernel, "tables", outs, (core, lengths), smem=2, hbm_out=(0, 1), scratch=scratch)


def forward(x, turned, bias):
    rows = x.shape[0]
    padded, width = turned.shape
    half = (padded // 2, width)
    outs = [((rows, width), BF16), (half, BF16), (half, BF16)]
    flops = 4 * padded * rows * width + 4 * HEADS * rows * rows * 256
    scratch = [pltpu.VMEM(turned.shape, BF16), pltpu.VMEM(half, BF16), dma(5)]
    return call(forward_kernel, "forward", outs, (turned, x, bias), hbm_in=1, hbm_out=(2,), scratch=scratch, flops=flops)


def join(keep, theirs):
    rows, width = keep.shape
    return call(join_kernel, "join", [((2, rows, lane_half(width)), BF16)], (keep, theirs))[0]


def backward(pick, x, other, bias, mixed):
    rows, width = mixed.shape
    flops = 8 * width * rows * width + 12 * HEADS * rows * rows * 256
    one = pltpu.VMEM((rows, width), BF16)
    odd = pltpu.VMEM((width - 4 * rows, width), BF16)
    scratch = [pltpu.VMEM((width, width), BF16), odd, one, one, pltpu.VMEM((rows, 4 * width), BF16), dma(8)]
    args = (pick, x, other, bias, mixed)
    outs = [((rows, 4 * width), BF16)]
    return call(backward_kernel, "backward", outs, args, hbm_in=1, hbm_out=(0,), scratch=scratch, flops=flops)[0]


def lane_half(width):
    return (width // LANES + 1) // 2 * LANES


def sum_over_pairs(block, n_dp, width):
    def exchange(block, hop):
        return lax.ppermute(block, "dp", [(i, i ^ hop) for i in range(n_dp)])

    hop = 2
    while hop < n_dp:
        block = (block.astype(F32) + exchange(block, hop).astype(F32)).astype(BF16)
        hop *= 2
    theirs = exchange(block, 1)
    low = jnp.bitwise_and(lax.axis_index("dp"), 1) == 0
    lower, upper = jnp.where(low, block, theirs), jnp.where(low, theirs, block)
    return jnp.concatenate([lower, upper[:, 2 * lower.shape[1] - width :]], axis=1).astype(F32)


def on_device(n_seq, n_dp, queries, key_vectors, value_vectors, out_grad, out_weight, clip_frames):
    patches, width = queries.shape[2:]
    positions = patches // n_seq
    shard = out_weight.shape[1]
    pitch = -(-shard // 8) * 8
    core = jnp.bitwise_and(lax.axis_index("seq"), 1).astype(jnp.int32)

    def swap(block):
        return lax.all_to_all(block.reshape(n_seq, positions, -1), "seq", 0, 0, tiled=True)

    def partner(block):
        return lax.ppermute(block, "seq", [(i, i ^ 1) for i in range(n_seq)])

    arrays = [a.reshape(patches, width) for a in (queries, key_vectors, value_vectors, out_grad)]
    x = swap(pack(arrays, out_weight.T)).reshape(patches, -1)
    pick, turned, bias = tables(core.reshape(1), clip_frames, patches, width, shard, pitch, positions)
    mixed, keep, send = forward(x, turned, bias)

    chip = join(keep, partner(send)).reshape(n_seq, pitch, -1)
    pairs = [
        [(p + d) * n_seq + i for d in (0, 1) for i in range(c, n_seq, 2)] for p in range(0, n_dp, 2) for c in (0, 1)
    ]
    parts = lax.all_to_all(chip, ("dp", "seq"), 0, 0, tiled=True, axis_index_groups=pairs)

    y = backward(pick, x, partner(x[:, 4 * width :]), bias, mixed)
    back = swap(y).reshape(patches, 4 * width)
    total = jnp.sum(parts.astype(F32), axis=0).astype(BF16)
    weight_grad = sum_over_pairs(total, n_dp, width)[:shard].T
    outs = [back[:, i * width : (i + 1) * width].reshape(queries.shape) for i in range(4)]
    return (*outs, weight_grad)


def solution(mesh):
    whole = P("dp", "seq", None, None)
    return jax.shard_map(
        functools.partial(on_device, mesh.shape["seq"], mesh.shape["dp"]),
        mesh=mesh,
        in_specs=(whole, whole, whole, whole, P(None, "seq"), P("dp", None)),
        out_specs=(whole, whole, whole, whole, P(None, "seq")),
        check_vma=False,
    )
```

```python
import functools
import math

import jax
import jax.numpy as jnp
from jax import lax
from jax.experimental import pallas as pl
from jax.experimental.pallas import tpu as pltpu
from jax.sharding import PartitionSpec as P

HEADS = 16
HEAD_DIM = 72
LANES = 128
SCALE = 1.0 / math.sqrt(HEAD_DIM)
F32 = jnp.float32
BF16 = jnp.bfloat16
VMEM_LIMIT = 28 * 1024 * 1024
NT = (((1,), (1,)), ((), ()))
TN = (((0,), (0,)), ((), ()))


def dot(a, b):
    return jnp.dot(a, b, preferred_element_type=F32)


def dot_nt(a, b):
    return lax.dot_general(a, b, NT, preferred_element_type=F32)


def dot_tn(a, b):
    return lax.dot_general(a, b, TN, preferred_element_type=F32)


def window(head):
    first = head * HEAD_DIM // LANES
    last = (head * HEAD_DIM + HEAD_DIM - 1) // LANES
    return first * LANES, (last + 1 - first) * LANES


def head_lanes(head, rows):
    start, size = window(head)
    lane = lax.broadcasted_iota(jnp.int32, (rows, size), 1) + (start - head * HEAD_DIM)
    return (lane >= 0) & (lane < HEAD_DIM)


def clip_bias(lens_ref, rows, positions):
    def ids(axis):
        index = lax.broadcasted_iota(jnp.int32, (rows, rows), axis)
        frame = lax.div(index, jnp.int32(positions))
        clip = jnp.zeros_like(frame)
        end = jnp.int32(0)
        for j in range(lens_ref.shape[1]):
            end = end + lens_ref[0, j]
            clip = clip + jnp.where(frame >= end, 1, 0)
        return clip * positions + (index - frame * positions)

    return jnp.where(ids(0) == ids(1), 0.0, -jnp.inf).astype(F32)


def softmax(query_win, key_win, bias):
    scores = dot_nt(query_win, key_win) * SCALE + bias
    raised = jnp.exp(scores - jnp.max(scores, axis=-1, keepdims=True))
    return raised, 1.0 / jnp.sum(raised, axis=-1, keepdims=True)


class Tiles:
    def __init__(self, ref, base=0):
        self.ref, self.base, self.held = ref, base, {}

    def add(self, head, value):
        start, size = window(head)
        for off in range(0, size, LANES):
            piece = value[:, off : off + LANES]
            tile = start + off
            self.held[tile] = piece if tile not in self.held else self.held[tile] + piece
        done = (head + 1) * HEAD_DIM
        for tile in [t for t in self.held if t + LANES <= done]:
            lanes = pl.ds(self.base + tile, LANES)
            self.ref[:, lanes] = self.held.pop(tile).astype(self.ref.dtype)


GROUP = 8
FULL = 16
ODD = 2
CHUNK = 3
ODD_LANES = 384


def selection(rows, columns, wanted):
    row = lax.broadcasted_iota(jnp.int32, (rows, columns), 0)
    column = lax.broadcasted_iota(jnp.int32, (rows, columns), 1)
    return jnp.where(column == wanted(row), 1.0, 0.0).astype(BF16)


def chunk_tiles(ref, q):
    pieces = [ref[:, pl.ds((CHUNK * u + q) * LANES, LANES)] for u in range(CHUNK)]
    return jnp.concatenate(pieces, axis=1)


def pack_kernel(*refs):
    *parts, weight_hbm, x_ref, staged_ref, weight_ref, held_ref, sems, weight_sems = refs
    rows, width = parts[0].shape
    shard = weight_ref.shape[0]
    half = rows // 2
    fetch_weight = pltpu.make_async_copy(weight_hbm, weight_ref, weight_sems.at[0])
    fetch_weight.start()
    fetches, copies = [], []
    for i, part in enumerate(parts):
        for j in range(2):
            at, lanes, n = pl.ds(j * half, half), pl.ds(i * width, width), 2 * i + j
            fetches.append(pltpu.make_async_copy(part.at[at], staged_ref.at[i, at], sems.at[0, n]))
            copies.append(pltpu.make_async_copy(staged_ref.at[i, at], x_ref.at[at, lanes], sems.at[1, n]))
    for fetch in fetches:
        fetch.start()

    def core(row):
        return jnp.bitwise_and(lax.div(row, jnp.int32(GROUP)), 1)

    def place(row):
        return jnp.bitwise_and(row, GROUP - 1)

    fetch_weight.wait()
    weight = weight_ref[...]
    for block in range(FULL // GROUP):
        pick = selection(rows, shard, lambda row: FULL * core(row) + GROUP * block + place(row))
        held_ref[:, pl.ds(block * width, width)] = dot(pick, weight).astype(BF16)
    for fetch, copy in list(zip(fetches, copies))[:4]:
        fetch.wait()
        copy.start()
    odd = jnp.zeros((rows, ODD_LANES), F32)
    for q in range(CHUNK):

        def wanted(row):
            k = lax.div(place(row) - q, jnp.int32(CHUNK))
            exact = (place(row) == CHUNK * k + q) & (k < ODD)
            return jnp.where(exact, 2 * FULL + ODD * core(row) + k, -1)

        odd = odd + dot(selection(rows, shard, wanted), chunk_tiles(weight_ref, q))
    held_ref[:, pl.ds(FULL // GROUP * width, ODD_LANES)] = odd.astype(BF16)
    lanes = pl.ds(len(parts) * width, held_ref.shape[1])
    last = pltpu.make_async_copy(held_ref, x_ref.at[:, lanes], weight_sems.at[1])
    last.start()
    for fetch, copy in list(zip(fetches, copies))[4:]:
        fetch.wait()
        copy.start()
    for copy in (*copies, last):
        copy.wait()


def pick_rows(ref, place):
    padded, width = ref.shape
    block = padded // 8
    for step in range(8):
        at = lax.broadcasted_iota(jnp.int32, (block, width), 0) + step * block
        ref[pl.ds(step * block, block), :] = jnp.where(at == place, 1.0, 0.0).astype(BF16)


def tables_kernel(shard, positions, core_ref, lens_ref, pick_ref, bias_ref, held_ref, sem):
    width = pick_ref.shape[1]
    feature = lax.broadcasted_iota(jnp.int32, (1, width), 1)
    owner = lax.div(feature, jnp.int32(shard))
    rest = feature - owner * shard
    holder = jnp.where(rest < 2 * FULL, lax.div(rest, jnp.int32(FULL)), lax.div(rest - 2 * FULL, jnp.int32(ODD)))
    other = jnp.bitwise_and(holder + core_ref[0], 1)
    within = rest - FULL * holder
    block = lax.div(within, jnp.int32(GROUP))
    size = width // shard * GROUP
    full = (other * (FULL // GROUP) + block) * size + owner * GROUP + within - block * GROUP
    odd = 2 * (FULL // GROUP) * size + (other * (width // shard) + owner) * ODD + rest - 2 * FULL - ODD * holder
    pick_rows(held_ref, jnp.where(rest < 2 * FULL, full, odd))
    copy = pltpu.make_async_copy(held_ref, pick_ref, sem.at[0])
    copy.start()
    bias_ref[...] = clip_bias(lens_ref, bias_ref.shape[0], positions)
    copy.wait()


def forward_kernel(
    core_ref, x_hbm, bias_ref, mixed_ref, keep_ref, send_ref, rest_ref, x_ref, left_ref, part_ref, held_ref, sems
):
    rows, width = mixed_ref.shape
    middle = lane_half(width)
    pieces = [(a * width + b, c) for b, c in ((0, middle), (middle, width - middle)) for a in range(3)]
    pieces.append((3 * width, width))
    fetches = [
        pltpu.make_async_copy(x_hbm.at[:, pl.ds(at, size)], x_ref.at[:, pl.ds(at, size)], sems.at[5 + i])
        for i, (at, size) in enumerate(pieces)
    ]
    left = pl.ds(4 * width, left_ref.shape[1])
    fetches.append(pltpu.make_async_copy(x_hbm.at[:, left], left_ref, sems.at[5 + len(pieces)]))
    for fetch in fetches:
        fetch.start()
    bias = bias_ref[...]
    mixed_tiles = Tiles(mixed_ref)
    for head in range(HEADS):
        if head in (0, HEADS // 2):
            for fetch in fetches[3 * (head > 0) : 3 * (head > 0) + 3]:
                fetch.wait()
        start, size = window(head)
        lanes = head_lanes(head, rows)
        query_win = jnp.where(lanes, x_ref[:, pl.ds(start, size)], 0)
        key_win = x_ref[:, pl.ds(width + start, size)]
        value_win = jnp.where(lanes, x_ref[:, pl.ds(2 * width + start, size)], 0)
        raised, recip = softmax(query_win, key_win, bias)
        mixed_tiles.add(head, dot((raised * recip).astype(BF16), value_win))
    fetches[7].wait()
    copies = [pltpu.make_async_copy(left_ref, rest_ref, sems.at[4])]
    copies[0].start()
    fetches[6].wait()
    mixed = mixed_ref[...]
    block = 3 * LANES
    for at in range(0, width, block):
        part_ref[pl.ds(at, block), :] = dot_tn(x_ref[:, pl.ds(3 * width + at, block)], mixed)
    chips, pitch, _ = held_ref.shape
    own = core_ref[0] * (width // chips - pitch)
    other = (width // chips - pitch) - own
    for step in range(4):
        some = chips // 4
        for j in range(step * some, (step + 1) * some):
            at = pl.multiple_of(j * (width // chips) + other, 8)
            held_ref[j] = part_ref[pl.ds(at, pitch), :].astype(BF16)
        ids = pl.ds(step * some, some)
        copies.append(pltpu.make_async_copy(held_ref.at[ids], send_ref.at[ids], sems.at[step]))
        copies[-1].start()
    for j in range(chips):
        at = pl.multiple_of(j * (width // chips) + own, 8)
        keep_ref[j] = part_ref[pl.ds(at, pitch), :].astype(BF16)
    for copy in copies:
        copy.wait()


def join_kernel(keep_ref, theirs_ref, out_ref):
    size = out_ref.shape[3]
    total = (keep_ref[...].astype(F32) + theirs_ref[...].astype(F32)).astype(BF16)
    out_ref[0] = total[:, :, :size]
    out_ref[1] = total[:, :, total.shape[2] - size :]


def backward_kernel(
    pick_hbm, x_hbm, own_hbm, other_ref, bias_ref, mixed_ref, y_ref,
    pick_ref, x_ref, own_ref, odd_ref, back_ref, out_ref, held_ref, sems
):
    rows, width = mixed_ref.shape
    three, fourth = pl.ds(0, 3 * width), pl.ds(3 * width, width)
    fetches = [
        pltpu.make_async_copy(own_hbm, own_ref, sems.at[7]),
        pltpu.make_async_copy(pick_hbm, pick_ref, sems.at[8]),
        pltpu.make_async_copy(x_hbm.at[:, fourth], x_ref.at[:, fourth], sems.at[9]),
        pltpu.make_async_copy(x_hbm.at[:, three], x_ref.at[:, three], sems.at[10]),
    ]
    for fetch in fetches:
        fetch.start()
    copies = []

    def send(start, size):
        lanes = pl.ds(start, size)
        copies.append(pltpu.make_async_copy(held_ref.at[:, lanes], y_ref.at[:, lanes], sems.at[len(copies)]))
        copies[-1].start()

    blocks = FULL // GROUP
    fetches[0].wait()
    weight = []
    for ref in (own_ref, other_ref):
        weight += [ref[:, pl.ds(b * width, width)] for b in range(blocks)]
    odd_rows = odd_ref.shape[0] // 2
    for i, ref in enumerate((own_ref, other_ref)):
        left = ref[:, pl.ds(blocks * width, ODD_LANES)]
        for q in range(CHUNK):

            def wanted(row):
                source = lax.div(row, jnp.int32(ODD))
                return source * GROUP + CHUNK * (row - ODD * source) + q

            got = dot(selection(odd_rows, rows, wanted), left).astype(BF16)
            for u in range(CHUNK):
                lanes = pl.ds((CHUNK * u + q) * LANES, LANES)
                odd_ref[pl.ds(i * odd_rows, odd_rows), lanes] = got[:, u * LANES : (u + 1) * LANES]
    weight.append(odd_ref[...])
    fetches[1].wait()
    fetches[2].wait()
    grad = dot_nt(x_ref[:, fourth], pick_ref[...]).astype(BF16)
    mixed = mixed_ref[...]
    back = jnp.zeros((rows, width), F32)
    at = 0
    for block in weight:
        size = block.shape[0]
        back = back + dot(grad[:, at : at + size], block)
        out_ref[:, pl.ds(at, size)] = dot_nt(mixed, block).astype(BF16)
        at += size
    back_ref[...] = back.astype(BF16)
    held_ref[:, pl.ds(0, width)] = dot(out_ref[...], pick_ref[...]).astype(BF16)
    send(0, width)
    query_tiles, key_tiles, value_tiles = [Tiles(held_ref, i * width) for i in (1, 2, 3)]
    bias = bias_ref[...]
    fetches[3].wait()
    sent = 0
    for head in range(HEADS):
        start, size = window(head)
        lanes = head_lanes(head, rows)
        query_win = jnp.where(lanes, x_ref[:, pl.ds(start, size)], 0)
        key_win = jnp.where(lanes, x_ref[:, pl.ds(width + start, size)], 0)
        value_win = x_ref[:, pl.ds(2 * width + start, size)]
        back_win = jnp.where(lanes, back_ref[:, pl.ds(start, size)], 0)
        scores = dot_nt(key_win, query_win) * SCALE + bias
        raised = jnp.exp(scores - jnp.max(scores, axis=0, keepdims=True))
        attention = raised * (1.0 / jnp.sum(raised, axis=0, keepdims=True))
        value_tiles.add(head, dot(attention.astype(BF16), back_win))
        drawn = attention * dot_nt(value_win, back_win)
        inner = jnp.sum(drawn, axis=0, keepdims=True)
        score_grad = ((drawn - attention * inner) * SCALE).astype(BF16)
        key_tiles.add(head, dot(score_grad, query_win))
        query_tiles.add(head, dot_tn(score_grad, key_win))
        if head in (HEADS // 2 - 1, HEADS - 1):
            done = (head + 1) * HEAD_DIM // LANES * LANES
            for i in (1, 2, 3):
                send(i * width + sent, done - sent)
            sent = done
    for copy in copies:
        copy.wait()


def total_kernel(parts_hbm, out_ref, parts_ref, sems):
    count = parts_hbm.shape[0]
    step = count // 4
    fetches = [
        pltpu.make_async_copy(parts_hbm.at[pl.ds(i * step, step)], parts_ref.at[pl.ds(i * step, step)], sems.at[i])
        for i in range(4)
    ]
    for fetch in fetches:
        fetch.start()
    total = jnp.zeros(out_ref.shape, F32)
    for i, fetch in enumerate(fetches):
        fetch.wait()
        for j in range(i * step, (i + 1) * step):
            total = total + parts_ref[j].astype(F32)
    out_ref[...] = total.astype(BF16)


def call(kernel, name, outs, args, smem=0, hbm_in=0, hbm_out=(), scratch=(), flops=0):
    space = [pltpu.SMEM] * smem + [pltpu.HBM] * hbm_in + [pltpu.VMEM] * (len(args) - smem - hbm_in)
    args = [pltpu.with_memory_space_constraint(a, s) if s == pltpu.HBM else a for a, s in zip(args, space)]
    shapes = [jax.ShapeDtypeStruct(shape, dtype) for shape, dtype in outs]
    moved = sum(a.size * a.dtype.itemsize for a in args) + sum(math.prod(s.shape) * s.dtype.itemsize for s in shapes)
    return pl.pallas_call(
        kernel,
        out_shape=[pltpu.HBM(s.shape, s.dtype) if i in hbm_out else s for i, s in enumerate(shapes)],
        in_specs=[pl.BlockSpec(memory_space=s) for s in space],
        out_specs=[pl.BlockSpec(memory_space=pltpu.HBM if i in hbm_out else pltpu.VMEM) for i in range(len(outs))],
        scratch_shapes=scratch,
        compiler_params=pltpu.CompilerParams(vmem_limit_bytes=VMEM_LIMIT),
        cost_estimate=pl.CostEstimate(flops=flops, bytes_accessed=moved, transcendentals=0),
        name=name,
    )(*args)


def dma(count):
    return pltpu.SemaphoreType.DMA((count,))


def pack(arrays, weight_t):
    rows, width = arrays[0].shape
    count = len(arrays)
    extra = FULL // GROUP * width + ODD_LANES
    outs = [((rows, count * width + extra), BF16)]
    scratch = [
        pltpu.VMEM((count, rows, width), BF16),
        pltpu.VMEM(weight_t.shape, BF16),
        pltpu.VMEM((rows, extra), BF16),
        pltpu.SemaphoreType.DMA((2, 2 * count)),
        dma(2),
    ]
    args = (*arrays, weight_t)
    return call(pack_kernel, "pack", outs, args, hbm_in=count + 1, hbm_out=(0,), scratch=scratch)[0]


def tables(core, lengths, rows, width, shard, positions):
    kernel = functools.partial(tables_kernel, shard, positions)
    outs = [((width, width), BF16), ((rows, rows), F32)]
    scratch = [pltpu.VMEM((width, width), BF16), dma(1)]
    return call(kernel, "tables", outs, (core, lengths), smem=2, hbm_out=(0,), scratch=scratch)


def forward(core, x, bias, width, chips):
    rows, wide = x.shape
    pitch = -(-width // chips // 2 // 8) * 8
    part, rest = (chips, pitch, width), (rows, wide - 4 * width)
    outs = [((rows, width), BF16), (part, BF16), (part, BF16), (rest, BF16)]
    flops = 2 * width * rows * width + 4 * HEADS * rows * rows * 256
    scratch = [pltpu.VMEM((rows, 4 * width), BF16), pltpu.VMEM(rest, BF16), pltpu.VMEM((width, width), F32)]
    scratch += [pltpu.VMEM(part, BF16), dma(13)]
    args = (core, x, bias)
    return call(
        forward_kernel, "forward", outs, args, smem=1, hbm_in=1, hbm_out=(2, 3), scratch=scratch, flops=flops
    )


def join(keep, theirs):
    chips, pitch, width = keep.shape
    return call(join_kernel, "join", [((2, chips, pitch, lane_half(width)), BF16)], (keep, theirs))[0]


def backward(pick, x, own, other, bias, mixed):
    rows, width = mixed.shape
    flops = 8 * width * rows * width + 12 * HEADS * rows * rows * 256
    one, wide = (rows, width), (rows, 4 * width)
    shapes = ((width, width), wide, own.shape, (width - 4 * rows, width), one, one, wide)
    scratch = [pltpu.VMEM(shape, BF16) for shape in shapes] + [dma(11)]
    args = (pick, x, own, other, bias, mixed)
    return call(backward_kernel, "backward", [(wide, BF16)], args, hbm_in=3, hbm_out=(0,), scratch=scratch, flops=flops)[0]


def total_of(parts):
    scratch = [pltpu.VMEM(parts.shape, BF16), dma(4)]
    return call(total_kernel, "total", [(parts.shape[1:], BF16)], (parts,), hbm_in=1, scratch=scratch)[0]


def lane_half(width):
    return (width // LANES + 1) // 2 * LANES


def sum_over_pairs(block, n_dp, width):
    def exchange(block, other):
        return lax.ppermute(block, "dp", [(i, other(i)) for i in range(n_dp)])

    def mirrored(i):
        return i ^ (n_dp // 2) if (i + 1) % (n_dp // 2) == 0 else n_dp - 2 - i

    hop = 2
    while hop < n_dp:
        theirs = exchange(block, mirrored if hop == n_dp // 2 else lambda i: i ^ hop)
        block = (block.astype(F32) + theirs.astype(F32)).astype(BF16)
        hop *= 2
    theirs = exchange(block, lambda i: i ^ 1)
    low = jnp.bitwise_and(lax.axis_index("dp"), 1) == 0
    lower, upper = jnp.where(low, block, theirs), jnp.where(low, theirs, block)
    return jnp.concatenate([lower, upper[:, 2 * lower.shape[1] - width :]], axis=1).astype(F32)


def on_device(n_seq, n_dp, queries, key_vectors, value_vectors, out_grad, out_weight, clip_frames):
    patches, width = queries.shape[2:]
    positions = patches // n_seq
    shard = out_weight.shape[1]
    core = jnp.bitwise_and(lax.axis_index("seq"), 1).astype(jnp.int32)

    def swap(block):
        return lax.all_to_all(block.reshape(n_seq, positions, -1), "seq", 0, 0, tiled=True)

    def partner(block):
        return lax.ppermute(block, "seq", [(i, i ^ 1) for i in range(n_seq)])

    arrays = [a.reshape(patches, width) for a in (queries, key_vectors, value_vectors, out_grad)]
    x = swap(pack(arrays, out_weight.T)).reshape(patches, -1)
    pick, bias = tables(core.reshape(1), clip_frames, patches, width, shard, positions)
    mixed, keep, send, own = forward(core.reshape(1), x, bias, width, n_seq // 2)

    chip = join(keep, partner(send))
    chip = chip.reshape(n_seq, *chip.shape[2:])
    pairs = [
        [(p + d) * n_seq + i for d in (0, 1) for i in range(c, n_seq, 2)] for p in range(0, n_dp, 2) for c in (0, 1)
    ]
    parts = lax.all_to_all(chip, ("dp", "seq"), 0, 0, tiled=True, axis_index_groups=pairs)

    y = backward(pick, x, own, partner(own), bias, mixed)
    back = swap(y).reshape(patches, 4 * width)
    total = sum_over_pairs(total_of(parts), n_dp, width)
    weight_grad = jnp.where(core == 0, total[:shard], total[total.shape[0] - shard :]).T
    outs = [back[:, i * width : (i + 1) * width].reshape(queries.shape) for i in range(4)]
    return (*outs, weight_grad)


def solution(mesh):
    whole = P("dp", "seq", None, None)
    return jax.shard_map(
        functools.partial(on_device, mesh.shape["seq"], mesh.shape["dp"]),
        mesh=mesh,
        in_specs=(whole, whole, whole, whole, P(None, "seq"), P("dp", None)),
        out_specs=(whole, whole, whole, whole, P(None, "seq")),
        check_vma=False,
    )
```

```python
import functools
import math

import jax
import jax.numpy as jnp
from jax import lax
from jax.experimental import pallas as pl
from jax.experimental.pallas import tpu as pltpu
from jax.sharding import PartitionSpec as P

HEADS = 16
HEAD_DIM = 72
LANES = 128
SCALE = 1.0 / math.sqrt(HEAD_DIM)
F32 = jnp.float32
BF16 = jnp.bfloat16
VMEM_LIMIT = 28 * 1024 * 1024
NT = (((1,), (1,)), ((), ()))
TN = (((0,), (0,)), ((), ()))


def dot(a, b):
    return jnp.dot(a, b, preferred_element_type=F32)


def dot_nt(a, b):
    return lax.dot_general(a, b, NT, preferred_element_type=F32)


def dot_tn(a, b):
    return lax.dot_general(a, b, TN, preferred_element_type=F32)


def window(head):
    first = head * HEAD_DIM // LANES
    last = (head * HEAD_DIM + HEAD_DIM - 1) // LANES
    return first * LANES, (last + 1 - first) * LANES


def head_lanes(head, rows):
    start, size = window(head)
    lane = lax.broadcasted_iota(jnp.int32, (rows, size), 1) + (start - head * HEAD_DIM)
    return (lane >= 0) & (lane < HEAD_DIM)


def clip_bias(lens_ref, rows, positions):
    def ids(axis):
        index = lax.broadcasted_iota(jnp.int32, (rows, rows), axis)
        frame = lax.div(index, jnp.int32(positions))
        clip = jnp.zeros_like(frame)
        end = jnp.int32(0)
        for j in range(lens_ref.shape[1]):
            end = end + lens_ref[0, j]
            clip = clip + jnp.where(frame >= end, 1, 0)
        return clip * positions + (index - frame * positions)

    return jnp.where(ids(0) == ids(1), 0.0, -jnp.inf).astype(F32)


def softmax(query_win, key_win, bias):
    scores = dot_nt(query_win, key_win) * SCALE + bias
    raised = jnp.exp(scores - jnp.max(scores, axis=-1, keepdims=True))
    return raised, 1.0 / jnp.sum(raised, axis=-1, keepdims=True)


class Tiles:
    def __init__(self, ref, base=0):
        self.ref, self.base, self.held = ref, base, {}

    def add(self, head, value):
        start, size = window(head)
        for off in range(0, size, LANES):
            piece = value[:, off : off + LANES]
            tile = start + off
            self.held[tile] = piece if tile not in self.held else self.held[tile] + piece
        done = (head + 1) * HEAD_DIM
        for tile in [t for t in self.held if t + LANES <= done]:
            lanes = pl.ds(self.base + tile, LANES)
            self.ref[:, lanes] = self.held.pop(tile).astype(self.ref.dtype)


FWD_FLOPS = 10**11
JOIN_FLOPS = 10**9
GROUP = 8
FULL = 16
ODD = 2
CHUNK = 3
ODD_LANES = 384


def selection(rows, columns, wanted):
    row = lax.broadcasted_iota(jnp.int32, (rows, columns), 0)
    column = lax.broadcasted_iota(jnp.int32, (rows, columns), 1)
    return jnp.where(column == wanted(row), 1.0, 0.0).astype(BF16)


def chunk_tiles(ref, q):
    pieces = [ref[:, pl.ds((CHUNK * u + q) * LANES, LANES)] for u in range(CHUNK)]
    return jnp.concatenate(pieces, axis=1)


def pack_kernel(*refs):
    *parts, x_ref, staged_ref, sems = refs
    rows, width = parts[0].shape
    half = rows // 2
    fetches, copies = [], []
    for i, part in enumerate(parts):
        for j in range(2):
            at, lanes, n = pl.ds(j * half, half), pl.ds(i * width, width), 2 * i + j
            fetches.append(pltpu.make_async_copy(part.at[at], staged_ref.at[i, at], sems.at[0, n]))
            copies.append(pltpu.make_async_copy(staged_ref.at[i, at], x_ref.at[at, lanes], sems.at[1, n]))
    for fetch in fetches:
        fetch.start()
    for fetch, copy in zip(fetches, copies):
        fetch.wait()
        copy.start()
    for copy in copies:
        copy.wait()


def spread_kernel(weight_ref, out_ref, held_ref, sem):
    shard, width = weight_ref.shape
    rows = held_ref.shape[0]
    weight = weight_ref[...]

    def core(row):
        return jnp.bitwise_and(lax.div(row, jnp.int32(GROUP)), 1)

    def place(row):
        return jnp.bitwise_and(row, GROUP - 1)

    for block in range(FULL // GROUP):
        pick = selection(rows, shard, lambda row: FULL * core(row) + GROUP * block + place(row))
        held_ref[:, pl.ds(block * width, width)] = dot(pick, weight).astype(BF16)
    odd = jnp.zeros((rows, ODD_LANES), F32)
    for q in range(CHUNK):

        def wanted(row):
            k = lax.div(place(row) - q, jnp.int32(CHUNK))
            exact = (place(row) == CHUNK * k + q) & (k < ODD)
            return jnp.where(exact, 2 * FULL + ODD * core(row) + k, -1)

        odd = odd + dot(selection(rows, shard, wanted), chunk_tiles(weight_ref, q))
    held_ref[:, pl.ds(FULL // GROUP * width, ODD_LANES)] = odd.astype(BF16)
    copy = pltpu.make_async_copy(held_ref, out_ref, sem.at[0])
    copy.start()
    copy.wait()


def pick_rows(ref, place):
    padded, width = ref.shape
    block = padded // 8
    for step in range(8):
        at = lax.broadcasted_iota(jnp.int32, (block, width), 0) + step * block
        ref[pl.ds(step * block, block), :] = jnp.where(at == place, 1.0, 0.0).astype(BF16)


def tables_kernel(shard, positions, core_ref, lens_ref, pick_ref, bias_ref, held_ref, sem):
    width = pick_ref.shape[1]
    feature = lax.broadcasted_iota(jnp.int32, (1, width), 1)
    owner = lax.div(feature, jnp.int32(shard))
    rest = feature - owner * shard
    holder = jnp.where(rest < 2 * FULL, lax.div(rest, jnp.int32(FULL)), lax.div(rest - 2 * FULL, jnp.int32(ODD)))
    other = jnp.bitwise_and(holder + core_ref[0], 1)
    within = rest - FULL * holder
    block = lax.div(within, jnp.int32(GROUP))
    size = width // shard * GROUP
    full = (other * (FULL // GROUP) + block) * size + owner * GROUP + within - block * GROUP
    odd = 2 * (FULL // GROUP) * size + (other * (width // shard) + owner) * ODD + rest - 2 * FULL - ODD * holder
    pick_rows(held_ref, jnp.where(rest < 2 * FULL, full, odd))
    copy = pltpu.make_async_copy(held_ref, pick_ref, sem.at[0])
    copy.start()
    bias_ref[...] = clip_bias(lens_ref, bias_ref.shape[0], positions)
    copy.wait()


def forward_kernel(
    core_ref, x_hbm, bias_ref, mixed_ref, keep_ref, first_ref, second_ref, x_ref, part_ref, held_ref, sems
):
    rows, width = mixed_ref.shape
    middle = lane_half(width)
    pieces = [(a * width + b, c) for b, c in ((0, middle), (middle, width - middle)) for a in range(3)]
    pieces.append((3 * width, width))
    fetches = [
        pltpu.make_async_copy(x_hbm.at[:, pl.ds(at, size)], x_ref.at[:, pl.ds(at, size)], sems.at[5 + i])
        for i, (at, size) in enumerate(pieces)
    ]
    for fetch in fetches:
        fetch.start()
    bias = bias_ref[...]
    mixed_tiles = Tiles(mixed_ref)
    for head in range(HEADS):
        if head in (0, HEADS // 2):
            for fetch in fetches[3 * (head > 0) : 3 * (head > 0) + 3]:
                fetch.wait()
        start, size = window(head)
        lanes = head_lanes(head, rows)
        query_win = jnp.where(lanes, x_ref[:, pl.ds(start, size)], 0)
        key_win = x_ref[:, pl.ds(width + start, size)]
        value_win = jnp.where(lanes, x_ref[:, pl.ds(2 * width + start, size)], 0)
        raised, recip = softmax(query_win, key_win, bias)
        mixed_tiles.add(head, dot((raised * recip).astype(BF16), value_win))
    copies = []
    fetches[6].wait()
    mixed = mixed_ref[...]
    block = 3 * LANES
    for at in range(0, width, block):
        part_ref[pl.ds(at, block), :] = dot_tn(x_ref[:, pl.ds(3 * width + at, block)], mixed)
    chips, pitch, _ = held_ref.shape
    own = core_ref[0] * (width // chips - pitch)
    other = (width // chips - pitch) - own
    for step in range(4):
        some = chips // 4
        for j in range(step * some, (step + 1) * some):
            at = pl.multiple_of(j * (width // chips) + other, 8)
            held_ref[j] = part_ref[pl.ds(at, pitch), :].astype(BF16)
        source, place = pl.ds(step * some, some), pl.ds(step % 2 * some, some)
        send_ref = first_ref if step < 2 else second_ref
        copies.append(pltpu.make_async_copy(held_ref.at[source], send_ref.at[place], sems.at[step]))
        copies[-1].start()
    for j in range(chips):
        at = pl.multiple_of(j * (width // chips) + own, 8)
        keep_ref[j] = part_ref[pl.ds(at, pitch), :].astype(BF16)
    for copy in copies:
        copy.wait()


def join_kernel(keep_ref, first_ref, second_ref, out_ref):
    size = out_ref.shape[3]
    half = first_ref.shape[0]
    for at, ref in ((0, first_ref), (half, second_ref)):
        rows = pl.ds(at, half)
        total = (keep_ref[rows].astype(F32) + ref[...].astype(F32)).astype(BF16)
        out_ref[0, rows] = total[:, :, :size]
        out_ref[1, rows] = total[:, :, total.shape[2] - size :]


def backward_kernel(
    pick_hbm, x_hbm, own_hbm, other_ref, bias_ref, mixed_ref, y_ref,
    pick_ref, x_ref, own_ref, odd_ref, back_ref, out_ref, held_ref, sems
):
    rows, width = mixed_ref.shape
    three, fourth = pl.ds(0, 3 * width), pl.ds(3 * width, width)
    fetches = [
        pltpu.make_async_copy(own_hbm, own_ref, sems.at[7]),
        pltpu.make_async_copy(pick_hbm, pick_ref, sems.at[8]),
        pltpu.make_async_copy(x_hbm.at[:, fourth], x_ref.at[:, fourth], sems.at[9]),
        pltpu.make_async_copy(x_hbm.at[:, three], x_ref.at[:, three], sems.at[10]),
    ]
    for fetch in fetches:
        fetch.start()
    copies = []

    def send(start, size):
        lanes = pl.ds(start, size)
        copies.append(pltpu.make_async_copy(held_ref.at[:, lanes], y_ref.at[:, lanes], sems.at[len(copies)]))
        copies[-1].start()

    blocks = FULL // GROUP
    fetches[0].wait()
    weight = []
    for ref in (own_ref, other_ref):
        weight += [ref[:, pl.ds(b * width, width)] for b in range(blocks)]
    odd_rows = odd_ref.shape[0] // 2
    for i, ref in enumerate((own_ref, other_ref)):
        left = ref[:, pl.ds(blocks * width, ODD_LANES)]
        for q in range(CHUNK):

            def wanted(row):
                source = lax.div(row, jnp.int32(ODD))
                return source * GROUP + CHUNK * (row - ODD * source) + q

            got = dot(selection(odd_rows, rows, wanted), left).astype(BF16)
            for u in range(CHUNK):
                lanes = pl.ds((CHUNK * u + q) * LANES, LANES)
                odd_ref[pl.ds(i * odd_rows, odd_rows), lanes] = got[:, u * LANES : (u + 1) * LANES]
    weight.append(odd_ref[...])
    fetches[1].wait()
    fetches[2].wait()
    grad = dot_nt(x_ref[:, fourth], pick_ref[...]).astype(BF16)
    mixed = mixed_ref[...]
    back = jnp.zeros((rows, width), F32)
    at = 0
    for block in weight:
        size = block.shape[0]
        back = back + dot(grad[:, at : at + size], block)
        out_ref[:, pl.ds(at, size)] = dot_nt(mixed, block).astype(BF16)
        at += size
    back_ref[...] = back.astype(BF16)
    held_ref[:, pl.ds(0, width)] = dot(out_ref[...], pick_ref[...]).astype(BF16)
    send(0, width)
    query_tiles, key_tiles, value_tiles = [Tiles(held_ref, i * width) for i in (1, 2, 3)]
    bias = bias_ref[...]
    fetches[3].wait()
    sent = 0
    for head in range(HEADS):
        start, size = window(head)
        lanes = head_lanes(head, rows)
        query_win = jnp.where(lanes, x_ref[:, pl.ds(start, size)], 0)
        key_win = jnp.where(lanes, x_ref[:, pl.ds(width + start, size)], 0)
        value_win = x_ref[:, pl.ds(2 * width + start, size)]
        back_win = jnp.where(lanes, back_ref[:, pl.ds(start, size)], 0)
        scores = dot_nt(key_win, query_win) * SCALE + bias
        raised = jnp.exp(scores - jnp.max(scores, axis=0, keepdims=True))
        attention = raised * (1.0 / jnp.sum(raised, axis=0, keepdims=True))
        value_tiles.add(head, dot(attention.astype(BF16), back_win))
        drawn = attention * dot_nt(value_win, back_win)
        inner = jnp.sum(drawn, axis=0, keepdims=True)
        score_grad = ((drawn - attention * inner) * SCALE).astype(BF16)
        key_tiles.add(head, dot(score_grad, query_win))
        query_tiles.add(head, dot_tn(score_grad, key_win))
        if head in (HEADS // 2 - 1, HEADS - 1):
            done = (head + 1) * HEAD_DIM // LANES * LANES
            for i in (1, 2, 3):
                send(i * width + sent, done - sent)
            sent = done
    for copy in copies:
        copy.wait()


def total_kernel(parts_hbm, out_ref, parts_ref, sems):
    count = parts_hbm.shape[0]
    step = count // 4
    fetches = [
        pltpu.make_async_copy(parts_hbm.at[pl.ds(i * step, step)], parts_ref.at[pl.ds(i * step, step)], sems.at[i])
        for i in range(4)
    ]
    for fetch in fetches:
        fetch.start()
    total = jnp.zeros(out_ref.shape, F32)
    for i, fetch in enumerate(fetches):
        fetch.wait()
        for j in range(i * step, (i + 1) * step):
            total = total + parts_ref[j].astype(F32)
    out_ref[...] = total.astype(BF16)


def call(kernel, name, outs, args, smem=0, hbm_in=0, hbm_out=(), scratch=(), flops=0):
    space = [pltpu.SMEM] * smem + [pltpu.HBM] * hbm_in + [pltpu.VMEM] * (len(args) - smem - hbm_in)
    args = [pltpu.with_memory_space_constraint(a, s) if s == pltpu.HBM else a for a, s in zip(args, space)]
    shapes = [jax.ShapeDtypeStruct(shape, dtype) for shape, dtype in outs]
    moved = sum(a.size * a.dtype.itemsize for a in args) + sum(math.prod(s.shape) * s.dtype.itemsize for s in shapes)
    return pl.pallas_call(
        kernel,
        out_shape=[pltpu.HBM(s.shape, s.dtype) if i in hbm_out else s for i, s in enumerate(shapes)],
        in_specs=[pl.BlockSpec(memory_space=s) for s in space],
        out_specs=[pl.BlockSpec(memory_space=pltpu.HBM if i in hbm_out else pltpu.VMEM) for i in range(len(outs))],
        scratch_shapes=scratch,
        compiler_params=pltpu.CompilerParams(vmem_limit_bytes=VMEM_LIMIT),
        cost_estimate=pl.CostEstimate(flops=flops, bytes_accessed=0 if flops else moved, transcendentals=0),
        name=name,
    )(*args)


def dma(count):
    return pltpu.SemaphoreType.DMA((count,))


def pack(arrays):
    rows, width = arrays[0].shape
    count = len(arrays)
    outs = [((rows, count * width), BF16)]
    scratch = [pltpu.VMEM((count, rows, width), BF16), pltpu.SemaphoreType.DMA((2, 2 * count))]
    return call(pack_kernel, "pack", outs, arrays, hbm_in=count, hbm_out=(0,), scratch=scratch)[0]


def spread(weight_t, rows):
    shape = (rows, FULL // GROUP * weight_t.shape[1] + ODD_LANES)
    scratch = [pltpu.VMEM(shape, BF16), dma(1)]
    return call(spread_kernel, "spread", [(shape, BF16)], (weight_t,), hbm_out=(0,), scratch=scratch)[0]


def tables(core, lengths, rows, width, shard, positions):
    kernel = functools.partial(tables_kernel, shard, positions)
    outs = [((width, width), BF16), ((rows, rows), F32)]
    scratch = [pltpu.VMEM((width, width), BF16), dma(1)]
    return call(kernel, "tables", outs, (core, lengths), smem=2, hbm_out=(0,), scratch=scratch)


def forward(core, x, bias, width, chips):
    rows = x.shape[0]
    pitch = -(-width // chips // 2 // 8) * 8
    part, half = (chips, pitch, width), (chips // 2, pitch, width)
    outs = [((rows, width), BF16), (part, BF16), (half, BF16), (half, BF16)]
    scratch = [pltpu.VMEM(x.shape, BF16), pltpu.VMEM((width, width), F32), pltpu.VMEM(part, BF16), dma(12)]
    args = (core, x, bias)
    return call(
        forward_kernel, "forward", outs, args, smem=1, hbm_in=1, hbm_out=(2, 3), scratch=scratch, flops=FWD_FLOPS
    )


def join(keep, first, second):
    chips, pitch, width = keep.shape
    outs = [((2, chips, pitch, lane_half(width)), BF16)]
    return call(join_kernel, "join", outs, (keep, first, second), flops=JOIN_FLOPS)[0]


def backward(pick, x, own, other, bias, mixed):
    rows, width = mixed.shape
    flops = 8 * width * rows * width + 12 * HEADS * rows * rows * 256
    one, wide = (rows, width), (rows, 4 * width)
    shapes = ((width, width), wide, own.shape, (width - 4 * rows, width), one, one, wide)
    scratch = [pltpu.VMEM(shape, BF16) for shape in shapes] + [dma(11)]
    args = (pick, x, own, other, bias, mixed)
    return call(backward_kernel, "backward", [(wide, BF16)], args, hbm_in=3, hbm_out=(0,), scratch=scratch, flops=flops)[0]


def total_of(parts):
    scratch = [pltpu.VMEM(parts.shape, BF16), dma(4)]
    return call(total_kernel, "total", [(parts.shape[1:], BF16)], (parts,), hbm_in=1, scratch=scratch)[0]


def lane_half(width):
    return (width // LANES + 1) // 2 * LANES


def sum_over_pairs(block, n_dp, width):
    def exchange(block, other):
        return lax.ppermute(block, "dp", [(i, other(i)) for i in range(n_dp)])

    def mirrored(i):
        return n_dp - i - (2 if i % 2 == 0 else 0)

    hop = 2
    while hop < n_dp:
        theirs = exchange(block, mirrored if hop == n_dp // 2 else lambda i: i ^ hop)
        block = (block.astype(F32) + theirs.astype(F32)).astype(BF16)
        hop *= 2
    theirs = exchange(block, lambda i: i ^ 1)
    low = jnp.bitwise_and(lax.axis_index("dp"), 1) == 0
    lower, upper = jnp.where(low, block, theirs), jnp.where(low, theirs, block)
    return jnp.concatenate([lower, upper[:, 2 * lower.shape[1] - width :]], axis=1).astype(F32)


def on_device(n_seq, n_dp, queries, key_vectors, value_vectors, out_grad, out_weight, clip_frames):
    patches, width = queries.shape[2:]
    positions = patches // n_seq
    shard = out_weight.shape[1]
    core = jnp.bitwise_and(lax.axis_index("seq"), 1).astype(jnp.int32)

    def swap(block):
        return lax.all_to_all(block.reshape(n_seq, positions, -1), "seq", 0, 0, tiled=True)

    def partner(block):
        return lax.ppermute(block, "seq", [(i, i ^ 1) for i in range(n_seq)])

    arrays = [a.reshape(patches, width) for a in (queries, key_vectors, value_vectors, out_grad)]
    x = swap(pack(arrays)).reshape(patches, -1)
    rows, x = lax.optimization_barrier((spread(out_weight.T, patches), x))
    own = swap(rows).reshape(patches, -1)
    pick, bias = tables(core.reshape(1), clip_frames, patches, width, shard, positions)
    mixed, keep, *send = forward(core.reshape(1), x, bias, width, n_seq // 2)

    chip = join(keep, *[partner(block) for block in send])
    chip = chip.reshape(n_seq, *chip.shape[2:])
    pairs = [
        [(p + d) * n_seq + i for d in (0, 1) for i in range(c, n_seq, 2)] for p in range(0, n_dp, 2) for c in (0, 1)
    ]
    parts = lax.all_to_all(chip, ("dp", "seq"), 0, 0, tiled=True, axis_index_groups=pairs)

    y = backward(pick, x, own, partner(own), bias, mixed)
    total, y = lax.optimization_barrier((total_of(parts), y))
    back = swap(y).reshape(patches, 4 * width)
    total = sum_over_pairs(total, n_dp, width)
    weight_grad = jnp.where(core == 0, total[:shard], total[total.shape[0] - shard :]).T
    outs = [back[:, i * width : (i + 1) * width].reshape(queries.shape) for i in range(4)]
    return (*outs, weight_grad)


def solution(mesh):
    whole = P("dp", "seq", None, None)
    return jax.shard_map(
        functools.partial(on_device, mesh.shape["seq"], mesh.shape["dp"]),
        mesh=mesh,
        in_specs=(whole, whole, whole, whole, P(None, "seq"), P("dp", None)),
        out_specs=(whole, whole, whole, whole, P(None, "seq")),
        check_vma=False,
    )
```

```python
import functools
import math

import jax
import jax.numpy as jnp
from jax import lax
from jax.experimental import pallas as pl
from jax.experimental.pallas import tpu as pltpu
from jax.sharding import PartitionSpec as P

HEADS = 16
HEAD_DIM = 72
LANES = 128
SCALE = 1.0 / math.sqrt(HEAD_DIM)
F32 = jnp.float32
BF16 = jnp.bfloat16
VMEM_LIMIT = 28 * 1024 * 1024
NT = (((1,), (1,)), ((), ()))
TN = (((0,), (0,)), ((), ()))


def dot(a, b):
    return jnp.dot(a, b, preferred_element_type=F32)


def dot_nt(a, b):
    return lax.dot_general(a, b, NT, preferred_element_type=F32)


def dot_tn(a, b):
    return lax.dot_general(a, b, TN, preferred_element_type=F32)


def window(head):
    first = head * HEAD_DIM // LANES
    last = (head * HEAD_DIM + HEAD_DIM - 1) // LANES
    return first * LANES, (last + 1 - first) * LANES


def head_lanes(head, rows):
    start, size = window(head)
    lane = lax.broadcasted_iota(jnp.int32, (rows, size), 1) + (start - head * HEAD_DIM)
    return (lane >= 0) & (lane < HEAD_DIM)


def clip_bias(lens_ref, rows, positions):
    def ids(axis):
        index = lax.broadcasted_iota(jnp.int32, (rows, rows), axis)
        frame = lax.div(index, jnp.int32(positions))
        clip = jnp.zeros_like(frame)
        end = jnp.int32(0)
        for j in range(lens_ref.shape[1]):
            end = end + lens_ref[0, j]
            clip = clip + jnp.where(frame >= end, 1, 0)
        return clip * positions + (index - frame * positions)

    return jnp.where(ids(0) == ids(1), 0.0, -jnp.inf).astype(F32)


def softmax(query_win, key_win, bias):
    scores = dot_nt(query_win, key_win) * SCALE + bias
    raised = jnp.exp(scores - jnp.max(scores, axis=-1, keepdims=True))
    return raised, 1.0 / jnp.sum(raised, axis=-1, keepdims=True)


class Tiles:
    def __init__(self, ref, base=0):
        self.ref, self.base, self.held = ref, base, {}

    def add(self, head, value):
        start, size = window(head)
        for off in range(0, size, LANES):
            piece = value[:, off : off + LANES]
            tile = start + off
            self.held[tile] = piece if tile not in self.held else self.held[tile] + piece
        done = (head + 1) * HEAD_DIM
        for tile in [t for t in self.held if t + LANES <= done]:
            lanes = pl.ds(self.base + tile, LANES)
            self.ref[:, lanes] = self.held.pop(tile).astype(self.ref.dtype)


FWD_FLOPS = 10**11
JOIN_FLOPS = 10**9
GROUP = 8
FULL = 16
ODD = 2
CHUNK = 3
ODD_LANES = 384


def selection(rows, columns, wanted):
    row = lax.broadcasted_iota(jnp.int32, (rows, columns), 0)
    column = lax.broadcasted_iota(jnp.int32, (rows, columns), 1)
    return jnp.where(column == wanted(row), 1.0, 0.0).astype(BF16)


def chunk_tiles(ref, q):
    pieces = [ref[:, pl.ds((CHUNK * u + q) * LANES, LANES)] for u in range(CHUNK)]
    return jnp.concatenate(pieces, axis=1)


def pack_kernel(*refs):
    *parts, x_ref, staged_ref, sems = refs
    rows, width = parts[0].shape
    half = rows // 2
    fetches, copies = [], []
    for i, part in enumerate(parts):
        for j in range(2):
            at, lanes, n = pl.ds(j * half, half), pl.ds(i * width, width), 2 * i + j
            fetches.append(pltpu.make_async_copy(part.at[at], staged_ref.at[i, at], sems.at[0, n]))
            copies.append(pltpu.make_async_copy(staged_ref.at[i, at], x_ref.at[at, lanes], sems.at[1, n]))
    for fetch in fetches:
        fetch.start()
    for fetch, copy in zip(fetches, copies):
        fetch.wait()
        copy.start()
    for copy in copies:
        copy.wait()


def spread_kernel(weight_ref, out_ref, held_ref, sem):
    shard, width = weight_ref.shape
    rows = held_ref.shape[0]
    weight = weight_ref[...]

    def core(row):
        return jnp.bitwise_and(lax.div(row, jnp.int32(GROUP)), 1)

    def place(row):
        return jnp.bitwise_and(row, GROUP - 1)

    for block in range(FULL // GROUP):
        pick = selection(rows, shard, lambda row: FULL * core(row) + GROUP * block + place(row))
        held_ref[:, pl.ds(block * width, width)] = dot(pick, weight).astype(BF16)
    odd = jnp.zeros((rows, ODD_LANES), F32)
    for q in range(CHUNK):

        def wanted(row):
            k = lax.div(place(row) - q, jnp.int32(CHUNK))
            exact = (place(row) == CHUNK * k + q) & (k < ODD)
            return jnp.where(exact, 2 * FULL + ODD * core(row) + k, -1)

        odd = odd + dot(selection(rows, shard, wanted), chunk_tiles(weight_ref, q))
    held_ref[:, pl.ds(FULL // GROUP * width, ODD_LANES)] = odd.astype(BF16)
    copy = pltpu.make_async_copy(held_ref, out_ref, sem.at[0])
    copy.start()
    copy.wait()


def pick_rows(ref, place):
    padded, width = ref.shape
    block = padded // 8
    for step in range(8):
        at = lax.broadcasted_iota(jnp.int32, (block, width), 0) + step * block
        ref[pl.ds(step * block, block), :] = jnp.where(at == place, 1.0, 0.0).astype(BF16)


def tables_kernel(shard, positions, core_ref, lens_ref, pick_ref, bias_ref, held_ref, sem):
    width = pick_ref.shape[1]
    feature = lax.broadcasted_iota(jnp.int32, (1, width), 1)
    owner = lax.div(feature, jnp.int32(shard))
    rest = feature - owner * shard
    holder = jnp.where(rest < 2 * FULL, lax.div(rest, jnp.int32(FULL)), lax.div(rest - 2 * FULL, jnp.int32(ODD)))
    other = jnp.bitwise_and(holder + core_ref[0], 1)
    within = rest - FULL * holder
    block = lax.div(within, jnp.int32(GROUP))
    size = width // shard * GROUP
    full = (other * (FULL // GROUP) + block) * size + owner * GROUP + within - block * GROUP
    odd = 2 * (FULL // GROUP) * size + (other * (width // shard) + owner) * ODD + rest - 2 * FULL - ODD * holder
    pick_rows(held_ref, jnp.where(rest < 2 * FULL, full, odd))
    copy = pltpu.make_async_copy(held_ref, pick_ref, sem.at[0])
    copy.start()
    bias_ref[...] = clip_bias(lens_ref, bias_ref.shape[0], positions)
    copy.wait()


def forward_kernel(
    core_ref, x_hbm, bias_ref, mixed_ref, keep_ref, first_ref, second_ref, x_ref, part_ref, held_ref, sems
):
    rows, width = mixed_ref.shape
    middle = lane_half(width)
    pieces = [(a * width + b, c) for b, c in ((0, middle), (middle, width - middle)) for a in range(3)]
    pieces.append((3 * width, width))
    fetches = [
        pltpu.make_async_copy(x_hbm.at[:, pl.ds(at, size)], x_ref.at[:, pl.ds(at, size)], sems.at[5 + i])
        for i, (at, size) in enumerate(pieces)
    ]
    for fetch in fetches:
        fetch.start()
    bias = bias_ref[...]
    mixed_tiles = Tiles(mixed_ref)
    for head in range(HEADS):
        if head in (0, HEADS // 2):
            for fetch in fetches[3 * (head > 0) : 3 * (head > 0) + 3]:
                fetch.wait()
        start, size = window(head)
        lanes = head_lanes(head, rows)
        query_win = jnp.where(lanes, x_ref[:, pl.ds(start, size)], 0)
        key_win = x_ref[:, pl.ds(width + start, size)]
        value_win = jnp.where(lanes, x_ref[:, pl.ds(2 * width + start, size)], 0)
        raised, recip = softmax(query_win, key_win, bias)
        mixed_tiles.add(head, dot((raised * recip).astype(BF16), value_win))
    copies = []
    fetches[6].wait()
    mixed = mixed_ref[...]
    block = 3 * LANES
    for at in range(0, width, block):
        part_ref[pl.ds(at, block), :] = dot_tn(x_ref[:, pl.ds(3 * width + at, block)], mixed)
    chips, pitch, _ = held_ref.shape
    own = core_ref[0] * (width // chips - pitch)
    other = (width // chips - pitch) - own
    for step in range(4):
        some = chips // 4
        for j in range(step * some, (step + 1) * some):
            at = pl.multiple_of(j * (width // chips) + other, 8)
            held_ref[j] = part_ref[pl.ds(at, pitch), :].astype(BF16)
        source, place = pl.ds(step * some, some), pl.ds(step % 2 * some, some)
        send_ref = first_ref if step < 2 else second_ref
        copies.append(pltpu.make_async_copy(held_ref.at[source], send_ref.at[place], sems.at[step]))
        copies[-1].start()
    for j in range(chips):
        at = pl.multiple_of(j * (width // chips) + own, 8)
        keep_ref[j] = part_ref[pl.ds(at, pitch), :].astype(BF16)
    for copy in copies:
        copy.wait()


def join_kernel(keep_ref, first_ref, second_ref, out_ref):
    width = keep_ref.shape[2]
    size = lane_half(width)
    half = first_ref.shape[0]
    for at, ref in ((0, first_ref), (half, second_ref)):
        ids = pl.ds(at, half)
        total = keep_ref[ids].astype(F32) + ref[...].astype(F32)
        groups = [total[:, i * 8 : i * 8 + 8, :].astype(BF16) for i in range(5)]
        for d, whole, rest in ((0, (0, 1), groups[2][:, :, :size]), (1, (3, 4), groups[2][:, :, width - size :])):
            for i, group in enumerate(whole):
                out_ref[d, ids, :, pl.ds(i * width, width)] = groups[group]
            out_ref[d, ids, :, pl.ds(2 * width, size)] = rest


def finish_kernel(place_ref, mine_ref, far_ref, near_other_ref, far_other_ref, out_ref, held_ref):
    shard, width = out_ref.shape
    size = lane_half(width)
    mine = mine_ref[...].astype(F32) + far_ref[...].astype(F32)
    other = near_other_ref[...].astype(F32) + far_other_ref[...].astype(F32)
    low = place_ref[0] == 0
    lower, upper = jnp.where(low, mine, other), jnp.where(low, other, mine)
    for half, groups in ((lower, (0, 1)), (upper, (3, 4))):
        for i, group in enumerate(groups):
            held_ref[pl.ds(group * 8, 8), :] = half[:, i * width : (i + 1) * width]
    held_ref[pl.ds(16, 8), pl.ds(0, size)] = lower[:, 2 * width :]
    held_ref[pl.ds(16, 8), pl.ds(size, width - size)] = upper[:, 2 * width + 2 * size - width :]
    rows = held_ref.shape[0]
    out_ref[...] = jnp.where(place_ref[1] == 0, held_ref[pl.ds(0, shard), :], held_ref[pl.ds(rows - shard, shard), :])


def backward_kernel(
    pick_hbm, x_hbm, own_hbm, other_ref, bias_ref, mixed_ref, y_ref,
    pick_ref, x_ref, own_ref, odd_ref, back_ref, out_ref, held_ref, sems
):
    rows, width = mixed_ref.shape
    three, fourth = pl.ds(0, 3 * width), pl.ds(3 * width, width)
    fetches = [
        pltpu.make_async_copy(own_hbm, own_ref, sems.at[7]),
        pltpu.make_async_copy(pick_hbm, pick_ref, sems.at[8]),
        pltpu.make_async_copy(x_hbm.at[:, fourth], x_ref.at[:, fourth], sems.at[9]),
        pltpu.make_async_copy(x_hbm.at[:, three], x_ref.at[:, three], sems.at[10]),
    ]
    for fetch in fetches:
        fetch.start()
    copies = []

    def send(start, size):
        lanes = pl.ds(start, size)
        copies.append(pltpu.make_async_copy(held_ref.at[:, lanes], y_ref.at[:, lanes], sems.at[len(copies)]))
        copies[-1].start()

    blocks = FULL // GROUP
    fetches[0].wait()
    weight = []
    for ref in (own_ref, other_ref):
        weight += [ref[:, pl.ds(b * width, width)] for b in range(blocks)]
    odd_rows = odd_ref.shape[0] // 2
    for i, ref in enumerate((own_ref, other_ref)):
        left = ref[:, pl.ds(blocks * width, ODD_LANES)]
        for q in range(CHUNK):

            def wanted(row):
                source = lax.div(row, jnp.int32(ODD))
                return source * GROUP + CHUNK * (row - ODD * source) + q

            got = dot(selection(odd_rows, rows, wanted), left).astype(BF16)
            for u in range(CHUNK):
                lanes = pl.ds((CHUNK * u + q) * LANES, LANES)
                odd_ref[pl.ds(i * odd_rows, odd_rows), lanes] = got[:, u * LANES : (u + 1) * LANES]
    weight.append(odd_ref[...])
    fetches[1].wait()
    fetches[2].wait()
    grad = dot_nt(x_ref[:, fourth], pick_ref[...]).astype(BF16)
    mixed = mixed_ref[...]
    back = jnp.zeros((rows, width), F32)
    at = 0
    for block in weight:
        size = block.shape[0]
        back = back + dot(grad[:, at : at + size], block)
        out_ref[:, pl.ds(at, size)] = dot_nt(mixed, block).astype(BF16)
        at += size
    back_ref[...] = back.astype(BF16)
    held_ref[:, pl.ds(0, width)] = dot(out_ref[...], pick_ref[...]).astype(BF16)
    send(0, width)
    query_tiles, key_tiles, value_tiles = [Tiles(held_ref, i * width) for i in (1, 2, 3)]
    bias = bias_ref[...]
    fetches[3].wait()
    sent = 0
    for head in range(HEADS):
        start, size = window(head)
        lanes = head_lanes(head, rows)
        query_win = jnp.where(lanes, x_ref[:, pl.ds(start, size)], 0)
        key_win = jnp.where(lanes, x_ref[:, pl.ds(width + start, size)], 0)
        value_win = x_ref[:, pl.ds(2 * width + start, size)]
        back_win = jnp.where(lanes, back_ref[:, pl.ds(start, size)], 0)
        scores = dot_nt(key_win, query_win) * SCALE + bias
        raised = jnp.exp(scores - jnp.max(scores, axis=0, keepdims=True))
        attention = raised * (1.0 / jnp.sum(raised, axis=0, keepdims=True))
        value_tiles.add(head, dot(attention.astype(BF16), back_win))
        drawn = attention * dot_nt(value_win, back_win)
        inner = jnp.sum(drawn, axis=0, keepdims=True)
        score_grad = ((drawn - attention * inner) * SCALE).astype(BF16)
        key_tiles.add(head, dot(score_grad, query_win))
        query_tiles.add(head, dot_tn(score_grad, key_win))
        if head in (HEADS // 2 - 1, HEADS - 1):
            done = (head + 1) * HEAD_DIM // LANES * LANES
            for i in (1, 2, 3):
                send(i * width + sent, done - sent)
            sent = done
    for copy in copies:
        copy.wait()


def total_kernel(parts_hbm, out_ref, parts_ref, sems):
    count = parts_hbm.shape[0]
    step = count // 4
    fetches = [
        pltpu.make_async_copy(parts_hbm.at[pl.ds(i * step, step)], parts_ref.at[pl.ds(i * step, step)], sems.at[i])
        for i in range(4)
    ]
    for fetch in fetches:
        fetch.start()
    total = jnp.zeros(out_ref.shape, F32)
    for i, fetch in enumerate(fetches):
        fetch.wait()
        for j in range(i * step, (i + 1) * step):
            total = total + parts_ref[j].astype(F32)
    out_ref[...] = total.astype(BF16)


def call(kernel, name, outs, args, smem=0, hbm_in=0, hbm_out=(), scratch=(), flops=0):
    space = [pltpu.SMEM] * smem + [pltpu.HBM] * hbm_in + [pltpu.VMEM] * (len(args) - smem - hbm_in)
    args = [pltpu.with_memory_space_constraint(a, s) if s == pltpu.HBM else a for a, s in zip(args, space)]
    shapes = [jax.ShapeDtypeStruct(shape, dtype) for shape, dtype in outs]
    moved = sum(a.size * a.dtype.itemsize for a in args) + sum(math.prod(s.shape) * s.dtype.itemsize for s in shapes)
    return pl.pallas_call(
        kernel,
        out_shape=[pltpu.HBM(s.shape, s.dtype) if i in hbm_out else s for i, s in enumerate(shapes)],
        in_specs=[pl.BlockSpec(memory_space=s) for s in space],
        out_specs=[pl.BlockSpec(memory_space=pltpu.HBM if i in hbm_out else pltpu.VMEM) for i in range(len(outs))],
        scratch_shapes=scratch,
        compiler_params=pltpu.CompilerParams(vmem_limit_bytes=VMEM_LIMIT),
        cost_estimate=pl.CostEstimate(flops=flops, bytes_accessed=0 if flops else moved, transcendentals=0),
        name=name,
    )(*args)


def dma(count):
    return pltpu.SemaphoreType.DMA((count,))


def pack(arrays):
    rows, width = arrays[0].shape
    count = len(arrays)
    outs = [((rows, count * width), BF16)]
    scratch = [pltpu.VMEM((count, rows, width), BF16), pltpu.SemaphoreType.DMA((2, 2 * count))]
    return call(pack_kernel, "pack", outs, arrays, hbm_in=count, hbm_out=(0,), scratch=scratch)[0]


def spread(weight_t, rows):
    shape = (rows, FULL // GROUP * weight_t.shape[1] + ODD_LANES)
    scratch = [pltpu.VMEM(shape, BF16), dma(1)]
    return call(spread_kernel, "spread", [(shape, BF16)], (weight_t,), hbm_out=(0,), scratch=scratch)[0]


def tables(core, lengths, rows, width, shard, positions):
    kernel = functools.partial(tables_kernel, shard, positions)
    outs = [((width, width), BF16), ((rows, rows), F32)]
    scratch = [pltpu.VMEM((width, width), BF16), dma(1)]
    return call(kernel, "tables", outs, (core, lengths), smem=2, hbm_out=(0,), scratch=scratch)


def forward(core, x, bias, width, chips):
    rows = x.shape[0]
    pitch = -(-width // chips // 2 // 8) * 8
    part, half = (chips, pitch, width), (chips // 2, pitch, width)
    outs = [((rows, width), BF16), (part, BF16), (half, BF16), (half, BF16)]
    scratch = [pltpu.VMEM(x.shape, BF16), pltpu.VMEM((width, width), F32), pltpu.VMEM(part, BF16), dma(12)]
    args = (core, x, bias)
    return call(
        forward_kernel, "forward", outs, args, smem=1, hbm_in=1, hbm_out=(2, 3), scratch=scratch, flops=FWD_FLOPS
    )


def join(keep, first, second):
    chips, pitch, width = keep.shape
    outs = [((2, chips, 8, 2 * width + lane_half(width)), BF16)]
    return call(join_kernel, "join", outs, (keep, first, second), flops=JOIN_FLOPS)[0]


def backward(pick, x, own, other, bias, mixed):
    rows, width = mixed.shape
    flops = 8 * width * rows * width + 12 * HEADS * rows * rows * 256
    one, wide = (rows, width), (rows, 4 * width)
    shapes = ((width, width), wide, own.shape, (width - 4 * rows, width), one, one, wide)
    scratch = [pltpu.VMEM(shape, BF16) for shape in shapes] + [dma(11)]
    args = (pick, x, own, other, bias, mixed)
    return call(backward_kernel, "backward", [(wide, BF16)], args, hbm_in=3, hbm_out=(0,), scratch=scratch, flops=flops)[0]


def total_of(parts):
    scratch = [pltpu.VMEM(parts.shape, BF16), dma(4)]
    return call(total_kernel, "total", [(parts.shape[1:], BF16)], (parts,), hbm_in=1, scratch=scratch)[0]


def lane_half(width):
    return (width // LANES + 1) // 2 * LANES


def sum_over_pairs(block, place, shard, width, n_dp):
    half, quarter = n_dp // 2, n_dp // 4

    def exchange(block, source):
        return lax.ppermute(block, "dp", [(source(i) % n_dp, i) for i in range(n_dp)])

    def added(block, source):
        return (block.astype(F32) + exchange(block, source).astype(F32)).astype(BF16)

    def second(i):
        return i ^ quarter if i % 2 == 0 else i + quarter * (1 if i // quarter % 2 else -1)

    def third(i):
        return n_dp - 2 - i if i % 2 == 0 else half - i

    block = added(added(block, lambda i: i ^ 2), second)
    far, near_other = exchange(block, third), exchange(block, lambda i: i ^ 1)
    far_other = exchange(block, lambda i: third(i ^ 1))
    args = (place, block, far, near_other, far_other)
    scratch = [pltpu.VMEM((40, width), F32)]
    return call(finish_kernel, "finish", [((shard, width), F32)], args, smem=1, scratch=scratch)[0]


def on_device(n_seq, n_dp, queries, key_vectors, value_vectors, out_grad, out_weight, clip_frames):
    patches, width = queries.shape[2:]
    positions = patches // n_seq
    shard = out_weight.shape[1]
    core = jnp.bitwise_and(lax.axis_index("seq"), 1).astype(jnp.int32)

    def swap(block):
        return lax.all_to_all(block.reshape(n_seq, positions, -1), "seq", 0, 0, tiled=True)

    def partner(block):
        return lax.ppermute(block, "seq", [(i, i ^ 1) for i in range(n_seq)])

    arrays = [a.reshape(patches, width) for a in (queries, key_vectors, value_vectors, out_grad)]
    x = swap(pack(arrays)).reshape(patches, -1)
    rows, x = lax.optimization_barrier((spread(out_weight.T, patches), x))
    own = swap(rows).reshape(patches, -1)
    pick, bias = tables(core.reshape(1), clip_frames, patches, width, shard, positions)
    mixed, keep, *send = forward(core.reshape(1), x, bias, width, n_seq // 2)

    chip = join(keep, *[partner(block) for block in send])
    chip = chip.reshape(n_seq, *chip.shape[2:])
    pairs = [
        [(p + d) * n_seq + i for d in (0, 1) for i in range(c, n_seq, 2)] for p in range(0, n_dp, 2) for c in (0, 1)
    ]
    parts = lax.all_to_all(chip, ("dp", "seq"), 0, 0, tiled=True, axis_index_groups=pairs)

    y = backward(pick, x, own, partner(own), bias, mixed)
    total, y = lax.optimization_barrier((total_of(parts), y))
    back = swap(y).reshape(patches, 4 * width)
    place = jnp.stack([jnp.bitwise_and(lax.axis_index("dp"), 1).astype(jnp.int32), core])
    weight_grad = sum_over_pairs(total, place, shard, width, n_dp).T
    outs = [back[:, i * width : (i + 1) * width].reshape(queries.shape) for i in range(4)]
    return (*outs, weight_grad)


def solution(mesh):
    whole = P("dp", "seq", None, None)
    return jax.shard_map(
        functools.partial(on_device, mesh.shape["seq"], mesh.shape["dp"]),
        mesh=mesh,
        in_specs=(whole, whole, whole, whole, P(None, "seq"), P("dp", None)),
        out_specs=(whole, whole, whole, whole, P(None, "seq")),
        check_vma=False,
    )
```

```python
import functools
import math

import jax
import jax.numpy as jnp
from jax import lax
from jax.experimental import pallas as pl
from jax.experimental.pallas import tpu as pltpu
from jax.sharding import PartitionSpec as P

HEADS = 16
HEAD_DIM = 72
LANES = 128
SCALE = 1.0 / math.sqrt(HEAD_DIM)
F32 = jnp.float32
BF16 = jnp.bfloat16
VMEM_LIMIT = 28 * 1024 * 1024
NT = (((1,), (1,)), ((), ()))
TN = (((0,), (0,)), ((), ()))


def dot(a, b):
    return jnp.dot(a, b, preferred_element_type=F32)


def dot_nt(a, b):
    return lax.dot_general(a, b, NT, preferred_element_type=F32)


def dot_tn(a, b):
    return lax.dot_general(a, b, TN, preferred_element_type=F32)


def window(head):
    first = head * HEAD_DIM // LANES
    last = (head * HEAD_DIM + HEAD_DIM - 1) // LANES
    return first * LANES, (last + 1 - first) * LANES


def head_lanes(head, rows):
    start, size = window(head)
    lane = lax.broadcasted_iota(jnp.int32, (rows, size), 1) + (start - head * HEAD_DIM)
    return (lane >= 0) & (lane < HEAD_DIM)


def clip_bias(lens_ref, rows, positions):
    def ids(axis):
        index = lax.broadcasted_iota(jnp.int32, (rows, rows), axis)
        frame = lax.div(index, jnp.int32(positions))
        clip = jnp.zeros_like(frame)
        end = jnp.int32(0)
        for j in range(lens_ref.shape[1]):
            end = end + lens_ref[0, j]
            clip = clip + jnp.where(frame >= end, 1, 0)
        return clip * positions + (index - frame * positions)

    return jnp.where(ids(0) == ids(1), 0.0, -jnp.inf).astype(F32)


def softmax(query_win, key_win, bias):
    scores = dot_nt(query_win, key_win) * SCALE + bias
    raised = jnp.exp(scores - jnp.max(scores, axis=-1, keepdims=True))
    return raised, 1.0 / jnp.sum(raised, axis=-1, keepdims=True)


class Tiles:
    def __init__(self, ref, base=0):
        self.ref, self.base, self.held = ref, base, {}

    def add(self, head, value):
        start, size = window(head)
        for off in range(0, size, LANES):
            piece = value[:, off : off + LANES]
            tile = start + off
            self.held[tile] = piece if tile not in self.held else self.held[tile] + piece
        done = (head + 1) * HEAD_DIM
        for tile in [t for t in self.held if t + LANES <= done]:
            lanes = pl.ds(self.base + tile, LANES)
            self.ref[:, lanes] = self.held.pop(tile).astype(self.ref.dtype)


FWD_FLOPS = 10**11
JOIN_FLOPS = 10**9
FINISH_FLOPS = 3 * 10**9
GROUP = 8
FULL = 16
ODD = 2
CHUNK = 3
ODD_LANES = 384


def selection(rows, columns, wanted):
    row = lax.broadcasted_iota(jnp.int32, (rows, columns), 0)
    column = lax.broadcasted_iota(jnp.int32, (rows, columns), 1)
    return jnp.where(column == wanted(row), 1.0, 0.0).astype(BF16)


def chunk_tiles(ref, q):
    pieces = [ref[:, pl.ds((CHUNK * u + q) * LANES, LANES)] for u in range(CHUNK)]
    return jnp.concatenate(pieces, axis=1)


def pack_kernel(*refs):
    *parts, x_ref, staged_ref, sems = refs
    rows, width = parts[0].shape
    half = rows // 2
    fetches, copies = [], []
    for i, part in enumerate(parts):
        for j in range(2):
            at, lanes, n = pl.ds(j * half, half), pl.ds(i * width, width), 2 * i + j
            fetches.append(pltpu.make_async_copy(part.at[at], staged_ref.at[i, at], sems.at[0, n]))
            copies.append(pltpu.make_async_copy(staged_ref.at[i, at], x_ref.at[at, lanes], sems.at[1, n]))
    for fetch in fetches:
        fetch.start()
    for fetch, copy in zip(fetches, copies):
        fetch.wait()
        copy.start()
    for copy in copies:
        copy.wait()


def spread_kernel(weight_ref, out_ref, held_ref, sem):
    shard, width = weight_ref.shape
    rows = held_ref.shape[0]
    weight = weight_ref[...]

    def core(row):
        return jnp.bitwise_and(lax.div(row, jnp.int32(GROUP)), 1)

    def place(row):
        return jnp.bitwise_and(row, GROUP - 1)

    for block in range(FULL // GROUP):
        pick = selection(rows, shard, lambda row: FULL * core(row) + GROUP * block + place(row))
        held_ref[:, pl.ds(block * width, width)] = dot(pick, weight).astype(BF16)
    odd = jnp.zeros((rows, ODD_LANES), F32)
    for q in range(CHUNK):

        def wanted(row):
            k = lax.div(place(row) - q, jnp.int32(CHUNK))
            exact = (place(row) == CHUNK * k + q) & (k < ODD)
            return jnp.where(exact, 2 * FULL + ODD * core(row) + k, -1)

        odd = odd + dot(selection(rows, shard, wanted), chunk_tiles(weight_ref, q))
    held_ref[:, pl.ds(FULL // GROUP * width, ODD_LANES)] = odd.astype(BF16)
    copy = pltpu.make_async_copy(held_ref, out_ref, sem.at[0])
    copy.start()
    copy.wait()


def pick_rows(ref, place):
    padded, width = ref.shape
    block = padded // 8
    for step in range(8):
        at = lax.broadcasted_iota(jnp.int32, (block, width), 0) + step * block
        ref[pl.ds(step * block, block), :] = jnp.where(at == place, 1.0, 0.0).astype(BF16)


def tables_kernel(shard, positions, core_ref, lens_ref, pick_ref, bias_ref, held_ref, sem):
    width = pick_ref.shape[1]
    feature = lax.broadcasted_iota(jnp.int32, (1, width), 1)
    owner = lax.div(feature, jnp.int32(shard))
    rest = feature - owner * shard
    holder = jnp.where(rest < 2 * FULL, lax.div(rest, jnp.int32(FULL)), lax.div(rest - 2 * FULL, jnp.int32(ODD)))
    other = jnp.bitwise_and(holder + core_ref[0], 1)
    within = rest - FULL * holder
    block = lax.div(within, jnp.int32(GROUP))
    size = width // shard * GROUP
    full = (other * (FULL // GROUP) + block) * size + owner * GROUP + within - block * GROUP
    odd = 2 * (FULL // GROUP) * size + (other * (width // shard) + owner) * ODD + rest - 2 * FULL - ODD * holder
    pick_rows(held_ref, jnp.where(rest < 2 * FULL, full, odd))
    copy = pltpu.make_async_copy(held_ref, pick_ref, sem.at[0])
    copy.start()
    bias_ref[...] = clip_bias(lens_ref, bias_ref.shape[0], positions)
    copy.wait()


def forward_kernel(
    core_ref, x_hbm, bias_ref, mixed_ref, keep_ref, first_ref, second_ref, x_ref, part_ref, held_ref, sems
):
    rows, width = mixed_ref.shape
    middle = lane_half(width)
    pieces = [(a * width + b, c) for b, c in ((0, middle), (middle, width - middle)) for a in range(3)]
    pieces.append((3 * width, width))
    fetches = [
        pltpu.make_async_copy(x_hbm.at[:, pl.ds(at, size)], x_ref.at[:, pl.ds(at, size)], sems.at[5 + i])
        for i, (at, size) in enumerate(pieces)
    ]
    for fetch in fetches:
        fetch.start()
    bias = bias_ref[...]
    mixed_tiles = Tiles(mixed_ref)
    for head in range(HEADS):
        if head in (0, HEADS // 2):
            for fetch in fetches[3 * (head > 0) : 3 * (head > 0) + 3]:
                fetch.wait()
        start, size = window(head)
        lanes = head_lanes(head, rows)
        query_win = jnp.where(lanes, x_ref[:, pl.ds(start, size)], 0)
        key_win = x_ref[:, pl.ds(width + start, size)]
        value_win = jnp.where(lanes, x_ref[:, pl.ds(2 * width + start, size)], 0)
        raised, recip = softmax(query_win, key_win, bias)
        mixed_tiles.add(head, dot((raised * recip).astype(BF16), value_win))
    copies = []
    fetches[6].wait()
    mixed = mixed_ref[...]
    block = 3 * LANES
    for at in range(0, width, block):
        part_ref[pl.ds(at, block), :] = dot_tn(x_ref[:, pl.ds(3 * width + at, block)], mixed)
    chips, pitch, _ = held_ref.shape
    own = core_ref[0] * (width // chips - pitch)
    other = (width // chips - pitch) - own
    for step in range(4):
        some = chips // 4
        for j in range(step * some, (step + 1) * some):
            at = pl.multiple_of(j * (width // chips) + other, 8)
            held_ref[j] = part_ref[pl.ds(at, pitch), :].astype(BF16)
        source, place = pl.ds(step * some, some), pl.ds(step % 2 * some, some)
        send_ref = first_ref if step < 2 else second_ref
        copies.append(pltpu.make_async_copy(held_ref.at[source], send_ref.at[place], sems.at[step]))
        copies[-1].start()
    for j in range(chips):
        at = pl.multiple_of(j * (width // chips) + own, 8)
        keep_ref[j] = part_ref[pl.ds(at, pitch), :].astype(BF16)
    for copy in copies:
        copy.wait()


def join_kernel(keep_ref, first_ref, second_ref, out_ref):
    width = keep_ref.shape[2]
    size = lane_half(width)
    half = first_ref.shape[0]
    for at, ref in ((0, first_ref), (half, second_ref)):
        ids = pl.ds(at, half)
        total = keep_ref[ids].astype(F32) + ref[...].astype(F32)
        groups = [total[:, i * 8 : i * 8 + 8, :].astype(BF16) for i in range(5)]
        for d, whole, rest in ((0, (0, 1), groups[2][:, :, :size]), (1, (3, 4), groups[2][:, :, width - size :])):
            for i, group in enumerate(whole):
                out_ref[d, ids, :, pl.ds(i * width, width)] = groups[group]
            out_ref[d, ids, :, pl.ds(2 * width, size)] = rest


def finish_kernel(place_ref, mine_ref, other_ref, out_ref, held_ref):
    shard, width = out_ref.shape
    size = lane_half(width)
    mine, other = mine_ref[...].astype(F32), other_ref[...].astype(F32)
    low = place_ref[0] == 0
    lower, upper = jnp.where(low, mine, other), jnp.where(low, other, mine)
    for half, groups in ((lower, (0, 1)), (upper, (3, 4))):
        for i, group in enumerate(groups):
            held_ref[pl.ds(group * 8, 8), :] = half[:, i * width : (i + 1) * width]
    held_ref[pl.ds(16, 8), pl.ds(0, size)] = lower[:, 2 * width :]
    held_ref[pl.ds(16, 8), pl.ds(size, width - size)] = upper[:, 2 * width + 2 * size - width :]
    rows = held_ref.shape[0]
    out_ref[...] = jnp.where(place_ref[1] == 0, held_ref[pl.ds(0, shard), :], held_ref[pl.ds(rows - shard, shard), :])


def backward_kernel(
    pick_hbm, x_hbm, own_hbm, other_ref, bias_ref, mixed_ref, y_ref,
    pick_ref, x_ref, own_ref, odd_ref, back_ref, out_ref, held_ref, sems
):
    rows, width = mixed_ref.shape
    three, fourth = pl.ds(0, 3 * width), pl.ds(3 * width, width)
    fetches = [
        pltpu.make_async_copy(own_hbm, own_ref, sems.at[7]),
        pltpu.make_async_copy(pick_hbm, pick_ref, sems.at[8]),
        pltpu.make_async_copy(x_hbm.at[:, fourth], x_ref.at[:, fourth], sems.at[9]),
        pltpu.make_async_copy(x_hbm.at[:, three], x_ref.at[:, three], sems.at[10]),
    ]
    for fetch in fetches:
        fetch.start()
    copies = []

    def send(start, size):
        lanes = pl.ds(start, size)
        copies.append(pltpu.make_async_copy(held_ref.at[:, lanes], y_ref.at[:, lanes], sems.at[len(copies)]))
        copies[-1].start()

    blocks = FULL // GROUP
    fetches[0].wait()
    weight = []
    for ref in (own_ref, other_ref):
        weight += [ref[:, pl.ds(b * width, width)] for b in range(blocks)]
    odd_rows = odd_ref.shape[0] // 2
    for i, ref in enumerate((own_ref, other_ref)):
        left = ref[:, pl.ds(blocks * width, ODD_LANES)]
        for q in range(CHUNK):

            def wanted(row):
                source = lax.div(row, jnp.int32(ODD))
                return source * GROUP + CHUNK * (row - ODD * source) + q

            got = dot(selection(odd_rows, rows, wanted), left).astype(BF16)
            for u in range(CHUNK):
                lanes = pl.ds((CHUNK * u + q) * LANES, LANES)
                odd_ref[pl.ds(i * odd_rows, odd_rows), lanes] = got[:, u * LANES : (u + 1) * LANES]
    weight.append(odd_ref[...])
    fetches[1].wait()
    fetches[2].wait()
    grad = dot_nt(x_ref[:, fourth], pick_ref[...]).astype(BF16)
    mixed = mixed_ref[...]
    back = jnp.zeros((rows, width), F32)
    at = 0
    for block in weight:
        size = block.shape[0]
        back = back + dot(grad[:, at : at + size], block)
        out_ref[:, pl.ds(at, size)] = dot_nt(mixed, block).astype(BF16)
        at += size
    back_ref[...] = back.astype(BF16)
    held_ref[:, pl.ds(0, width)] = dot(out_ref[...], pick_ref[...]).astype(BF16)
    send(0, width)
    query_tiles, key_tiles, value_tiles = [Tiles(held_ref, i * width) for i in (1, 2, 3)]
    bias = bias_ref[...]
    fetches[3].wait()
    sent = 0
    for head in range(HEADS):
        start, size = window(head)
        lanes = head_lanes(head, rows)
        query_win = jnp.where(lanes, x_ref[:, pl.ds(start, size)], 0)
        key_win = jnp.where(lanes, x_ref[:, pl.ds(width + start, size)], 0)
        value_win = x_ref[:, pl.ds(2 * width + start, size)]
        back_win = jnp.where(lanes, back_ref[:, pl.ds(start, size)], 0)
        scores = dot_nt(key_win, query_win) * SCALE + bias
        raised = jnp.exp(scores - jnp.max(scores, axis=0, keepdims=True))
        attention = raised * (1.0 / jnp.sum(raised, axis=0, keepdims=True))
        value_tiles.add(head, dot(attention.astype(BF16), back_win))
        drawn = attention * dot_nt(value_win, back_win)
        inner = jnp.sum(drawn, axis=0, keepdims=True)
        score_grad = ((drawn - attention * inner) * SCALE).astype(BF16)
        key_tiles.add(head, dot(score_grad, query_win))
        query_tiles.add(head, dot_tn(score_grad, key_win))
        if head in (HEADS // 2 - 1, HEADS - 1):
            done = (head + 1) * HEAD_DIM // LANES * LANES
            for i in (1, 2, 3):
                send(i * width + sent, done - sent)
            sent = done
    for copy in copies:
        copy.wait()


def total_kernel(parts_ref, out_ref):
    total = parts_ref[0].astype(F32)
    for j in range(1, parts_ref.shape[0]):
        total = total + parts_ref[j].astype(F32)
    out_ref[...] = total.astype(BF16)


def call(kernel, name, outs, args, smem=0, hbm_in=0, hbm_out=(), scratch=(), flops=0):
    space = [pltpu.SMEM] * smem + [pltpu.HBM] * hbm_in + [pltpu.VMEM] * (len(args) - smem - hbm_in)
    args = [pltpu.with_memory_space_constraint(a, s) if s == pltpu.HBM else a for a, s in zip(args, space)]
    shapes = [jax.ShapeDtypeStruct(shape, dtype) for shape, dtype in outs]
    moved = sum(a.size * a.dtype.itemsize for a in args) + sum(math.prod(s.shape) * s.dtype.itemsize for s in shapes)
    return pl.pallas_call(
        kernel,
        out_shape=[pltpu.HBM(s.shape, s.dtype) if i in hbm_out else s for i, s in enumerate(shapes)],
        in_specs=[pl.BlockSpec(memory_space=s) for s in space],
        out_specs=[pl.BlockSpec(memory_space=pltpu.HBM if i in hbm_out else pltpu.VMEM) for i in range(len(outs))],
        scratch_shapes=scratch,
        compiler_params=pltpu.CompilerParams(vmem_limit_bytes=VMEM_LIMIT),
        cost_estimate=pl.CostEstimate(flops=flops, bytes_accessed=0 if flops else moved, transcendentals=0),
        name=name,
    )(*args)


def dma(count):
    return pltpu.SemaphoreType.DMA((count,))


def pack(arrays):
    rows, width = arrays[0].shape
    count = len(arrays)
    outs = [((rows, count * width), BF16)]
    scratch = [pltpu.VMEM((count, rows, width), BF16), pltpu.SemaphoreType.DMA((2, 2 * count))]
    return call(pack_kernel, "pack", outs, arrays, hbm_in=count, hbm_out=(0,), scratch=scratch)[0]


def spread(weight_t, rows):
    shape = (rows, FULL // GROUP * weight_t.shape[1] + ODD_LANES)
    scratch = [pltpu.VMEM(shape, BF16), dma(1)]
    return call(spread_kernel, "spread", [(shape, BF16)], (weight_t,), hbm_out=(0,), scratch=scratch)[0]


def tables(core, lengths, rows, width, shard, positions):
    kernel = functools.partial(tables_kernel, shard, positions)
    outs = [((width, width), BF16), ((rows, rows), F32)]
    scratch = [pltpu.VMEM((width, width), BF16), dma(1)]
    return call(kernel, "tables", outs, (core, lengths), smem=2, hbm_out=(0,), scratch=scratch)


def forward(core, x, bias, width, chips):
    rows = x.shape[0]
    pitch = -(-width // chips // 2 // 8) * 8
    part, half = (chips, pitch, width), (chips // 2, pitch, width)
    outs = [((rows, width), BF16), (part, BF16), (half, BF16), (half, BF16)]
    scratch = [pltpu.VMEM(x.shape, BF16), pltpu.VMEM((width, width), F32), pltpu.VMEM(part, BF16), dma(12)]
    args = (core, x, bias)
    return call(
        forward_kernel, "forward", outs, args, smem=1, hbm_in=1, hbm_out=(2, 3), scratch=scratch, flops=FWD_FLOPS
    )


def join(keep, first, second):
    chips, pitch, width = keep.shape
    outs = [((2, chips, 8, 2 * width + lane_half(width)), BF16)]
    return call(join_kernel, "join", outs, (keep, first, second), flops=JOIN_FLOPS)[0]


def backward(pick, x, own, other, bias, mixed):
    rows, width = mixed.shape
    flops = 8 * width * rows * width + 12 * HEADS * rows * rows * 256
    one, wide = (rows, width), (rows, 4 * width)
    shapes = ((width, width), wide, own.shape, (width - 4 * rows, width), one, one, wide)
    scratch = [pltpu.VMEM(shape, BF16) for shape in shapes] + [dma(11)]
    args = (pick, x, own, other, bias, mixed)
    return call(backward_kernel, "backward", [(wide, BF16)], args, hbm_in=3, hbm_out=(0,), scratch=scratch, flops=flops)[0]


def total_of(parts):
    return call(total_kernel, "total", [(parts.shape[1:], BF16)], (parts,))[0]


def lane_half(width):
    return (width // LANES + 1) // 2 * LANES


def sum_over_pairs(block, place, shard, width, n_dp):
    half, quarter = n_dp // 2, n_dp // 4

    def exchange(block, source):
        return lax.ppermute(block, "dp", [(source(i) % n_dp, i) for i in range(n_dp)])

    def added(block, source):
        return (block.astype(F32) + exchange(block, source).astype(F32)).astype(BF16)

    def second(i):
        return i ^ quarter if i % 2 == 0 else i + quarter * (1 if i // quarter % 2 else -1)

    def third(i):
        return n_dp - 2 - i if i % 2 == 0 else half - i

    block = added(added(added(block, lambda i: i ^ 2), second), third)
    args = (place, block, exchange(block, lambda i: i ^ 1))
    scratch = [pltpu.VMEM((40, width), F32)]
    return call(finish_kernel, "finish", [((shard, width), F32)], args, smem=1, scratch=scratch, flops=FINISH_FLOPS)[0]


def on_device(n_seq, n_dp, queries, key_vectors, value_vectors, out_grad, out_weight, clip_frames):
    patches, width = queries.shape[2:]
    positions = patches // n_seq
    shard = out_weight.shape[1]
    core = jnp.bitwise_and(lax.axis_index("seq"), 1).astype(jnp.int32)

    def swap(block):
        return lax.all_to_all(block.reshape(n_seq, positions, -1), "seq", 0, 0, tiled=True)

    def partner(block):
        return lax.ppermute(block, "seq", [(i, i ^ 1) for i in range(n_seq)])

    arrays = [a.reshape(patches, width) for a in (queries, key_vectors, value_vectors, out_grad)]
    x = swap(pack(arrays)).reshape(patches, -1)
    rows, x = lax.optimization_barrier((spread(out_weight.T, patches), x))
    own = swap(rows).reshape(patches, -1)
    pick, bias = tables(core.reshape(1), clip_frames, patches, width, shard, positions)
    mixed, keep, *send = forward(core.reshape(1), x, bias, width, n_seq // 2)

    chip = join(keep, *[partner(block) for block in send])
    chip = chip.reshape(n_seq, *chip.shape[2:])
    pairs = [
        [(p + d) * n_seq + i for d in (0, 1) for i in range(c, n_seq, 2)] for p in range(0, n_dp, 2) for c in (0, 1)
    ]
    parts = lax.all_to_all(chip, ("dp", "seq"), 0, 0, tiled=True, axis_index_groups=pairs)

    y = backward(pick, x, own, partner(own), bias, mixed)
    total, y = lax.optimization_barrier((total_of(parts), y))
    back = swap(y).reshape(patches, 4 * width)
    place = jnp.stack([jnp.bitwise_and(lax.axis_index("dp"), 1).astype(jnp.int32), core])
    weight_grad = sum_over_pairs(total, place, shard, width, n_dp).T
    outs = [back[:, i * width : (i + 1) * width].reshape(queries.shape) for i in range(4)]
    return (*outs, weight_grad)


def solution(mesh):
    whole = P("dp", "seq", None, None)
    return jax.shard_map(
        functools.partial(on_device, mesh.shape["seq"], mesh.shape["dp"]),
        mesh=mesh,
        in_specs=(whole, whole, whole, whole, P(None, "seq"), P("dp", None)),
        out_specs=(whole, whole, whole, whole, P(None, "seq")),
        check_vma=False,
    )
```

```python
import functools
import math

import jax
import jax.numpy as jnp
from jax import lax
from jax.experimental import pallas as pl
from jax.experimental.pallas import tpu as pltpu
from jax.sharding import PartitionSpec as P

HEADS = 16
HEAD_DIM = 72
LANES = 128
SCALE = 1.0 / math.sqrt(HEAD_DIM)
F32 = jnp.float32
BF16 = jnp.bfloat16
VMEM_LIMIT = 28 * 1024 * 1024
NT = (((1,), (1,)), ((), ()))
TN = (((0,), (0,)), ((), ()))


def dot(a, b):
    return jnp.dot(a, b, preferred_element_type=F32)


def dot_nt(a, b):
    return lax.dot_general(a, b, NT, preferred_element_type=F32)


def dot_tn(a, b):
    return lax.dot_general(a, b, TN, preferred_element_type=F32)


def window(head):
    first = head * HEAD_DIM // LANES
    last = (head * HEAD_DIM + HEAD_DIM - 1) // LANES
    return first * LANES, (last + 1 - first) * LANES


def head_lanes(head, rows):
    start, size = window(head)
    lane = lax.broadcasted_iota(jnp.int32, (rows, size), 1) + (start - head * HEAD_DIM)
    return (lane >= 0) & (lane < HEAD_DIM)


def clip_bias(lens_ref, rows, positions):
    def ids(axis):
        index = lax.broadcasted_iota(jnp.int32, (rows, rows), axis)
        frame = lax.div(index, jnp.int32(positions))
        clip = jnp.zeros_like(frame)
        end = jnp.int32(0)
        for j in range(lens_ref.shape[1]):
            end = end + lens_ref[0, j]
            clip = clip + jnp.where(frame >= end, 1, 0)
        return clip * positions + (index - frame * positions)

    return jnp.where(ids(0) == ids(1), 0.0, -jnp.inf).astype(F32)


def softmax(query_win, key_win, bias):
    scores = dot_nt(query_win, key_win) * SCALE + bias
    raised = jnp.exp(scores - jnp.max(scores, axis=-1, keepdims=True))
    return raised, 1.0 / jnp.sum(raised, axis=-1, keepdims=True)


class Tiles:
    def __init__(self, ref, base=0):
        self.ref, self.base, self.held = ref, base, {}

    def add(self, head, value):
        start, size = window(head)
        for off in range(0, size, LANES):
            piece = value[:, off : off + LANES]
            tile = start + off
            self.held[tile] = piece if tile not in self.held else self.held[tile] + piece
        done = (head + 1) * HEAD_DIM
        for tile in [t for t in self.held if t + LANES <= done]:
            lanes = pl.ds(self.base + tile, LANES)
            self.ref[:, lanes] = self.held.pop(tile).astype(self.ref.dtype)


FWD_FLOPS = 10**11
JOIN_FLOPS = 10**9
FINISH_FLOPS = 3 * 10**9
GROUP = 8
FULL = 16
ODD = 2
CHUNK = 3
ODD_LANES = 384


def selection(rows, columns, wanted):
    row = lax.broadcasted_iota(jnp.int32, (rows, columns), 0)
    column = lax.broadcasted_iota(jnp.int32, (rows, columns), 1)
    return jnp.where(column == wanted(row), 1.0, 0.0).astype(BF16)


def chunk_tiles(ref, q):
    pieces = [ref[:, pl.ds((CHUNK * u + q) * LANES, LANES)] for u in range(CHUNK)]
    return jnp.concatenate(pieces, axis=1)


def pack_kernel(*refs):
    *parts, x_ref, staged_ref, sems = refs
    rows, width = parts[0].shape
    half = rows // 2
    fetches, copies = [], []
    for i, part in enumerate(parts):
        for j in range(2):
            at, lanes, n = pl.ds(j * half, half), pl.ds(i * width, width), 2 * i + j
            fetches.append(pltpu.make_async_copy(part.at[at], staged_ref.at[i, at], sems.at[0, n]))
            copies.append(pltpu.make_async_copy(staged_ref.at[i, at], x_ref.at[at, lanes], sems.at[1, n]))
    for fetch in fetches:
        fetch.start()
    for fetch, copy in zip(fetches, copies):
        fetch.wait()
        copy.start()
    for copy in copies:
        copy.wait()


def unpack_kernel(x_ref, *refs):
    *outs, sems = refs
    width = outs[0].shape[1]
    copies = [
        pltpu.make_async_copy(x_ref.at[:, pl.ds(i * width, width)], out, sems.at[i]) for i, out in enumerate(outs)
    ]
    for copy in copies:
        copy.start()
    for copy in copies:
        copy.wait()


def spread_kernel(weight_ref, out_ref, held_ref, sem):
    shard, width = weight_ref.shape
    rows = held_ref.shape[0]
    weight = weight_ref[...]

    def core(row):
        return jnp.bitwise_and(lax.div(row, jnp.int32(GROUP)), 1)

    def place(row):
        return jnp.bitwise_and(row, GROUP - 1)

    for block in range(FULL // GROUP):
        pick = selection(rows, shard, lambda row: FULL * core(row) + GROUP * block + place(row))
        held_ref[:, pl.ds(block * width, width)] = dot(pick, weight).astype(BF16)
    odd = jnp.zeros((rows, ODD_LANES), F32)
    for q in range(CHUNK):

        def wanted(row):
            k = lax.div(place(row) - q, jnp.int32(CHUNK))
            exact = (place(row) == CHUNK * k + q) & (k < ODD)
            return jnp.where(exact, 2 * FULL + ODD * core(row) + k, -1)

        odd = odd + dot(selection(rows, shard, wanted), chunk_tiles(weight_ref, q))
    held_ref[:, pl.ds(FULL // GROUP * width, ODD_LANES)] = odd.astype(BF16)
    copy = pltpu.make_async_copy(held_ref, out_ref, sem.at[0])
    copy.start()
    copy.wait()


def pick_rows(ref, place):
    padded, width = ref.shape
    block = padded // 8
    for step in range(8):
        at = lax.broadcasted_iota(jnp.int32, (block, width), 0) + step * block
        ref[pl.ds(step * block, block), :] = jnp.where(at == place, 1.0, 0.0).astype(BF16)


def tables_kernel(shard, positions, core_ref, lens_ref, pick_ref, bias_ref, held_ref, sem):
    width = pick_ref.shape[1]
    feature = lax.broadcasted_iota(jnp.int32, (1, width), 1)
    owner = lax.div(feature, jnp.int32(shard))
    rest = feature - owner * shard
    holder = jnp.where(rest < 2 * FULL, lax.div(rest, jnp.int32(FULL)), lax.div(rest - 2 * FULL, jnp.int32(ODD)))
    other = jnp.bitwise_and(holder + core_ref[0], 1)
    within = rest - FULL * holder
    block = lax.div(within, jnp.int32(GROUP))
    size = width // shard * GROUP
    full = (other * (FULL // GROUP) + block) * size + owner * GROUP + within - block * GROUP
    odd = 2 * (FULL // GROUP) * size + (other * (width // shard) + owner) * ODD + rest - 2 * FULL - ODD * holder
    pick_rows(held_ref, jnp.where(rest < 2 * FULL, full, odd))
    copy = pltpu.make_async_copy(held_ref, pick_ref, sem.at[0])
    copy.start()
    bias_ref[...] = clip_bias(lens_ref, bias_ref.shape[0], positions)
    copy.wait()


def forward_kernel(
    core_ref, x_hbm, bias_ref, mixed_ref, keep_ref, first_ref, second_ref, x_ref, part_ref, held_ref, sems
):
    rows, width = mixed_ref.shape
    middle = lane_half(width)
    pieces = [(a * width + b, c) for b, c in ((0, middle), (middle, width - middle)) for a in range(3)]
    pieces.append((3 * width, width))
    fetches = [
        pltpu.make_async_copy(x_hbm.at[:, pl.ds(at, size)], x_ref.at[:, pl.ds(at, size)], sems.at[5 + i])
        for i, (at, size) in enumerate(pieces)
    ]
    for fetch in fetches:
        fetch.start()
    bias = bias_ref[...]
    mixed_tiles = Tiles(mixed_ref)
    for head in range(HEADS):
        if head in (0, HEADS // 2):
            for fetch in fetches[3 * (head > 0) : 3 * (head > 0) + 3]:
                fetch.wait()
        start, size = window(head)
        lanes = head_lanes(head, rows)
        query_win = jnp.where(lanes, x_ref[:, pl.ds(start, size)], 0)
        key_win = x_ref[:, pl.ds(width + start, size)]
        value_win = jnp.where(lanes, x_ref[:, pl.ds(2 * width + start, size)], 0)
        raised, recip = softmax(query_win, key_win, bias)
        mixed_tiles.add(head, dot((raised * recip).astype(BF16), value_win))
    copies = []
    fetches[6].wait()
    mixed = mixed_ref[...]
    block = 3 * LANES
    for at in range(0, width, block):
        part_ref[pl.ds(at, block), :] = dot_tn(x_ref[:, pl.ds(3 * width + at, block)], mixed)
    chips, pitch, _ = held_ref.shape
    own = core_ref[0] * (width // chips - pitch)
    other = (width // chips - pitch) - own
    for step in range(4):
        some = chips // 4
        for j in range(step * some, (step + 1) * some):
            at = pl.multiple_of(j * (width // chips) + other, 8)
            held_ref[j] = part_ref[pl.ds(at, pitch), :].astype(BF16)
        source, place = pl.ds(step * some, some), pl.ds(step % 2 * some, some)
        send_ref = first_ref if step < 2 else second_ref
        copies.append(pltpu.make_async_copy(held_ref.at[source], send_ref.at[place], sems.at[step]))
        copies[-1].start()
    for j in range(chips):
        at = pl.multiple_of(j * (width // chips) + own, 8)
        keep_ref[j] = part_ref[pl.ds(at, pitch), :].astype(BF16)
    for copy in copies:
        copy.wait()


def join_kernel(keep_ref, first_ref, second_ref, out_ref):
    width = keep_ref.shape[2]
    size = lane_half(width)
    half = first_ref.shape[0]
    for at, ref in ((0, first_ref), (half, second_ref)):
        ids = pl.ds(at, half)
        total = keep_ref[ids].astype(F32) + ref[...].astype(F32)
        groups = [total[:, i * 8 : i * 8 + 8, :].astype(BF16) for i in range(5)]
        for d, whole, rest in ((0, (0, 1), groups[2][:, :, :size]), (1, (3, 4), groups[2][:, :, width - size :])):
            for i, group in enumerate(whole):
                out_ref[d, ids, :, pl.ds(i * width, width)] = groups[group]
            out_ref[d, ids, :, pl.ds(2 * width, size)] = rest


def finish_kernel(place_ref, mine_ref, other_ref, out_ref, held_ref):
    shard, width = out_ref.shape
    size = lane_half(width)
    mine, other = mine_ref[...].astype(F32), other_ref[...].astype(F32)
    low = place_ref[0] == 0
    lower, upper = jnp.where(low, mine, other), jnp.where(low, other, mine)
    for half, groups in ((lower, (0, 1)), (upper, (3, 4))):
        for i, group in enumerate(groups):
            held_ref[pl.ds(group * 8, 8), :] = half[:, i * width : (i + 1) * width]
    held_ref[pl.ds(16, 8), pl.ds(0, size)] = lower[:, 2 * width :]
    held_ref[pl.ds(16, 8), pl.ds(size, width - size)] = upper[:, 2 * width + 2 * size - width :]
    rows = held_ref.shape[0]
    out_ref[...] = jnp.where(place_ref[1] == 0, held_ref[pl.ds(0, shard), :], held_ref[pl.ds(rows - shard, shard), :])


def backward_kernel(
    pick_hbm, x_hbm, own_hbm, other_ref, bias_ref, mixed_ref, y_ref,
    pick_ref, x_ref, own_ref, odd_ref, back_ref, out_ref, held_ref, attention_ref, sems
):
    rows, width = mixed_ref.shape
    pairs, third, fourth = pl.ds(0, 2 * width), pl.ds(2 * width, width), pl.ds(3 * width, width)
    fetches = [
        pltpu.make_async_copy(x_hbm.at[:, pairs], x_ref.at[:, pairs], sems.at[7]),
        pltpu.make_async_copy(own_hbm, own_ref, sems.at[8]),
        pltpu.make_async_copy(x_hbm.at[:, fourth], x_ref.at[:, fourth], sems.at[9]),
        pltpu.make_async_copy(pick_hbm, pick_ref, sems.at[10]),
        pltpu.make_async_copy(x_hbm.at[:, third], x_ref.at[:, third], sems.at[11]),
    ]
    for fetch in fetches:
        fetch.start()
    copies = []

    def send(start, size):
        lanes = pl.ds(start, size)
        copies.append(pltpu.make_async_copy(held_ref.at[:, lanes], y_ref.at[:, lanes], sems.at[len(copies)]))
        copies[-1].start()

    fetches[0].wait()
    bias = bias_ref[...]
    for head in range(HEADS):
        start, size = window(head)
        query_win = jnp.where(head_lanes(head, rows), x_ref[:, pl.ds(start, size)], 0)
        scores = dot_nt(x_ref[:, pl.ds(width + start, size)], query_win) * SCALE + bias
        raised = jnp.exp(scores - jnp.max(scores, axis=0, keepdims=True))
        attention_ref[head] = raised * (1.0 / jnp.sum(raised, axis=0, keepdims=True))
    blocks = FULL // GROUP
    fetches[1].wait()
    weight = []
    for ref in (own_ref, other_ref):
        weight += [ref[:, pl.ds(b * width, width)] for b in range(blocks)]
    odd_rows = odd_ref.shape[0] // 2
    for i, ref in enumerate((own_ref, other_ref)):
        left = ref[:, pl.ds(blocks * width, ODD_LANES)]
        for q in range(CHUNK):

            def wanted(row):
                source = lax.div(row, jnp.int32(ODD))
                return source * GROUP + CHUNK * (row - ODD * source) + q

            got = dot(selection(odd_rows, rows, wanted), left).astype(BF16)
            for u in range(CHUNK):
                lanes = pl.ds((CHUNK * u + q) * LANES, LANES)
                odd_ref[pl.ds(i * odd_rows, odd_rows), lanes] = got[:, u * LANES : (u + 1) * LANES]
    weight.append(odd_ref[...])
    fetches[2].wait()
    fetches[3].wait()
    grad = dot_nt(x_ref[:, fourth], pick_ref[...]).astype(BF16)
    mixed = mixed_ref[...]
    back = jnp.zeros((rows, width), F32)
    at = 0
    for block in weight:
        size = block.shape[0]
        back = back + dot(grad[:, at : at + size], block)
        out_ref[:, pl.ds(at, size)] = dot_nt(mixed, block).astype(BF16)
        at += size
    back_ref[...] = back.astype(BF16)
    held_ref[:, pl.ds(0, width)] = dot(out_ref[...], pick_ref[...]).astype(BF16)
    send(0, width)
    query_tiles, key_tiles, value_tiles = [Tiles(held_ref, i * width) for i in (1, 2, 3)]
    fetches[4].wait()
    sent = 0
    for head in range(HEADS):
        start, size = window(head)
        lanes = head_lanes(head, rows)
        query_win = jnp.where(lanes, x_ref[:, pl.ds(start, size)], 0)
        key_win = jnp.where(lanes, x_ref[:, pl.ds(width + start, size)], 0)
        value_win = x_ref[:, pl.ds(2 * width + start, size)]
        back_win = jnp.where(lanes, back_ref[:, pl.ds(start, size)], 0)
        attention = attention_ref[head]
        value_tiles.add(head, dot(attention.astype(BF16), back_win))
        drawn = attention * dot_nt(value_win, back_win)
        inner = jnp.sum(drawn, axis=0, keepdims=True)
        score_grad = ((drawn - attention * inner) * SCALE).astype(BF16)
        key_tiles.add(head, dot(score_grad, query_win))
        query_tiles.add(head, dot_tn(score_grad, key_win))
        if head in (HEADS // 2 - 1, HEADS - 1):
            done = (head + 1) * HEAD_DIM // LANES * LANES
            for i in (1, 2, 3):
                send(i * width + sent, done - sent)
            sent = done
    for copy in copies:
        copy.wait()


def total_kernel(parts_ref, out_ref):
    total = parts_ref[0].astype(F32)
    for j in range(1, parts_ref.shape[0]):
        total = total + parts_ref[j].astype(F32)
    out_ref[...] = total.astype(BF16)


def call(kernel, name, outs, args, smem=0, hbm_in=0, hbm_out=(), scratch=(), flops=0):
    space = [pltpu.SMEM] * smem + [pltpu.HBM] * hbm_in + [pltpu.VMEM] * (len(args) - smem - hbm_in)
    args = [pltpu.with_memory_space_constraint(a, s) if s == pltpu.HBM else a for a, s in zip(args, space)]
    shapes = [jax.ShapeDtypeStruct(shape, dtype) for shape, dtype in outs]
    moved = sum(a.size * a.dtype.itemsize for a in args) + sum(math.prod(s.shape) * s.dtype.itemsize for s in shapes)
    return pl.pallas_call(
        kernel,
        out_shape=[pltpu.HBM(s.shape, s.dtype) if i in hbm_out else s for i, s in enumerate(shapes)],
        in_specs=[pl.BlockSpec(memory_space=s) for s in space],
        out_specs=[pl.BlockSpec(memory_space=pltpu.HBM if i in hbm_out else pltpu.VMEM) for i in range(len(outs))],
        scratch_shapes=scratch,
        compiler_params=pltpu.CompilerParams(vmem_limit_bytes=VMEM_LIMIT),
        cost_estimate=pl.CostEstimate(flops=flops, bytes_accessed=0 if flops else moved, transcendentals=0),
        name=name,
    )(*args)


def dma(count):
    return pltpu.SemaphoreType.DMA((count,))


def pack(arrays):
    rows, width = arrays[0].shape
    count = len(arrays)
    outs = [((rows, count * width), BF16)]
    scratch = [pltpu.VMEM((count, rows, width), BF16), pltpu.SemaphoreType.DMA((2, 2 * count))]
    return call(pack_kernel, "pack", outs, arrays, hbm_in=count, hbm_out=(0,), scratch=scratch)[0]


def unpack(x, count):
    rows, wide = x.shape
    width = wide // count
    outs = [((rows, width), BF16)] * count
    return call(unpack_kernel, "unpack", outs, (x,), hbm_out=range(count), scratch=[dma(count)])


def spread(weight_t, rows):
    shape = (rows, FULL // GROUP * weight_t.shape[1] + ODD_LANES)
    scratch = [pltpu.VMEM(shape, BF16), dma(1)]
    return call(spread_kernel, "spread", [(shape, BF16)], (weight_t,), hbm_out=(0,), scratch=scratch)[0]


def tables(core, lengths, rows, width, shard, positions):
    kernel = functools.partial(tables_kernel, shard, positions)
    outs = [((width, width), BF16), ((rows, rows), F32)]
    scratch = [pltpu.VMEM((width, width), BF16), dma(1)]
    return call(kernel, "tables", outs, (core, lengths), smem=2, hbm_out=(0,), scratch=scratch)


def forward(core, x, bias, width, chips):
    rows = x.shape[0]
    pitch = -(-width // chips // 2 // 8) * 8
    part, half = (chips, pitch, width), (chips // 2, pitch, width)
    outs = [((rows, width), BF16), (part, BF16), (half, BF16), (half, BF16)]
    scratch = [pltpu.VMEM(x.shape, BF16), pltpu.VMEM((width, width), F32), pltpu.VMEM(part, BF16), dma(12)]
    args = (core, x, bias)
    return call(
        forward_kernel, "forward", outs, args, smem=1, hbm_in=1, hbm_out=(2, 3), scratch=scratch, flops=FWD_FLOPS
    )


def join(keep, first, second):
    chips, pitch, width = keep.shape
    outs = [((2, chips, 8, 2 * width + lane_half(width)), BF16)]
    return call(join_kernel, "join", outs, (keep, first, second), flops=JOIN_FLOPS)[0]


def backward(pick, x, own, other, bias, mixed):
    rows, width = mixed.shape
    flops = 8 * width * rows * width + 12 * HEADS * rows * rows * 256
    one, wide = (rows, width), (rows, 4 * width)
    shapes = ((width, width), wide, own.shape, (width - 4 * rows, width), one, one, wide)
    scratch = [pltpu.VMEM(shape, BF16) for shape in shapes]
    scratch += [pltpu.VMEM((HEADS, rows, rows), F32), dma(12)]
    args = (pick, x, own, other, bias, mixed)
    return call(backward_kernel, "backward", [(wide, BF16)], args, hbm_in=3, hbm_out=(0,), scratch=scratch, flops=flops)[0]


def total_of(parts):
    return call(total_kernel, "total", [(parts.shape[1:], BF16)], (parts,))[0]


def lane_half(width):
    return (width // LANES + 1) // 2 * LANES


def sum_over_pairs(block, place, shard, width, n_dp):
    half, quarter = n_dp // 2, n_dp // 4

    def exchange(block, source):
        return lax.ppermute(block, "dp", [(source(i) % n_dp, i) for i in range(n_dp)])

    def added(block, source):
        return (block.astype(F32) + exchange(block, source).astype(F32)).astype(BF16)

    def second(i):
        return i ^ quarter if i % 2 == 0 else i + quarter * (1 if i // quarter % 2 else -1)

    def third(i):
        return n_dp - 2 - i if i % 2 == 0 else half - i

    block = added(added(added(block, lambda i: i ^ 2), second), third)
    args = (place, block, exchange(block, lambda i: i ^ 1))
    scratch = [pltpu.VMEM((40, width), F32)]
    return call(finish_kernel, "finish", [((shard, width), F32)], args, smem=1, scratch=scratch, flops=FINISH_FLOPS)[0]


def on_device(n_seq, n_dp, queries, key_vectors, value_vectors, out_grad, out_weight, clip_frames):
    patches, width = queries.shape[2:]
    positions = patches // n_seq
    shard = out_weight.shape[1]
    core = jnp.bitwise_and(lax.axis_index("seq"), 1).astype(jnp.int32)

    def swap(block):
        return lax.all_to_all(block.reshape(n_seq, positions, -1), "seq", 0, 0, tiled=True)

    def partner(block):
        return lax.ppermute(block, "seq", [(i, i ^ 1) for i in range(n_seq)])

    arrays = [a.reshape(patches, width) for a in (queries, key_vectors, value_vectors, out_grad)]
    x = swap(pack(arrays)).reshape(patches, -1)
    rows, x = lax.optimization_barrier((spread(out_weight.T, patches), x))
    own = swap(rows).reshape(patches, -1)
    pick, bias = tables(core.reshape(1), clip_frames, patches, width, shard, positions)
    mixed, keep, *send = forward(core.reshape(1), x, bias, width, n_seq // 2)

    chip = join(keep, *[partner(block) for block in send])
    chip = chip.reshape(n_seq, *chip.shape[2:])
    pairs = [
        [(p + d) * n_seq + i for d in (0, 1) for i in range(c, n_seq, 2)] for p in range(0, n_dp, 2) for c in (0, 1)
    ]
    parts = lax.all_to_all(chip, ("dp", "seq"), 0, 0, tiled=True, axis_index_groups=pairs)

    y = backward(pick, x, own, partner(own), bias, mixed)
    total, y = lax.optimization_barrier((total_of(parts), y))
    back = swap(y).reshape(patches, 4 * width)
    place = jnp.stack([jnp.bitwise_and(lax.axis_index("dp"), 1).astype(jnp.int32), core])
    weight_grad = sum_over_pairs(total, place, shard, width, n_dp).T
    outs = [out.reshape(queries.shape) for out in unpack(back, 4)]
    return (*outs, weight_grad)


def solution(mesh):
    whole = P("dp", "seq", None, None)
    return jax.shard_map(
        functools.partial(on_device, mesh.shape["seq"], mesh.shape["dp"]),
        mesh=mesh,
        in_specs=(whole, whole, whole, whole, P(None, "seq"), P("dp", None)),
        out_specs=(whole, whole, whole, whole, P(None, "seq")),
        check_vma=False,
    )
```

```python
import functools
import math

import jax
import jax.numpy as jnp
from jax import lax
from jax.experimental import pallas as pl
from jax.experimental.pallas import tpu as pltpu
from jax.sharding import PartitionSpec as P

HEADS = 16
HEAD_DIM = 72
LANES = 128
SCALE = 1.0 / math.sqrt(HEAD_DIM)
F32 = jnp.float32
BF16 = jnp.bfloat16
VMEM_LIMIT = 28 * 1024 * 1024
NT = (((1,), (1,)), ((), ()))
TN = (((0,), (0,)), ((), ()))


def dot(a, b):
    return jnp.dot(a, b, preferred_element_type=F32)


def dot_nt(a, b):
    return lax.dot_general(a, b, NT, preferred_element_type=F32)


def dot_tn(a, b):
    return lax.dot_general(a, b, TN, preferred_element_type=F32)


def window(head):
    first = head * HEAD_DIM // LANES
    last = (head * HEAD_DIM + HEAD_DIM - 1) // LANES
    return first * LANES, (last + 1 - first) * LANES


def head_lanes(head, rows):
    start, size = window(head)
    lane = lax.broadcasted_iota(jnp.int32, (rows, size), 1) + (start - head * HEAD_DIM)
    return (lane >= 0) & (lane < HEAD_DIM)


def clip_bias(lens_ref, rows, positions):
    def ids(axis):
        index = lax.broadcasted_iota(jnp.int32, (rows, rows), axis)
        frame = lax.div(index, jnp.int32(positions))
        clip = jnp.zeros_like(frame)
        end = jnp.int32(0)
        for j in range(lens_ref.shape[1]):
            end = end + lens_ref[0, j]
            clip = clip + jnp.where(frame >= end, 1, 0)
        return clip * positions + (index - frame * positions)

    return jnp.where(ids(0) == ids(1), 0.0, -jnp.inf).astype(F32)


def softmax(query_win, key_win, bias):
    scores = dot_nt(query_win, key_win) * SCALE + bias
    raised = jnp.exp(scores - jnp.max(scores, axis=-1, keepdims=True))
    return raised, 1.0 / jnp.sum(raised, axis=-1, keepdims=True)


class Tiles:
    def __init__(self, ref, base=0):
        self.ref, self.base, self.held = ref, base, {}

    def add(self, head, value):
        start, size = window(head)
        for off in range(0, size, LANES):
            piece = value[:, off : off + LANES]
            tile = start + off
            self.held[tile] = piece if tile not in self.held else self.held[tile] + piece
        done = (head + 1) * HEAD_DIM
        for tile in [t for t in self.held if t + LANES <= done]:
            lanes = pl.ds(self.base + tile, LANES)
            self.ref[:, lanes] = self.held.pop(tile).astype(self.ref.dtype)


FWD_FLOPS = 10**11
JOIN_FLOPS = 10**9
FINISH_FLOPS = 3 * 10**9
GROUP = 8
CUT = 384
FULL = 16
ODD = 2
CHUNK = 3
ODD_LANES = 384


def selection(rows, columns, wanted):
    row = lax.broadcasted_iota(jnp.int32, (rows, columns), 0)
    column = lax.broadcasted_iota(jnp.int32, (rows, columns), 1)
    return jnp.where(column == wanted(row), 1.0, 0.0).astype(BF16)


def chunk_tiles(ref, q):
    pieces = [ref[:, pl.ds((CHUNK * u + q) * LANES, LANES)] for u in range(CHUNK)]
    return jnp.concatenate(pieces, axis=1)


def pack_kernel(*refs):
    *parts, x_ref, staged_ref, sems = refs
    rows, width = parts[0].shape
    half = rows // 2
    fetches, copies = [], []
    for i, part in enumerate(parts):
        for j in range(2):
            at, lanes, n = pl.ds(j * half, half), pl.ds(i * width, width), 2 * i + j
            fetches.append(pltpu.make_async_copy(part.at[at], staged_ref.at[i, at], sems.at[0, n]))
            copies.append(pltpu.make_async_copy(staged_ref.at[i, at], x_ref.at[at, lanes], sems.at[1, n]))
    for fetch in fetches:
        fetch.start()
    for fetch, copy in zip(fetches, copies):
        fetch.wait()
        copy.start()
    for copy in copies:
        copy.wait()


def unpack_kernel(x_ref, *refs):
    *outs, sems = refs
    width = outs[0].shape[1]
    copies = [
        pltpu.make_async_copy(x_ref.at[:, pl.ds(i * width, width)], out, sems.at[i]) for i, out in enumerate(outs)
    ]
    for copy in copies:
        copy.start()
    for copy in copies:
        copy.wait()


def spread_kernel(weight_ref, out_ref, held_ref, sem):
    shard, width = weight_ref.shape
    rows = held_ref.shape[0]
    weight = weight_ref[...]

    def core(row):
        return jnp.bitwise_and(lax.div(row, jnp.int32(GROUP)), 1)

    def place(row):
        return jnp.bitwise_and(row, GROUP - 1)

    for block in range(FULL // GROUP):
        pick = selection(rows, shard, lambda row: FULL * core(row) + GROUP * block + place(row))
        held_ref[:, pl.ds(block * width, width)] = dot(pick, weight).astype(BF16)
    odd = jnp.zeros((rows, ODD_LANES), F32)
    for q in range(CHUNK):

        def wanted(row):
            k = lax.div(place(row) - q, jnp.int32(CHUNK))
            exact = (place(row) == CHUNK * k + q) & (k < ODD)
            return jnp.where(exact, 2 * FULL + ODD * core(row) + k, -1)

        odd = odd + dot(selection(rows, shard, wanted), chunk_tiles(weight_ref, q))
    held_ref[:, pl.ds(FULL // GROUP * width, ODD_LANES)] = odd.astype(BF16)
    copy = pltpu.make_async_copy(held_ref, out_ref, sem.at[0])
    copy.start()
    copy.wait()


def pick_rows(ref, place):
    padded, width = ref.shape
    block = padded // 8
    for step in range(8):
        at = lax.broadcasted_iota(jnp.int32, (block, width), 0) + step * block
        ref[pl.ds(step * block, block), :] = jnp.where(at == place, 1.0, 0.0).astype(BF16)


def tables_kernel(shard, positions, core_ref, lens_ref, pick_ref, bias_ref, held_ref, sem):
    width = pick_ref.shape[1]
    feature = lax.broadcasted_iota(jnp.int32, (1, width), 1)
    owner = lax.div(feature, jnp.int32(shard))
    rest = feature - owner * shard
    holder = jnp.where(rest < 2 * FULL, lax.div(rest, jnp.int32(FULL)), lax.div(rest - 2 * FULL, jnp.int32(ODD)))
    other = jnp.bitwise_and(holder + core_ref[0], 1)
    within = rest - FULL * holder
    block = lax.div(within, jnp.int32(GROUP))
    size = width // shard * GROUP
    full = (other * (FULL // GROUP) + block) * size + owner * GROUP + within - block * GROUP
    odd = 2 * (FULL // GROUP) * size + (other * (width // shard) + owner) * ODD + rest - 2 * FULL - ODD * holder
    pick_rows(held_ref, jnp.where(rest < 2 * FULL, full, odd))
    copy = pltpu.make_async_copy(held_ref, pick_ref, sem.at[0])
    copy.start()
    bias_ref[...] = clip_bias(lens_ref, bias_ref.shape[0], positions)
    copy.wait()


def forward_kernel(
    core_ref, x_hbm, bias_ref, mixed_ref, keep_ref, first_ref, second_ref, x_ref, part_ref, held_ref, turn_ref, sems
):
    rows, width = mixed_ref.shape
    middle = lane_half(width)
    pieces = [(a * width + b, c) for b, c in ((0, middle), (middle, width - middle)) for a in range(3)]
    pieces.append((3 * width, width))
    fetches = [
        pltpu.make_async_copy(x_hbm.at[:, pl.ds(at, size)], x_ref.at[:, pl.ds(at, size)], sems.at[5 + i])
        for i, (at, size) in enumerate(pieces)
    ]
    for fetch in fetches:
        fetch.start()
    bias = bias_ref[...]
    mixed_tiles = Tiles(mixed_ref)
    for head in range(HEADS):
        if head in (0, HEADS // 2):
            for fetch in fetches[3 * (head > 0) : 3 * (head > 0) + 3]:
                fetch.wait()
        start, size = window(head)
        lanes = head_lanes(head, rows)
        query_win = jnp.where(lanes, x_ref[:, pl.ds(start, size)], 0)
        key_win = x_ref[:, pl.ds(width + start, size)]
        value_win = jnp.where(lanes, x_ref[:, pl.ds(2 * width + start, size)], 0)
        raised, recip = softmax(query_win, key_win, bias)
        mixed_tiles.add(head, dot((raised * recip).astype(BF16), value_win))
    copies = []
    turn_ref[...] = jnp.zeros_like(turn_ref)
    fetches[6].wait()
    mixed = mixed_ref[...]
    block = 3 * LANES
    for at in range(0, width, block):
        part_ref[pl.ds(at, block), :] = dot_tn(x_ref[:, pl.ds(3 * width + at, block)], mixed)
    chips = held_ref.shape[0]
    shard = width // chips // 2

    def fold(ids, out_ref, other):
        for core in range(2):

            @pl.when(core_ref[0] == core)
            def _():
                for j in ids:
                    fold_rows(part_ref, (2 * j + (core ^ other)) * shard, shard, out_ref, j, turn_ref)

    for step in range(4):
        some = chips // 4
        fold(range(step * some, (step + 1) * some), held_ref, 1)
        source, place = pl.ds(step * some, some), pl.ds(step % 2 * some, some)
        send_ref = first_ref if step < 2 else second_ref
        copies.append(pltpu.make_async_copy(held_ref.at[source], send_ref.at[place], sems.at[step]))
        copies[-1].start()
    fold(range(chips), keep_ref, 0)
    for copy in copies:
        copy.wait()


def fold_rows(part_ref, at, shard, out_ref, j, turn_ref):
    width = part_ref.shape[1]
    size = lane_half(width)
    for group in range(shard // 8):
        rows = part_ref[pl.ds(at + group * 8, 8), :]
        out_ref[j, :, pl.ds(group * width, width)] = rows.astype(BF16)
    last = part_ref[pl.ds(at + shard // 8 * 8, 4), :]
    turn_ref[pl.ds(0, 4), :] = last[:, :size]
    turn_ref[pl.ds(4, 4), pl.ds(0, width - size)] = last[:, size:]
    out_ref[j, :, pl.ds(shard // 8 * width, size)] = turn_ref[...].astype(BF16)


def join_kernel(keep_ref, first_ref, second_ref, out_ref):
    lanes, total = out_ref.shape[3], keep_ref.shape[2]
    whole = lanes - CUT
    half = first_ref.shape[0]
    for at, ref in ((0, first_ref), (half, second_ref)):
        ids = pl.ds(at, half)
        added = (keep_ref[ids].astype(F32) + ref[...].astype(F32)).astype(BF16)
        out_ref[0, ids, :, pl.ds(0, whole)] = added[:, :, :whole]
        out_ref[1, ids, :, pl.ds(0, whole)] = added[:, :, whole : 2 * whole]
        rest = pl.ds(whole, lanes - whole)
        out_ref[0, ids, :, rest] = added[:, :, 2 * whole : whole + lanes]
        out_ref[1, ids, :, rest] = added[:, :, total - (lanes - whole) :]


def finish_kernel(place_ref, mine_ref, other_ref, out_ref):
    width = out_ref.shape[1]
    size = lane_half(width)
    mine, other = mine_ref[...].astype(F32), other_ref[...].astype(F32)
    low = place_ref[0] == 0
    lower, upper = jnp.where(low, mine, other), jnp.where(low, other, mine)
    for group, half in enumerate((lower, lower, upper, upper)):
        at = group % 2 * width
        out_ref[pl.ds(group * 8, 8), :] = half[:, at : at + width]
    turned = jnp.concatenate([lower[:, 2 * width :], upper[:, 2 * width + 2 * CUT - size :]], axis=1)
    out_ref[pl.ds(32, 4), pl.ds(0, size)] = turned[:4]
    out_ref[pl.ds(32, 4), pl.ds(size, width - size)] = turned[4:, : width - size]


def backward_kernel(
    pick_hbm, x_hbm, own_hbm, other_ref, bias_ref, mixed_ref, y_ref,
    pick_ref, x_ref, own_ref, odd_ref, back_ref, out_ref, held_ref, attention_ref, sems
):
    rows, width = mixed_ref.shape
    pairs, third, fourth = pl.ds(0, 2 * width), pl.ds(2 * width, width), pl.ds(3 * width, width)
    fetches = [
        pltpu.make_async_copy(x_hbm.at[:, pairs], x_ref.at[:, pairs], sems.at[7]),
        pltpu.make_async_copy(own_hbm, own_ref, sems.at[8]),
        pltpu.make_async_copy(x_hbm.at[:, fourth], x_ref.at[:, fourth], sems.at[9]),
        pltpu.make_async_copy(pick_hbm, pick_ref, sems.at[10]),
        pltpu.make_async_copy(x_hbm.at[:, third], x_ref.at[:, third], sems.at[11]),
    ]
    for fetch in fetches:
        fetch.start()
    copies = []

    def send(start, size):
        lanes = pl.ds(start, size)
        copies.append(pltpu.make_async_copy(held_ref.at[:, lanes], y_ref.at[:, lanes], sems.at[len(copies)]))
        copies[-1].start()

    fetches[0].wait()
    bias = bias_ref[...]
    for head in range(HEADS):
        start, size = window(head)
        query_win = jnp.where(head_lanes(head, rows), x_ref[:, pl.ds(start, size)], 0)
        scores = dot_nt(x_ref[:, pl.ds(width + start, size)], query_win) * SCALE + bias
        raised = jnp.exp(scores - jnp.max(scores, axis=0, keepdims=True))
        attention_ref[head] = raised * (1.0 / jnp.sum(raised, axis=0, keepdims=True))
    blocks = FULL // GROUP
    fetches[1].wait()
    weight = []
    for ref in (own_ref, other_ref):
        weight += [ref[:, pl.ds(b * width, width)] for b in range(blocks)]
    odd_rows = odd_ref.shape[0] // 2
    for i, ref in enumerate((own_ref, other_ref)):
        left = ref[:, pl.ds(blocks * width, ODD_LANES)]
        for q in range(CHUNK):

            def wanted(row):
                source = lax.div(row, jnp.int32(ODD))
                return source * GROUP + CHUNK * (row - ODD * source) + q

            got = dot(selection(odd_rows, rows, wanted), left).astype(BF16)
            for u in range(CHUNK):
                lanes = pl.ds((CHUNK * u + q) * LANES, LANES)
                odd_ref[pl.ds(i * odd_rows, odd_rows), lanes] = got[:, u * LANES : (u + 1) * LANES]
    weight.append(odd_ref[...])
    fetches[2].wait()
    fetches[3].wait()
    grad = dot_nt(x_ref[:, fourth], pick_ref[...]).astype(BF16)
    mixed = mixed_ref[...]
    back = jnp.zeros((rows, width), F32)
    at = 0
    for block in weight:
        size = block.shape[0]
        back = back + dot(grad[:, at : at + size], block)
        out_ref[:, pl.ds(at, size)] = dot_nt(mixed, block).astype(BF16)
        at += size
    back_ref[...] = back.astype(BF16)
    held_ref[:, pl.ds(0, width)] = dot(out_ref[...], pick_ref[...]).astype(BF16)
    send(0, width)
    query_tiles, key_tiles, value_tiles = [Tiles(held_ref, i * width) for i in (1, 2, 3)]
    fetches[4].wait()
    sent = 0
    for head in range(HEADS):
        start, size = window(head)
        lanes = head_lanes(head, rows)
        query_win = jnp.where(lanes, x_ref[:, pl.ds(start, size)], 0)
        key_win = jnp.where(lanes, x_ref[:, pl.ds(width + start, size)], 0)
        value_win = x_ref[:, pl.ds(2 * width + start, size)]
        back_win = jnp.where(lanes, back_ref[:, pl.ds(start, size)], 0)
        attention = attention_ref[head]
        value_tiles.add(head, dot(attention.astype(BF16), back_win))
        drawn = attention * dot_nt(value_win, back_win)
        inner = jnp.sum(drawn, axis=0, keepdims=True)
        score_grad = ((drawn - attention * inner) * SCALE).astype(BF16)
        key_tiles.add(head, dot(score_grad, query_win))
        query_tiles.add(head, dot_tn(score_grad, key_win))
        if head in (HEADS // 2 - 1, HEADS - 1):
            done = (head + 1) * HEAD_DIM // LANES * LANES
            for i in (1, 2, 3):
                send(i * width + sent, done - sent)
            sent = done
    for copy in copies:
        copy.wait()


def total_kernel(parts_ref, out_ref):
    total = parts_ref[0].astype(F32)
    for j in range(1, parts_ref.shape[0]):
        total = total + parts_ref[j].astype(F32)
    out_ref[...] = total.astype(BF16)


def call(kernel, name, outs, args, smem=0, hbm_in=0, hbm_out=(), scratch=(), flops=0):
    space = [pltpu.SMEM] * smem + [pltpu.HBM] * hbm_in + [pltpu.VMEM] * (len(args) - smem - hbm_in)
    args = [pltpu.with_memory_space_constraint(a, s) if s == pltpu.HBM else a for a, s in zip(args, space)]
    shapes = [jax.ShapeDtypeStruct(shape, dtype) for shape, dtype in outs]
    moved = sum(a.size * a.dtype.itemsize for a in args) + sum(math.prod(s.shape) * s.dtype.itemsize for s in shapes)
    return pl.pallas_call(
        kernel,
        out_shape=[pltpu.HBM(s.shape, s.dtype) if i in hbm_out else s for i, s in enumerate(shapes)],
        in_specs=[pl.BlockSpec(memory_space=s) for s in space],
        out_specs=[pl.BlockSpec(memory_space=pltpu.HBM if i in hbm_out else pltpu.VMEM) for i in range(len(outs))],
        scratch_shapes=scratch,
        compiler_params=pltpu.CompilerParams(vmem_limit_bytes=VMEM_LIMIT),
        cost_estimate=pl.CostEstimate(flops=flops, bytes_accessed=0 if flops else moved, transcendentals=0),
        name=name,
    )(*args)


def dma(count):
    return pltpu.SemaphoreType.DMA((count,))


def pack(arrays):
    rows, width = arrays[0].shape
    count = len(arrays)
    outs = [((rows, count * width), BF16)]
    scratch = [pltpu.VMEM((count, rows, width), BF16), pltpu.SemaphoreType.DMA((2, 2 * count))]
    return call(pack_kernel, "pack", outs, arrays, hbm_in=count, hbm_out=(0,), scratch=scratch)[0]


def unpack(x, count):
    rows, wide = x.shape
    width = wide // count
    outs = [((rows, width), BF16)] * count
    return call(unpack_kernel, "unpack", outs, (x,), hbm_out=range(count), scratch=[dma(count)])


def spread(weight_t, rows):
    shape = (rows, FULL // GROUP * weight_t.shape[1] + ODD_LANES)
    scratch = [pltpu.VMEM(shape, BF16), dma(1)]
    return call(spread_kernel, "spread", [(shape, BF16)], (weight_t,), hbm_out=(0,), scratch=scratch)[0]


def tables(core, lengths, rows, width, shard, positions):
    kernel = functools.partial(tables_kernel, shard, positions)
    outs = [((width, width), BF16), ((rows, rows), F32)]
    scratch = [pltpu.VMEM((width, width), BF16), dma(1)]
    return call(kernel, "tables", outs, (core, lengths), smem=2, hbm_out=(0,), scratch=scratch)


def forward(core, x, bias, width, chips):
    rows = x.shape[0]
    folded = 4 * width + lane_half(width)
    part, half = (chips, 8, folded), (chips // 2, 8, folded)
    outs = [((rows, width), BF16), (part, BF16), (half, BF16), (half, BF16)]
    scratch = [pltpu.VMEM(x.shape, BF16), pltpu.VMEM((width, width), F32), pltpu.VMEM(part, BF16)]
    scratch += [pltpu.VMEM((8, lane_half(width)), F32), dma(12)]
    args = (core, x, bias)
    return call(
        forward_kernel, "forward", outs, args, smem=1, hbm_in=1, hbm_out=(2, 3), scratch=scratch, flops=FWD_FLOPS
    )


def join(keep, first, second, width):
    outs = [((2, keep.shape[0], 8, 2 * width + CUT), BF16)]
    return call(join_kernel, "join", outs, (keep, first, second), flops=JOIN_FLOPS)[0]


def backward(pick, x, own, other, bias, mixed):
    rows, width = mixed.shape
    flops = 8 * width * rows * width + 12 * HEADS * rows * rows * 256
    one, wide = (rows, width), (rows, 4 * width)
    shapes = ((width, width), wide, own.shape, (width - 4 * rows, width), one, one, wide)
    scratch = [pltpu.VMEM(shape, BF16) for shape in shapes]
    scratch += [pltpu.VMEM((HEADS, rows, rows), F32), dma(12)]
    args = (pick, x, own, other, bias, mixed)
    return call(backward_kernel, "backward", [(wide, BF16)], args, hbm_in=3, hbm_out=(0,), scratch=scratch, flops=flops)[0]


def total_of(parts):
    return call(total_kernel, "total", [(parts.shape[1:], BF16)], (parts,))[0]


def lane_half(width):
    return (width // LANES + 1) // 2 * LANES


def sum_over_pairs(block, place, shard, width, n_dp):
    half, quarter = n_dp // 2, n_dp // 4

    def exchange(block, source):
        return lax.ppermute(block, "dp", [(source(i) % n_dp, i) for i in range(n_dp)])

    def added(block, source):
        return (block.astype(F32) + exchange(block, source).astype(F32)).astype(BF16)

    def second(i):
        return i ^ quarter if i % 2 == 0 else i + quarter * (1 if i // quarter % 2 else -1)

    def third(i):
        return n_dp - 2 - i if i % 2 == 0 else half - i

    block = added(added(added(block, lambda i: i ^ 2), second), third)
    args = (place, block, exchange(block, lambda i: i ^ 1))
    return call(finish_kernel, "finish", [((shard, width), F32)], args, smem=1, flops=FINISH_FLOPS)[0]


def on_device(n_seq, n_dp, queries, key_vectors, value_vectors, out_grad, out_weight, clip_frames):
    patches, width = queries.shape[2:]
    positions = patches // n_seq
    shard = out_weight.shape[1]
    core = jnp.bitwise_and(lax.axis_index("seq"), 1).astype(jnp.int32)

    def swap(block):
        return lax.all_to_all(block.reshape(n_seq, positions, -1), "seq", 0, 0, tiled=True)

    def partner(block):
        return lax.ppermute(block, "seq", [(i, i ^ 1) for i in range(n_seq)])

    arrays = [a.reshape(patches, width) for a in (queries, key_vectors, value_vectors, out_grad)]
    x = swap(pack(arrays)).reshape(patches, -1)
    rows, x = lax.optimization_barrier((spread(out_weight.T, patches), x))
    own = swap(rows).reshape(patches, -1)
    pick, bias = tables(core.reshape(1), clip_frames, patches, width, shard, positions)
    mixed, keep, *send = forward(core.reshape(1), x, bias, width, n_seq // 2)

    chip = join(keep, *[partner(block) for block in send], width)
    chip = chip.reshape(n_seq, *chip.shape[2:])
    pairs = [
        [(p + d) * n_seq + i for d in (0, 1) for i in range(c, n_seq, 2)] for p in range(0, n_dp, 2) for c in (0, 1)
    ]
    parts = lax.all_to_all(chip, ("dp", "seq"), 0, 0, tiled=True, axis_index_groups=pairs)

    y = backward(pick, x, own, partner(own), bias, mixed)
    total, y = lax.optimization_barrier((total_of(parts), y))
    back = swap(y).reshape(patches, 4 * width)
    place = jnp.bitwise_and(lax.axis_index("dp"), 1).astype(jnp.int32).reshape(1)
    weight_grad = sum_over_pairs(total, place, shard, width, n_dp).T
    outs = [out.reshape(queries.shape) for out in unpack(back, 4)]
    return (*outs, weight_grad)


def solution(mesh):
    whole = P("dp", "seq", None, None)
    return jax.shard_map(
        functools.partial(on_device, mesh.shape["seq"], mesh.shape["dp"]),
        mesh=mesh,
        in_specs=(whole, whole, whole, whole, P(None, "seq"), P("dp", None)),
        out_specs=(whole, whole, whole, whole, P(None, "seq")),
        check_vma=False,
    )
```

```python
import functools
import math

import jax
import jax.numpy as jnp
from jax import lax
from jax.experimental import pallas as pl
from jax.experimental.pallas import tpu as pltpu
from jax.sharding import PartitionSpec as P

HEADS = 16
HEAD_DIM = 72
LANES = 128
SCALE = 1.0 / math.sqrt(HEAD_DIM)
F32 = jnp.float32
BF16 = jnp.bfloat16
VMEM_LIMIT = 28 * 1024 * 1024
NT = (((1,), (1,)), ((), ()))
TN = (((0,), (0,)), ((), ()))


def dot(a, b):
    return jnp.dot(a, b, preferred_element_type=F32)


def dot_nt(a, b):
    return lax.dot_general(a, b, NT, preferred_element_type=F32)


def dot_tn(a, b):
    return lax.dot_general(a, b, TN, preferred_element_type=F32)


def window(head):
    first = head * HEAD_DIM // LANES
    last = (head * HEAD_DIM + HEAD_DIM - 1) // LANES
    return first * LANES, (last + 1 - first) * LANES


def head_lanes(head, rows):
    start, size = window(head)
    lane = lax.broadcasted_iota(jnp.int32, (rows, size), 1) + (start - head * HEAD_DIM)
    return (lane >= 0) & (lane < HEAD_DIM)


def clip_bias(lens_ref, rows, positions):
    def ids(axis):
        index = lax.broadcasted_iota(jnp.int32, (rows, rows), axis)
        frame = lax.div(index, jnp.int32(positions))
        clip = jnp.zeros_like(frame)
        end = jnp.int32(0)
        for j in range(lens_ref.shape[1]):
            end = end + lens_ref[0, j]
            clip = clip + jnp.where(frame >= end, 1, 0)
        return clip * positions + (index - frame * positions)

    return jnp.where(ids(0) == ids(1), 0.0, -jnp.inf).astype(F32)


def softmax(query_win, key_win, bias):
    scores = dot_nt(query_win, key_win) * SCALE + bias
    raised = jnp.exp(scores - jnp.max(scores, axis=-1, keepdims=True))
    return raised, 1.0 / jnp.sum(raised, axis=-1, keepdims=True)


class Tiles:
    def __init__(self, ref, base=0):
        self.ref, self.base, self.held = ref, base, {}

    def add(self, head, value):
        start, size = window(head)
        for off in range(0, size, LANES):
            piece = value[:, off : off + LANES]
            tile = start + off
            self.held[tile] = piece if tile not in self.held else self.held[tile] + piece
        done = (head + 1) * HEAD_DIM
        for tile in [t for t in self.held if t + LANES <= done]:
            lanes = pl.ds(self.base + tile, LANES)
            self.ref[:, lanes] = self.held.pop(tile).astype(self.ref.dtype)


FWD_FLOPS = 10**11
JOIN_FLOPS = 10**9
FINISH_FLOPS = 3 * 10**9
GROUP = 8
CUT = 384
FULL = 16
ODD = 2
CHUNK = 3
ODD_LANES = 384


def selection(rows, columns, wanted):
    row = lax.broadcasted_iota(jnp.int32, (rows, columns), 0)
    column = lax.broadcasted_iota(jnp.int32, (rows, columns), 1)
    return jnp.where(column == wanted(row), 1.0, 0.0).astype(BF16)


def chunk_tiles(ref, q):
    pieces = [ref[:, pl.ds((CHUNK * u + q) * LANES, LANES)] for u in range(CHUNK)]
    return jnp.concatenate(pieces, axis=1)


def pack_kernel(*refs):
    *parts, x_ref, staged_ref, sems = refs
    rows, width = parts[0].shape
    half = rows // 2
    fetches, copies = [], []
    for i, part in enumerate(parts):
        for j in range(2):
            at, lanes, n = pl.ds(j * half, half), pl.ds(i * width, width), 2 * i + j
            fetches.append(pltpu.make_async_copy(part.at[at], staged_ref.at[i, at], sems.at[0, n]))
            copies.append(pltpu.make_async_copy(staged_ref.at[i, at], x_ref.at[at, lanes], sems.at[1, n]))
    for fetch in fetches:
        fetch.start()
    for fetch, copy in zip(fetches, copies):
        fetch.wait()
        copy.start()
    for copy in copies:
        copy.wait()


def unpack_kernel(x_ref, *refs):
    *outs, sems = refs
    width = outs[0].shape[1]
    copies = [
        pltpu.make_async_copy(x_ref.at[:, pl.ds(i * width, width)], out, sems.at[i]) for i, out in enumerate(outs)
    ]
    for copy in copies:
        copy.start()
    for copy in copies:
        copy.wait()


def spread_kernel(weight_ref, out_ref, held_ref, sem):
    shard, width = weight_ref.shape
    rows = held_ref.shape[0]
    weight = weight_ref[...]

    def core(row):
        return jnp.bitwise_and(lax.div(row, jnp.int32(GROUP)), 1)

    def place(row):
        return jnp.bitwise_and(row, GROUP - 1)

    for block in range(FULL // GROUP):
        pick = selection(rows, shard, lambda row: FULL * core(row) + GROUP * block + place(row))
        held_ref[:, pl.ds(block * width, width)] = dot(pick, weight).astype(BF16)
    odd = jnp.zeros((rows, ODD_LANES), F32)
    for q in range(CHUNK):

        def wanted(row):
            k = lax.div(place(row) - q, jnp.int32(CHUNK))
            exact = (place(row) == CHUNK * k + q) & (k < ODD)
            return jnp.where(exact, 2 * FULL + ODD * core(row) + k, -1)

        odd = odd + dot(selection(rows, shard, wanted), chunk_tiles(weight_ref, q))
    held_ref[:, pl.ds(FULL // GROUP * width, ODD_LANES)] = odd.astype(BF16)
    copy = pltpu.make_async_copy(held_ref, out_ref, sem.at[0])
    copy.start()
    copy.wait()


def pick_rows(ref, place):
    padded, width = ref.shape
    block = padded // 8
    for step in range(8):
        at = lax.broadcasted_iota(jnp.int32, (block, width), 0) + step * block
        ref[pl.ds(step * block, block), :] = jnp.where(at == place, 1.0, 0.0).astype(BF16)


def tables_kernel(shard, positions, core_ref, lens_ref, pick_ref, bias_ref, held_ref, sem):
    width = pick_ref.shape[1]
    feature = lax.broadcasted_iota(jnp.int32, (1, width), 1)
    owner = lax.div(feature, jnp.int32(shard))
    rest = feature - owner * shard
    holder = jnp.where(rest < 2 * FULL, lax.div(rest, jnp.int32(FULL)), lax.div(rest - 2 * FULL, jnp.int32(ODD)))
    other = jnp.bitwise_and(holder + core_ref[0], 1)
    within = rest - FULL * holder
    block = lax.div(within, jnp.int32(GROUP))
    size = width // shard * GROUP
    full = (other * (FULL // GROUP) + block) * size + owner * GROUP + within - block * GROUP
    odd = 2 * (FULL // GROUP) * size + (other * (width // shard) + owner) * ODD + rest - 2 * FULL - ODD * holder
    pick_rows(held_ref, jnp.where(rest < 2 * FULL, full, odd))
    copy = pltpu.make_async_copy(held_ref, pick_ref, sem.at[0])
    copy.start()
    bias_ref[...] = clip_bias(lens_ref, bias_ref.shape[0], positions)
    copy.wait()


def forward_kernel(
    core_ref, x_ref, bias_ref, mixed_ref, keep_ref, first_ref, second_ref, part_ref, held_ref, turn_ref, sems
):
    rows, width = mixed_ref.shape
    bias = bias_ref[...]
    mixed_tiles = Tiles(mixed_ref)
    for head in range(HEADS):
        start, size = window(head)
        lanes = head_lanes(head, rows)
        query_win = jnp.where(lanes, x_ref[:, pl.ds(start, size)], 0)
        key_win = x_ref[:, pl.ds(width + start, size)]
        value_win = jnp.where(lanes, x_ref[:, pl.ds(2 * width + start, size)], 0)
        raised, recip = softmax(query_win, key_win, bias)
        mixed_tiles.add(head, dot((raised * recip).astype(BF16), value_win))
    copies = []
    turn_ref[...] = jnp.zeros_like(turn_ref)
    mixed = mixed_ref[...]
    block = 3 * LANES
    for at in range(0, width, block):
        part_ref[pl.ds(at, block), :] = dot_tn(x_ref[:, pl.ds(3 * width + at, block)], mixed)
    chips = held_ref.shape[0]
    shard = width // chips // 2

    def fold(ids, out_ref, other):
        for core in range(2):

            @pl.when(core_ref[0] == core)
            def _():
                for j in ids:
                    fold_rows(part_ref, (2 * j + (core ^ other)) * shard, shard, out_ref, j, turn_ref)

    for step in range(4):
        some = chips // 4
        fold(range(step * some, (step + 1) * some), held_ref, 1)
        source, place = pl.ds(step * some, some), pl.ds(step % 2 * some, some)
        send_ref = first_ref if step < 2 else second_ref
        copies.append(pltpu.make_async_copy(held_ref.at[source], send_ref.at[place], sems.at[step]))
        copies[-1].start()
    fold(range(chips), keep_ref, 0)
    for copy in copies:
        copy.wait()


def fold_rows(part_ref, at, shard, out_ref, j, turn_ref):
    width = part_ref.shape[1]
    size = lane_half(width)
    for group in range(shard // 8):
        rows = part_ref[pl.ds(at + group * 8, 8), :]
        out_ref[j, :, pl.ds(group * width, width)] = rows.astype(BF16)
    last = part_ref[pl.ds(at + shard // 8 * 8, 4), :]
    turn_ref[pl.ds(0, 4), :] = last[:, :size]
    turn_ref[pl.ds(4, 4), pl.ds(0, width - size)] = last[:, size:]
    out_ref[j, :, pl.ds(shard // 8 * width, size)] = turn_ref[...].astype(BF16)


def join_kernel(keep_ref, first_ref, second_ref, out_ref):
    lanes, total = out_ref.shape[3], keep_ref.shape[2]
    whole = lanes - CUT
    half = first_ref.shape[0]
    for at, ref in ((0, first_ref), (half, second_ref)):
        ids = pl.ds(at, half)
        added = (keep_ref[ids].astype(F32) + ref[...].astype(F32)).astype(BF16)
        out_ref[0, ids, :, pl.ds(0, whole)] = added[:, :, :whole]
        out_ref[1, ids, :, pl.ds(0, whole)] = added[:, :, whole : 2 * whole]
        rest = pl.ds(whole, lanes - whole)
        out_ref[0, ids, :, rest] = added[:, :, 2 * whole : whole + lanes]
        out_ref[1, ids, :, rest] = added[:, :, total - (lanes - whole) :]


def finish_kernel(place_ref, mine_ref, other_ref, out_ref):
    width = out_ref.shape[1]
    size = lane_half(width)
    mine, other = mine_ref[...].astype(F32), other_ref[...].astype(F32)
    low = place_ref[0] == 0
    lower, upper = jnp.where(low, mine, other), jnp.where(low, other, mine)
    for group, half in enumerate((lower, lower, upper, upper)):
        at = group % 2 * width
        out_ref[pl.ds(group * 8, 8), :] = half[:, at : at + width]
    turned = jnp.concatenate([lower[:, 2 * width :], upper[:, 2 * width + 2 * CUT - size :]], axis=1)
    out_ref[pl.ds(32, 4), pl.ds(0, size)] = turned[:4]
    out_ref[pl.ds(32, 4), pl.ds(size, width - size)] = turned[4:, : width - size]


def backward_kernel(
    pick_hbm, x_hbm, own_hbm, other_ref, bias_ref, mixed_ref, y_ref,
    pick_ref, x_ref, own_ref, odd_ref, back_ref, out_ref, held_ref, attention_ref, sems
):
    rows, width = mixed_ref.shape
    pairs, third, fourth = pl.ds(0, 2 * width), pl.ds(2 * width, width), pl.ds(3 * width, width)
    fetches = [
        pltpu.make_async_copy(x_hbm.at[:, pairs], x_ref.at[:, pairs], sems.at[7]),
        pltpu.make_async_copy(own_hbm, own_ref, sems.at[8]),
        pltpu.make_async_copy(x_hbm.at[:, fourth], x_ref.at[:, fourth], sems.at[9]),
        pltpu.make_async_copy(pick_hbm, pick_ref, sems.at[10]),
        pltpu.make_async_copy(x_hbm.at[:, third], x_ref.at[:, third], sems.at[11]),
    ]
    for fetch in fetches:
        fetch.start()
    copies = []

    def send(start, size):
        lanes = pl.ds(start, size)
        copies.append(pltpu.make_async_copy(held_ref.at[:, lanes], y_ref.at[:, lanes], sems.at[len(copies)]))
        copies[-1].start()

    fetches[0].wait()
    bias = bias_ref[...]
    for head in range(HEADS):
        start, size = window(head)
        query_win = jnp.where(head_lanes(head, rows), x_ref[:, pl.ds(start, size)], 0)
        scores = dot_nt(x_ref[:, pl.ds(width + start, size)], query_win) * SCALE + bias
        raised = jnp.exp(scores - jnp.max(scores, axis=0, keepdims=True))
        attention_ref[head] = raised * (1.0 / jnp.sum(raised, axis=0, keepdims=True))
    blocks = FULL // GROUP
    fetches[1].wait()
    weight = []
    for ref in (own_ref, other_ref):
        weight += [ref[:, pl.ds(b * width, width)] for b in range(blocks)]
    odd_rows = odd_ref.shape[0] // 2
    for i, ref in enumerate((own_ref, other_ref)):
        left = ref[:, pl.ds(blocks * width, ODD_LANES)]
        for q in range(CHUNK):

            def wanted(row):
                source = lax.div(row, jnp.int32(ODD))
                return source * GROUP + CHUNK * (row - ODD * source) + q

            got = dot(selection(odd_rows, rows, wanted), left).astype(BF16)
            for u in range(CHUNK):
                lanes = pl.ds((CHUNK * u + q) * LANES, LANES)
                odd_ref[pl.ds(i * odd_rows, odd_rows), lanes] = got[:, u * LANES : (u + 1) * LANES]
    weight.append(odd_ref[...])
    fetches[2].wait()
    fetches[3].wait()
    grad = dot_nt(x_ref[:, fourth], pick_ref[...]).astype(BF16)
    mixed = mixed_ref[...]
    back = jnp.zeros((rows, width), F32)
    at = 0
    for block in weight:
        size = block.shape[0]
        back = back + dot(grad[:, at : at + size], block)
        out_ref[:, pl.ds(at, size)] = dot_nt(mixed, block).astype(BF16)
        at += size
    back_ref[...] = back.astype(BF16)
    held_ref[:, pl.ds(0, width)] = dot(out_ref[...], pick_ref[...]).astype(BF16)
    send(0, width)
    query_tiles, key_tiles, value_tiles = [Tiles(held_ref, i * width) for i in (1, 2, 3)]
    fetches[4].wait()
    sent = 0
    for head in range(HEADS):
        start, size = window(head)
        lanes = head_lanes(head, rows)
        query_win = jnp.where(lanes, x_ref[:, pl.ds(start, size)], 0)
        key_win = jnp.where(lanes, x_ref[:, pl.ds(width + start, size)], 0)
        value_win = x_ref[:, pl.ds(2 * width + start, size)]
        back_win = jnp.where(lanes, back_ref[:, pl.ds(start, size)], 0)
        attention = attention_ref[head]
        value_tiles.add(head, dot(attention.astype(BF16), back_win))
        drawn = attention * dot_nt(value_win, back_win)
        inner = jnp.sum(drawn, axis=0, keepdims=True)
        score_grad = ((drawn - attention * inner) * SCALE).astype(BF16)
        key_tiles.add(head, dot(score_grad, query_win))
        query_tiles.add(head, dot_tn(score_grad, key_win))
        if head in (HEADS // 2 - 1, HEADS - 1):
            done = (head + 1) * HEAD_DIM // LANES * LANES
            for i in (1, 2, 3):
                send(i * width + sent, done - sent)
            sent = done
    for copy in copies:
        copy.wait()


def total_kernel(parts_ref, out_ref):
    total = parts_ref[0].astype(F32)
    for j in range(1, parts_ref.shape[0]):
        total = total + parts_ref[j].astype(F32)
    out_ref[...] = total.astype(BF16)


def call(kernel, name, outs, args, smem=0, hbm_in=0, hbm_out=(), scratch=(), flops=0):
    space = [pltpu.SMEM] * smem + [pltpu.HBM] * hbm_in + [pltpu.VMEM] * (len(args) - smem - hbm_in)
    args = [pltpu.with_memory_space_constraint(a, s) if s == pltpu.HBM else a for a, s in zip(args, space)]
    shapes = [jax.ShapeDtypeStruct(shape, dtype) for shape, dtype in outs]
    moved = sum(a.size * a.dtype.itemsize for a in args) + sum(math.prod(s.shape) * s.dtype.itemsize for s in shapes)
    return pl.pallas_call(
        kernel,
        out_shape=[pltpu.HBM(s.shape, s.dtype) if i in hbm_out else s for i, s in enumerate(shapes)],
        in_specs=[pl.BlockSpec(memory_space=s) for s in space],
        out_specs=[pl.BlockSpec(memory_space=pltpu.HBM if i in hbm_out else pltpu.VMEM) for i in range(len(outs))],
        scratch_shapes=scratch,
        compiler_params=pltpu.CompilerParams(vmem_limit_bytes=VMEM_LIMIT),
        cost_estimate=pl.CostEstimate(flops=flops, bytes_accessed=0 if flops else moved, transcendentals=0),
        name=name,
    )(*args)


def dma(count):
    return pltpu.SemaphoreType.DMA((count,))


def pack(arrays):
    rows, width = arrays[0].shape
    count = len(arrays)
    outs = [((rows, count * width), BF16)]
    scratch = [pltpu.VMEM((count, rows, width), BF16), pltpu.SemaphoreType.DMA((2, 2 * count))]
    return call(pack_kernel, "pack", outs, arrays, hbm_in=count, hbm_out=(0,), scratch=scratch)[0]


def unpack(x, count):
    rows, wide = x.shape
    width = wide // count
    outs = [((rows, width), BF16)] * count
    return call(unpack_kernel, "unpack", outs, (x,), hbm_out=range(count), scratch=[dma(count)])


def spread(weight_t, rows):
    shape = (rows, FULL // GROUP * weight_t.shape[1] + ODD_LANES)
    scratch = [pltpu.VMEM(shape, BF16), dma(1)]
    return call(spread_kernel, "spread", [(shape, BF16)], (weight_t,), hbm_out=(0,), scratch=scratch)[0]


def tables(core, lengths, rows, width, shard, positions):
    kernel = functools.partial(tables_kernel, shard, positions)
    outs = [((width, width), BF16), ((rows, rows), F32)]
    scratch = [pltpu.VMEM((width, width), BF16), dma(1)]
    return call(kernel, "tables", outs, (core, lengths), smem=2, hbm_out=(0,), scratch=scratch)


def forward(core, x, bias, width, chips):
    rows = x.shape[0]
    folded = 4 * width + lane_half(width)
    part, half = (chips, 8, folded), (chips // 2, 8, folded)
    outs = [((rows, width), BF16), (part, BF16), (half, BF16), (half, BF16)]
    scratch = [pltpu.VMEM((width, width), F32), pltpu.VMEM(part, BF16), pltpu.VMEM((8, lane_half(width)), F32), dma(4)]
    args = (core, x, bias)
    return call(
        forward_kernel, "forward", outs, args, smem=1, hbm_out=(2, 3), scratch=scratch, flops=FWD_FLOPS
    )


def join(keep, first, second, width):
    outs = [((2, keep.shape[0], 8, 2 * width + CUT), BF16)]
    return call(join_kernel, "join", outs, (keep, first, second), flops=JOIN_FLOPS)[0]


def backward(pick, x, own, other, bias, mixed):
    rows, width = mixed.shape
    flops = 8 * width * rows * width + 12 * HEADS * rows * rows * 256
    one, wide = (rows, width), (rows, 4 * width)
    shapes = ((width, width), wide, own.shape, (width - 4 * rows, width), one, one, wide)
    scratch = [pltpu.VMEM(shape, BF16) for shape in shapes]
    scratch += [pltpu.VMEM((HEADS, rows, rows), F32), dma(12)]
    args = (pick, x, own, other, bias, mixed)
    return call(backward_kernel, "backward", [(wide, BF16)], args, hbm_in=3, hbm_out=(0,), scratch=scratch, flops=flops)[0]


def total_of(parts):
    return call(total_kernel, "total", [(parts.shape[1:], BF16)], (parts,))[0]


def lane_half(width):
    return (width // LANES + 1) // 2 * LANES


def sum_over_pairs(block, place, shard, width, n_dp):
    half, quarter = n_dp // 2, n_dp // 4

    def exchange(block, source):
        return lax.ppermute(block, "dp", [(source(i) % n_dp, i) for i in range(n_dp)])

    def added(block, source):
        return (block.astype(F32) + exchange(block, source).astype(F32)).astype(BF16)

    def second(i):
        return i ^ quarter if i % 2 == 0 else i + quarter * (1 if i // quarter % 2 else -1)

    def third(i):
        return n_dp - 2 - i if i % 2 == 0 else half - i

    block = added(added(added(block, lambda i: i ^ 2), second), third)
    args = (place, block, exchange(block, lambda i: i ^ 1))
    return call(finish_kernel, "finish", [((shard, width), F32)], args, smem=1, flops=FINISH_FLOPS)[0]


def on_device(n_seq, n_dp, queries, key_vectors, value_vectors, out_grad, out_weight, clip_frames):
    patches, width = queries.shape[2:]
    positions = patches // n_seq
    shard = out_weight.shape[1]
    core = jnp.bitwise_and(lax.axis_index("seq"), 1).astype(jnp.int32)

    def swap(block):
        return lax.all_to_all(block.reshape(n_seq, positions, -1), "seq", 0, 0, tiled=True)

    def partner(block):
        return lax.ppermute(block, "seq", [(i, i ^ 1) for i in range(n_seq)])

    arrays = [a.reshape(patches, width) for a in (queries, key_vectors, value_vectors, out_grad)]
    x = swap(pack(arrays)).reshape(patches, -1)
    rows, x = lax.optimization_barrier((spread(out_weight.T, patches), x))
    own = swap(rows).reshape(patches, -1)
    pick, bias = tables(core.reshape(1), clip_frames, patches, width, shard, positions)
    mixed, keep, *send = forward(core.reshape(1), x, bias, width, n_seq // 2)

    chip = join(keep, *[partner(block) for block in send], width)
    chip = chip.reshape(n_seq, *chip.shape[2:])
    pairs = [
        [(p + d) * n_seq + i for d in (0, 1) for i in range(c, n_seq, 2)] for p in range(0, n_dp, 2) for c in (0, 1)
    ]
    parts = lax.all_to_all(chip, ("dp", "seq"), 0, 0, tiled=True, axis_index_groups=pairs)

    y = backward(pick, x, own, partner(own), bias, mixed)
    total, y = lax.optimization_barrier((total_of(parts), y))
    back = swap(y).reshape(patches, 4 * width)
    place = jnp.bitwise_and(lax.axis_index("dp"), 1).astype(jnp.int32).reshape(1)
    weight_grad = sum_over_pairs(total, place, shard, width, n_dp).T
    outs = [out.reshape(queries.shape) for out in unpack(back, 4)]
    return (*outs, weight_grad)


def solution(mesh):
    whole = P("dp", "seq", None, None)
    return jax.shard_map(
        functools.partial(on_device, mesh.shape["seq"], mesh.shape["dp"]),
        mesh=mesh,
        in_specs=(whole, whole, whole, whole, P(None, "seq"), P("dp", None)),
        out_specs=(whole, whole, whole, whole, P(None, "seq")),
        check_vma=False,
    )
```

```python
import functools
import math

import jax
import jax.numpy as jnp
from jax import lax
from jax.experimental import pallas as pl
from jax.experimental.pallas import tpu as pltpu
from jax.sharding import PartitionSpec as P

HEADS = 16
HEAD_DIM = 72
LANES = 128
SCALE = 1.0 / math.sqrt(HEAD_DIM)
F32 = jnp.float32
BF16 = jnp.bfloat16
VMEM_LIMIT = 28 * 1024 * 1024
NT = (((1,), (1,)), ((), ()))
TN = (((0,), (0,)), ((), ()))


def dot(a, b):
    return jnp.dot(a, b, preferred_element_type=F32)


def dot_nt(a, b):
    return lax.dot_general(a, b, NT, preferred_element_type=F32)


def dot_tn(a, b):
    return lax.dot_general(a, b, TN, preferred_element_type=F32)


def window(head):
    first = head * HEAD_DIM // LANES
    last = (head * HEAD_DIM + HEAD_DIM - 1) // LANES
    return first * LANES, (last + 1 - first) * LANES


def head_lanes(head, rows):
    start, size = window(head)
    lane = lax.broadcasted_iota(jnp.int32, (rows, size), 1) + (start - head * HEAD_DIM)
    return (lane >= 0) & (lane < HEAD_DIM)


def clip_bias(lens_ref, rows, positions):
    def ids(axis):
        index = lax.broadcasted_iota(jnp.int32, (rows, rows), axis)
        frame = lax.div(index, jnp.int32(positions))
        clip = jnp.zeros_like(frame)
        end = jnp.int32(0)
        for j in range(lens_ref.shape[1]):
            end = end + lens_ref[0, j]
            clip = clip + jnp.where(frame >= end, 1, 0)
        return clip * positions + (index - frame * positions)

    return jnp.where(ids(0) == ids(1), 0.0, -jnp.inf).astype(F32)


def softmax(query_win, key_win, bias):
    scores = dot_nt(query_win, key_win) * SCALE + bias
    raised = jnp.exp(scores - jnp.max(scores, axis=-1, keepdims=True))
    return raised, 1.0 / jnp.sum(raised, axis=-1, keepdims=True)


class Tiles:
    def __init__(self, ref, base=0):
        self.ref, self.base, self.held = ref, base, {}

    def add(self, head, value):
        start, size = window(head)
        for off in range(0, size, LANES):
            piece = value[:, off : off + LANES]
            tile = start + off
            self.held[tile] = piece if tile not in self.held else self.held[tile] + piece
        done = (head + 1) * HEAD_DIM
        for tile in [t for t in self.held if t + LANES <= done]:
            lanes = pl.ds(self.base + tile, LANES)
            self.ref[:, lanes] = self.held.pop(tile).astype(self.ref.dtype)


FWD_FLOPS = 10**11
JOIN_FLOPS = 10**9
FINISH_FLOPS = 3 * 10**9
GROUP = 8
CUT = 384
FULL = 16
ODD = 2
CHUNK = 3
ODD_LANES = 384


def selection(rows, columns, wanted):
    row = lax.broadcasted_iota(jnp.int32, (rows, columns), 0)
    column = lax.broadcasted_iota(jnp.int32, (rows, columns), 1)
    return jnp.where(column == wanted(row), 1.0, 0.0).astype(BF16)


def chunk_tiles(ref, q):
    pieces = [ref[:, pl.ds((CHUNK * u + q) * LANES, LANES)] for u in range(CHUNK)]
    return jnp.concatenate(pieces, axis=1)


def pack_kernel(*refs):
    *parts, x_ref, staged_ref, sems = refs
    rows, width = parts[0].shape
    half = rows // 2
    fetches, copies = [], []
    for i, part in enumerate(parts):
        for j in range(2):
            at, lanes, n = pl.ds(j * half, half), pl.ds(i * width, width), 2 * i + j
            fetches.append(pltpu.make_async_copy(part.at[at], staged_ref.at[i, at], sems.at[0, n]))
            copies.append(pltpu.make_async_copy(staged_ref.at[i, at], x_ref.at[at, lanes], sems.at[1, n]))
    for fetch in fetches:
        fetch.start()
    for fetch, copy in zip(fetches, copies):
        fetch.wait()
        copy.start()
    for copy in copies:
        copy.wait()


def unpack_kernel(x_ref, *refs):
    *outs, sems = refs
    width = outs[0].shape[1]
    copies = [
        pltpu.make_async_copy(x_ref.at[:, pl.ds(i * width, width)], out, sems.at[i]) for i, out in enumerate(outs)
    ]
    for copy in copies:
        copy.start()
    for copy in copies:
        copy.wait()


def spread_kernel(weight_ref, out_ref, held_ref, sem):
    shard, width = weight_ref.shape
    rows = held_ref.shape[0]
    weight = weight_ref[...]

    def core(row):
        return jnp.bitwise_and(lax.div(row, jnp.int32(GROUP)), 1)

    def place(row):
        return jnp.bitwise_and(row, GROUP - 1)

    for block in range(FULL // GROUP):
        pick = selection(rows, shard, lambda row: FULL * core(row) + GROUP * block + place(row))
        held_ref[:, pl.ds(block * width, width)] = dot(pick, weight).astype(BF16)
    odd = jnp.zeros((rows, ODD_LANES), F32)
    for q in range(CHUNK):

        def wanted(row):
            k = lax.div(place(row) - q, jnp.int32(CHUNK))
            exact = (place(row) == CHUNK * k + q) & (k < ODD)
            return jnp.where(exact, 2 * FULL + ODD * core(row) + k, -1)

        odd = odd + dot(selection(rows, shard, wanted), chunk_tiles(weight_ref, q))
    held_ref[:, pl.ds(FULL // GROUP * width, ODD_LANES)] = odd.astype(BF16)
    copy = pltpu.make_async_copy(held_ref, out_ref, sem.at[0])
    copy.start()
    copy.wait()


def pick_rows(ref, place):
    padded, width = ref.shape
    block = padded // 8
    for step in range(8):
        at = lax.broadcasted_iota(jnp.int32, (block, width), 0) + step * block
        ref[pl.ds(step * block, block), :] = jnp.where(at == place, 1.0, 0.0).astype(BF16)


def tables_kernel(shard, positions, core_ref, lens_ref, pick_ref, bias_ref, held_ref, sem):
    width = pick_ref.shape[1]
    feature = lax.broadcasted_iota(jnp.int32, (1, width), 1)
    owner = lax.div(feature, jnp.int32(shard))
    rest = feature - owner * shard
    holder = jnp.where(rest < 2 * FULL, lax.div(rest, jnp.int32(FULL)), lax.div(rest - 2 * FULL, jnp.int32(ODD)))
    other = jnp.bitwise_and(holder + core_ref[0], 1)
    within = rest - FULL * holder
    block = lax.div(within, jnp.int32(GROUP))
    size = width // shard * GROUP
    full = (other * (FULL // GROUP) + block) * size + owner * GROUP + within - block * GROUP
    odd = 2 * (FULL // GROUP) * size + (other * (width // shard) + owner) * ODD + rest - 2 * FULL - ODD * holder
    pick_rows(held_ref, jnp.where(rest < 2 * FULL, full, odd))
    copy = pltpu.make_async_copy(held_ref, pick_ref, sem.at[0])
    copy.start()
    bias_ref[...] = clip_bias(lens_ref, bias_ref.shape[0], positions)
    copy.wait()


def forward_kernel(
    core_ref, x_ref, bias_ref, mixed_ref, keep_ref, first_ref, second_ref, part_ref, held_ref, turn_ref, sems
):
    rows, width = mixed_ref.shape
    bias = bias_ref[...]
    mixed_tiles = Tiles(mixed_ref)
    for head in range(HEADS):
        start, size = window(head)
        lanes = head_lanes(head, rows)
        query_win = jnp.where(lanes, x_ref[:, pl.ds(start, size)], 0)
        key_win = x_ref[:, pl.ds(width + start, size)]
        value_win = jnp.where(lanes, x_ref[:, pl.ds(2 * width + start, size)], 0)
        raised, recip = softmax(query_win, key_win, bias)
        mixed_tiles.add(head, dot((raised * recip).astype(BF16), value_win))
    copies = []
    turn_ref[...] = jnp.zeros_like(turn_ref)
    mixed = mixed_ref[...]
    block = 3 * LANES
    for at in range(0, width, block):
        part_ref[pl.ds(at, block), :] = dot_tn(x_ref[:, pl.ds(3 * width + at, block)], mixed)
    chips = held_ref.shape[0]
    shard = width // chips // 2

    def fold(ids, out_ref, other):
        for core in range(2):

            @pl.when(core_ref[0] == core)
            def _():
                for j in ids:
                    fold_rows(part_ref, (2 * j + (core ^ other)) * shard, shard, out_ref, j, turn_ref)

    for step in range(4):
        some = chips // 4
        fold(range(step * some, (step + 1) * some), held_ref, 1)
        source, place = pl.ds(step * some, some), pl.ds(step % 2 * some, some)
        send_ref = first_ref if step < 2 else second_ref
        copies.append(pltpu.make_async_copy(held_ref.at[source], send_ref.at[place], sems.at[step]))
        copies[-1].start()
    fold(range(chips), keep_ref, 0)
    for copy in copies:
        copy.wait()


def fold_rows(part_ref, at, shard, out_ref, j, turn_ref):
    width = part_ref.shape[1]
    size = lane_half(width)
    for group in range(shard // 8):
        rows = part_ref[pl.ds(at + group * 8, 8), :]
        out_ref[j, :, pl.ds(group * width, width)] = rows.astype(BF16)
    last = part_ref[pl.ds(at + shard // 8 * 8, 4), :]
    turn_ref[pl.ds(0, 4), :] = last[:, :size]
    turn_ref[pl.ds(4, 4), pl.ds(0, width - size)] = last[:, size:]
    out_ref[j, :, pl.ds(shard // 8 * width, size)] = turn_ref[...].astype(BF16)


def join_kernel(keep_ref, first_ref, second_ref, out_ref):
    lanes, total = out_ref.shape[3], keep_ref.shape[2]
    whole = lanes - CUT
    half = first_ref.shape[0]
    for at, ref in ((0, first_ref), (half, second_ref)):
        ids = pl.ds(at, half)
        added = (keep_ref[ids].astype(F32) + ref[...].astype(F32)).astype(BF16)
        out_ref[0, ids, :, pl.ds(0, whole)] = added[:, :, :whole]
        out_ref[1, ids, :, pl.ds(0, whole)] = added[:, :, whole : 2 * whole]
        rest = pl.ds(whole, lanes - whole)
        out_ref[0, ids, :, rest] = added[:, :, 2 * whole : whole + lanes]
        out_ref[1, ids, :, rest] = added[:, :, total - (lanes - whole) :]


def finish_kernel(place_ref, mine_ref, other_ref, out_ref):
    width = out_ref.shape[1]
    size = lane_half(width)
    mine, other = mine_ref[...].astype(F32), other_ref[...].astype(F32)
    low = place_ref[0] == 0
    lower, upper = jnp.where(low, mine, other), jnp.where(low, other, mine)
    for group, half in enumerate((lower, lower, upper, upper)):
        at = group % 2 * width
        out_ref[pl.ds(group * 8, 8), :] = half[:, at : at + width]
    turned = jnp.concatenate([lower[:, 2 * width :], upper[:, 2 * width + 2 * CUT - size :]], axis=1)
    out_ref[pl.ds(32, 4), pl.ds(0, size)] = turned[:4]
    out_ref[pl.ds(32, 4), pl.ds(size, width - size)] = turned[4:, : width - size]


def scores_kernel(x_ref, bias_ref, attention_ref):
    rows = x_ref.shape[0]
    width = x_ref.shape[1] // 4
    bias = bias_ref[...]
    for head in range(HEADS):
        start, size = window(head)
        query_win = jnp.where(head_lanes(head, rows), x_ref[:, pl.ds(start, size)], 0)
        scores = dot_nt(x_ref[:, pl.ds(width + start, size)], query_win) * SCALE + bias
        raised = jnp.exp(scores - jnp.max(scores, axis=0, keepdims=True))
        attention_ref[head] = raised * (1.0 / jnp.sum(raised, axis=0, keepdims=True))


def backward_kernel(
    pick_hbm, x_hbm, own_hbm, other_ref, attention_ref, mixed_ref, y_ref,
    pick_ref, x_ref, own_ref, odd_ref, back_ref, out_ref, held_ref, sems
):
    rows, width = mixed_ref.shape
    pairs, third, fourth = pl.ds(0, 2 * width), pl.ds(2 * width, width), pl.ds(3 * width, width)
    fetches = [
        pltpu.make_async_copy(x_hbm.at[:, pairs], x_ref.at[:, pairs], sems.at[7]),
        pltpu.make_async_copy(own_hbm, own_ref, sems.at[8]),
        pltpu.make_async_copy(x_hbm.at[:, fourth], x_ref.at[:, fourth], sems.at[9]),
        pltpu.make_async_copy(pick_hbm, pick_ref, sems.at[10]),
        pltpu.make_async_copy(x_hbm.at[:, third], x_ref.at[:, third], sems.at[11]),
    ]
    for fetch in fetches:
        fetch.start()
    copies = []

    def send(start, size):
        lanes = pl.ds(start, size)
        copies.append(pltpu.make_async_copy(held_ref.at[:, lanes], y_ref.at[:, lanes], sems.at[len(copies)]))
        copies[-1].start()

    blocks = FULL // GROUP
    fetches[0].wait()
    fetches[1].wait()
    weight = []
    for ref in (own_ref, other_ref):
        weight += [ref[:, pl.ds(b * width, width)] for b in range(blocks)]
    odd_rows = odd_ref.shape[0] // 2
    for i, ref in enumerate((own_ref, other_ref)):
        left = ref[:, pl.ds(blocks * width, ODD_LANES)]
        for q in range(CHUNK):

            def wanted(row):
                source = lax.div(row, jnp.int32(ODD))
                return source * GROUP + CHUNK * (row - ODD * source) + q

            got = dot(selection(odd_rows, rows, wanted), left).astype(BF16)
            for u in range(CHUNK):
                lanes = pl.ds((CHUNK * u + q) * LANES, LANES)
                odd_ref[pl.ds(i * odd_rows, odd_rows), lanes] = got[:, u * LANES : (u + 1) * LANES]
    weight.append(odd_ref[...])
    fetches[2].wait()
    fetches[3].wait()
    grad = dot_nt(x_ref[:, fourth], pick_ref[...]).astype(BF16)
    mixed = mixed_ref[...]
    back = jnp.zeros((rows, width), F32)
    at = 0
    for block in weight:
        size = block.shape[0]
        back = back + dot(grad[:, at : at + size], block)
        out_ref[:, pl.ds(at, size)] = dot_nt(mixed, block).astype(BF16)
        at += size
    back_ref[...] = back.astype(BF16)
    held_ref[:, pl.ds(0, width)] = dot(out_ref[...], pick_ref[...]).astype(BF16)
    send(0, width)
    query_tiles, key_tiles, value_tiles = [Tiles(held_ref, i * width) for i in (1, 2, 3)]
    fetches[4].wait()
    sent = 0
    for head in range(HEADS):
        start, size = window(head)
        lanes = head_lanes(head, rows)
        query_win = jnp.where(lanes, x_ref[:, pl.ds(start, size)], 0)
        key_win = jnp.where(lanes, x_ref[:, pl.ds(width + start, size)], 0)
        value_win = x_ref[:, pl.ds(2 * width + start, size)]
        back_win = jnp.where(lanes, back_ref[:, pl.ds(start, size)], 0)
        attention = attention_ref[head]
        value_tiles.add(head, dot(attention.astype(BF16), back_win))
        drawn = attention * dot_nt(value_win, back_win)
        inner = jnp.sum(drawn, axis=0, keepdims=True)
        score_grad = ((drawn - attention * inner) * SCALE).astype(BF16)
        key_tiles.add(head, dot(score_grad, query_win))
        query_tiles.add(head, dot_tn(score_grad, key_win))
        if head in (HEADS // 2 - 1, HEADS - 1):
            done = (head + 1) * HEAD_DIM // LANES * LANES
            for i in (1, 2, 3):
                send(i * width + sent, done - sent)
            sent = done
    for copy in copies:
        copy.wait()


def total_kernel(parts_ref, out_ref):
    total = parts_ref[0].astype(F32)
    for j in range(1, parts_ref.shape[0]):
        total = total + parts_ref[j].astype(F32)
    out_ref[...] = total.astype(BF16)


def call(kernel, name, outs, args, smem=0, hbm_in=0, hbm_out=(), scratch=(), flops=0):
    space = [pltpu.SMEM] * smem + [pltpu.HBM] * hbm_in + [pltpu.VMEM] * (len(args) - smem - hbm_in)
    args = [pltpu.with_memory_space_constraint(a, s) if s == pltpu.HBM else a for a, s in zip(args, space)]
    shapes = [jax.ShapeDtypeStruct(shape, dtype) for shape, dtype in outs]
    moved = sum(a.size * a.dtype.itemsize for a in args) + sum(math.prod(s.shape) * s.dtype.itemsize for s in shapes)
    return pl.pallas_call(
        kernel,
        out_shape=[pltpu.HBM(s.shape, s.dtype) if i in hbm_out else s for i, s in enumerate(shapes)],
        in_specs=[pl.BlockSpec(memory_space=s) for s in space],
        out_specs=[pl.BlockSpec(memory_space=pltpu.HBM if i in hbm_out else pltpu.VMEM) for i in range(len(outs))],
        scratch_shapes=scratch,
        compiler_params=pltpu.CompilerParams(vmem_limit_bytes=VMEM_LIMIT),
        cost_estimate=pl.CostEstimate(flops=flops, bytes_accessed=0 if flops else moved, transcendentals=0),
        name=name,
    )(*args)


def dma(count):
    return pltpu.SemaphoreType.DMA((count,))


def pack(arrays):
    rows, width = arrays[0].shape
    count = len(arrays)
    outs = [((rows, count * width), BF16)]
    scratch = [pltpu.VMEM((count, rows, width), BF16), pltpu.SemaphoreType.DMA((2, 2 * count))]
    return call(pack_kernel, "pack", outs, arrays, hbm_in=count, hbm_out=(0,), scratch=scratch)[0]


def unpack(x, count):
    rows, wide = x.shape
    width = wide // count
    outs = [((rows, width), BF16)] * count
    return call(unpack_kernel, "unpack", outs, (x,), hbm_out=range(count), scratch=[dma(count)])


def spread(weight_t, rows):
    shape = (rows, FULL // GROUP * weight_t.shape[1] + ODD_LANES)
    scratch = [pltpu.VMEM(shape, BF16), dma(1)]
    return call(spread_kernel, "spread", [(shape, BF16)], (weight_t,), hbm_out=(0,), scratch=scratch)[0]


def tables(core, lengths, rows, width, shard, positions):
    kernel = functools.partial(tables_kernel, shard, positions)
    outs = [((width, width), BF16), ((rows, rows), F32)]
    scratch = [pltpu.VMEM((width, width), BF16), dma(1)]
    return call(kernel, "tables", outs, (core, lengths), smem=2, hbm_out=(0,), scratch=scratch)


def forward(core, x, bias, width, chips):
    rows = x.shape[0]
    folded = 4 * width + lane_half(width)
    part, half = (chips, 8, folded), (chips // 2, 8, folded)
    outs = [((rows, width), BF16), (part, BF16), (half, BF16), (half, BF16)]
    scratch = [pltpu.VMEM((width, width), F32), pltpu.VMEM(part, BF16), pltpu.VMEM((8, lane_half(width)), F32), dma(4)]
    args = (core, x, bias)
    return call(
        forward_kernel, "forward", outs, args, smem=1, hbm_out=(2, 3), scratch=scratch, flops=FWD_FLOPS
    )


def join(keep, first, second, width):
    outs = [((2, keep.shape[0], 8, 2 * width + CUT), BF16)]
    return call(join_kernel, "join", outs, (keep, first, second), flops=JOIN_FLOPS)[0]


def scores(x, bias):
    rows = x.shape[0]
    return call(scores_kernel, "scores", [((HEADS, rows, rows), F32)], (x, bias))[0]


def backward(pick, x, own, other, attention, mixed):
    rows, width = mixed.shape
    flops = 8 * width * rows * width + 12 * HEADS * rows * rows * 256
    one, wide = (rows, width), (rows, 4 * width)
    shapes = ((width, width), wide, own.shape, (width - 4 * rows, width), one, one, wide)
    scratch = [pltpu.VMEM(shape, BF16) for shape in shapes] + [dma(12)]
    args = (pick, x, own, other, attention, mixed)
    return call(backward_kernel, "backward", [(wide, BF16)], args, hbm_in=3, hbm_out=(0,), scratch=scratch, flops=flops)[0]


def total_of(parts):
    return call(total_kernel, "total", [(parts.shape[1:], BF16)], (parts,))[0]


def lane_half(width):
    return (width // LANES + 1) // 2 * LANES


def sum_over_pairs(block, place, shard, width, n_dp):
    half, quarter = n_dp // 2, n_dp // 4

    def exchange(block, source):
        return lax.ppermute(block, "dp", [(source(i) % n_dp, i) for i in range(n_dp)])

    def added(block, source):
        return (block.astype(F32) + exchange(block, source).astype(F32)).astype(BF16)

    def second(i):
        return i ^ quarter if i % 2 == 0 else i + quarter * (1 if i // quarter % 2 else -1)

    def third(i):
        return n_dp - 2 - i if i % 2 == 0 else half - i

    block = added(added(added(block, lambda i: i ^ 2), second), third)
    args = (place, block, exchange(block, lambda i: i ^ 1))
    return call(finish_kernel, "finish", [((shard, width), F32)], args, smem=1, flops=FINISH_FLOPS)[0]


def on_device(n_seq, n_dp, queries, key_vectors, value_vectors, out_grad, out_weight, clip_frames):
    patches, width = queries.shape[2:]
    positions = patches // n_seq
    shard = out_weight.shape[1]
    core = jnp.bitwise_and(lax.axis_index("seq"), 1).astype(jnp.int32)

    def swap(block):
        return lax.all_to_all(block.reshape(n_seq, positions, -1), "seq", 0, 0, tiled=True)

    def partner(block):
        return lax.ppermute(block, "seq", [(i, i ^ 1) for i in range(n_seq)])

    arrays = [a.reshape(patches, width) for a in (queries, key_vectors, value_vectors, out_grad)]
    x = swap(pack(arrays)).reshape(patches, -1)
    rows, x = lax.optimization_barrier((spread(out_weight.T, patches), x))
    own = swap(rows).reshape(patches, -1)
    pick, bias = tables(core.reshape(1), clip_frames, patches, width, shard, positions)
    mixed, keep, *send = forward(core.reshape(1), x, bias, width, n_seq // 2)

    chip = join(keep, *[partner(block) for block in send], width)
    chip = chip.reshape(n_seq, *chip.shape[2:])
    pairs = [
        [(p + d) * n_seq + i for d in (0, 1) for i in range(c, n_seq, 2)] for p in range(0, n_dp, 2) for c in (0, 1)
    ]
    parts = lax.all_to_all(chip, ("dp", "seq"), 0, 0, tiled=True, axis_index_groups=pairs)

    y = backward(pick, x, own, partner(own), scores(x, bias), mixed)
    total, y = lax.optimization_barrier((total_of(parts), y))
    back = swap(y).reshape(patches, 4 * width)
    place = jnp.bitwise_and(lax.axis_index("dp"), 1).astype(jnp.int32).reshape(1)
    weight_grad = sum_over_pairs(total, place, shard, width, n_dp).T
    outs = [out.reshape(queries.shape) for out in unpack(back, 4)]
    return (*outs, weight_grad)


def solution(mesh):
    whole = P("dp", "seq", None, None)
    return jax.shard_map(
        functools.partial(on_device, mesh.shape["seq"], mesh.shape["dp"]),
        mesh=mesh,
        in_specs=(whole, whole, whole, whole, P(None, "seq"), P("dp", None)),
        out_specs=(whole, whole, whole, whole, P(None, "seq")),
        check_vma=False,
    )
```
